128 devices in a mesh: member: 8 (over x, core), space: 16 (over z, y).
Axes of the slice: x: 4, y: 4, z: 4, core: 2. Of those that a mesh axis runs over, the one named last changes fastest.
Arguments:
- spectra: float32 [32, 12, 320, 641], P('member', None, 'space'), may hold values from -6 to 6
- legendre: bfloat16 [320, 641, 384], P('space'), as said below
- sin_lat: float32 [384], replicated, may hold values from 0 to 1, as said below
- gravity: float32 [2, 2], replicated, may hold values from 0.1 to 2, as said below
- stability: float32 [2, 2], replicated, may hold values from 0.1 to 2, as said below
- clones: int32 [4, 2], replicated, may hold values from 0 to 31, as said below
Outputs:
- new_state: float32 [32, 12, 320, 641], P('member', None, 'space')
The draws below stay inside these ranges and needn't reach their ends.
Inputs may be any that keep to these rules, and one draw needn't show every extreme that they name: `clones`: column 0 holds 4 distinct killed trajectories, column 1 for each a survivor; no survivor is killed, and a survivor may be copied onto several killed trajectories. legendre[p, j, l] is the associated Legendre function of the (m, n) of position (p, j), normalized so that its square integrates to one over -1 to 1, at mu = sin_lat[l]. `sin_lat`: decreasing from the pole towards the equator. `gravity`: diagonal entries 1 to 2, off-diagonal entries 0.1 to 0.6. `stability`: diagonal entries 1 to 2, off-diagonal entries 0.1 to 0.6.
All inputs are finite; a program needn't handle non-finite values.
Results may differ from the reference program's by a relative error of at most 0.0016.
Values may be sent and summed in bfloat16 or wider, within the bound.
A program may use at most 128 MiB of HBM per device.

```python
import math
import jax
import jax.numpy as jnp
from jax import lax

NW = 640
NLAT = 768
NLON = 1280
TRAJ_DEV = 4
PAIRS = 320
NHALF = 384
MEMBERS = 32
KILLED = 4


def latitude_sines(key):
    jitter = jax.random.uniform(jax.random.fold_in(key, 11), (NHALF,), jnp.float32, -0.35, 0.35)
    colatitude = math.pi * (jnp.arange(NHALF, dtype=jnp.float32) + 0.5 + jitter) / NLAT
    return jnp.cos(colatitude)


def draw_sin_lat(key, part):
    return latitude_sines(key)


def draw_legendre(key, part):
    cosine = latitude_sines(key)[None, :]
    sine_theta = jnp.sqrt(1.0 - cosine * cosine)
    factor_index = jnp.arange(1, NW, dtype=jnp.float32)
    log_factor = jnp.concatenate([jnp.zeros((1,), jnp.float32), jnp.cumsum(jnp.log((2.0 * factor_index + 1.0) / (2.0 * factor_index)))])
    pair_index = jnp.arange(PAIRS, dtype=jnp.int32)[:, None]

    def advance_row(carry, column):
        latest, before = carry
        leading = column < NW - pair_index
        wave_order = jnp.where(leading, pair_index, NW - 1 - pair_index)
        offset = jnp.where(leading, column, column - (NW - pair_index))
        order_real = wave_order.astype(jnp.float32)
        degree = (wave_order + offset).astype(jnp.float32)
        diagonal = jnp.exp(0.5 * jnp.log(0.5) + 0.5 * log_factor[wave_order] + order_real * jnp.log(sine_theta))
        second = jnp.sqrt(2.0 * order_real + 3.0) * cosine * latest
        prior = degree - 1.0
        span_now = jnp.where(offset >= 2, degree * degree - order_real * order_real, 1.0)
        span_prior = jnp.where(offset >= 2, prior * prior - order_real * order_real, 1.0)
        ahead = jnp.sqrt(jnp.maximum(4.0 * degree * degree - 1.0, 1.0) / span_now)
        behind = jnp.sqrt(jnp.maximum(4.0 * prior * prior - 1.0, 1.0) / span_prior)
        general = ahead * (cosine * latest - before / behind)
        value = jnp.where(offset == 0, diagonal, jnp.where(offset == 1, second, general))
        return ((value, latest), value)
    zero_initial_state = jnp.zeros((PAIRS, NHALF), jnp.float32)
    final_carry, stacked = lax.scan(advance_row, (zero_initial_state, zero_initial_state), jnp.arange(NW + 1, dtype=jnp.int32))
    return jnp.transpose(stacked, (1, 0, 2)).astype(jnp.bfloat16)


def coupling_matrix(key):
    diagonal = jax.random.uniform(jax.random.fold_in(key, 1), (2,), jnp.float32, 1.0, 2.0)
    crossed = jax.random.uniform(jax.random.fold_in(key, 2), (2,), jnp.float32, 0.1, 0.6)
    return jnp.stack([jnp.stack([diagonal[0], crossed[0]]), jnp.stack([crossed[1], diagonal[1]])])


def draw_gravity(key, part):
    return coupling_matrix(jax.random.fold_in(key, 21))


def draw_stability(key, part):
    return coupling_matrix(jax.random.fold_in(key, 22))


def draw_clones(key, part):
    groups = MEMBERS // TRAJ_DEV
    base = jax.random.randint(jax.random.fold_in(key, 7), (), 0, groups).astype(jnp.int32)
    order = jax.random.permutation(jax.random.fold_in(key, 3), MEMBERS).astype(jnp.int32)
    index_all = jnp.arange(MEMBERS, dtype=jnp.int32)
    group_of = index_all // TRAJ_DEV
    near_row = (base + 1) % groups * TRAJ_DEV + jax.random.randint(jax.random.fold_in(key, 8), (), 0, TRAJ_DEV).astype(jnp.int32)
    far_row = (base + groups // 2) % groups * TRAJ_DEV + jax.random.randint(jax.random.fold_in(key, 9), (), 0, TRAJ_DEV).astype(jnp.int32)
    scores = jnp.where(group_of == base, order + MEMBERS, order)
    scores = jnp.where(index_all == near_row, -2, jnp.where(index_all == far_row, -1, scores))
    ranked = jnp.argsort(scores, stable=True).astype(jnp.int32)
    removed_members = ranked[:KILLED]
    alive_members = ranked[KILLED:]
    count_alive = MEMBERS - KILLED
    pick_one = jax.random.randint(jax.random.fold_in(key, 4), (KILLED,), 0, count_alive)
    pick_two = jax.random.randint(jax.random.fold_in(key, 5), (KILLED,), 0, count_alive)
    pick_three = jax.random.randint(jax.random.fold_in(key, 6), (KILLED,), 0, count_alive)
    selected_members = jnp.minimum(jnp.minimum(pick_one, pick_two), pick_three)
    remaining_members = alive_members[selected_members].astype(jnp.int32)
    owned_rows_list = base * TRAJ_DEV + jax.random.randint(jax.random.fold_in(key, 10), (2,), 0, TRAJ_DEV).astype(jnp.int32)
    remaining_members = jnp.concatenate([owned_rows_list, remaining_members[2:]])
    return jnp.stack([removed_members, remaining_members], axis=1).astype(jnp.int32)


def level_of(key, dims, shards, smallest, top_value):
    def one(dim, parts):
        draws = jax.random.uniform(jax.random.fold_in(jax.random.fold_in(key, 6), dim), (parts,), jnp.float32, smallest / len(shards), top_value / len(shards))
        return jnp.repeat(jnp.exp(draws), dims[dim] // parts).reshape((-1,) + (1,) * (len(dims) - dim - 1))

    factor_of = one(*shards[0])
    for cut in shards[1:]:
        factor_of = factor_of * one(*cut)
    return factor_of


def gaussian(rng, dims, scale, most, cuts=(), held_as=jnp.bfloat16):
    loudness = level_of(rng, dims, cuts, -0.22, 0.18) if cuts else 1.0
    entries = jax.random.normal(rng, dims, jnp.float32) * scale * loudness
    return jnp.minimum(jnp.maximum(entries, -most), most).astype(held_as)


def setup_inputs(seed: int = 0) -> dict:
    streams_of = jax.random.split(jax.random.key(seed), 7)
    spectra = gaussian(streams_of[0], (MEMBERS, 12, PAIRS, NW + 1), 1.0, 6.0, ((0, 8), (2, 16)), jnp.float32)
    legendre = draw_legendre(jax.random.fold_in(streams_of[6], 71), 0)
    sin_lat = draw_sin_lat(jax.random.fold_in(streams_of[6], 71), 0)
    gravity = draw_gravity(jax.random.fold_in(streams_of[6], 71), 0)
    stability = draw_stability(jax.random.fold_in(streams_of[6], 71), 0)
    clones = draw_clones(jax.random.fold_in(streams_of[6], 71), 0)
    return {"spectra": spectra, "legendre": legendre, "sin_lat": sin_lat, "gravity": gravity, "stability": stability, "clones": clones}


time_step = 0.25
wave_scale = 16.0
diffusion = 0.02

def pair_layout(pair_index, row_length, truncation):
    column = jnp.arange(row_length, dtype=jnp.int32)[None, :]
    lower_pair = pair_index[:, None]
    leading = column < truncation - lower_pair
    wave_order = jnp.where(leading, lower_pair, truncation - 1 - lower_pair)
    offset = jnp.where(leading, column, column - (truncation - lower_pair))
    parity = (1 - 2 * (offset % 2)).astype(jnp.float32)
    return (leading.astype(jnp.float32), parity, wave_order + offset)

def fourier_table(pair_count, truncation, longitudes):
    halves = jnp.arange(2, dtype=jnp.int32)[:, None]
    pair_all = jnp.arange(pair_count, dtype=jnp.int32)[None, :]
    wave_order = jnp.where(halves == 0, pair_all, truncation - 1 - pair_all)
    column = jnp.arange(longitudes, dtype=jnp.int32)
    phase = wave_order[:, :, None] * column[None, None, :] % longitudes
    angle = phase.astype(jnp.float32) * (2.0 * math.pi / longitudes)
    return jnp.stack([jnp.cos(angle), -jnp.sin(angle)]).astype(jnp.bfloat16)

def legendre_input(spectra, leading, parity):
    rounded = spectra.astype(jnp.bfloat16)
    halves = jnp.stack([leading, 1.0 - leading])
    mirror_sign = jnp.stack([jnp.ones_like(parity), parity])
    factor = (halves[:, None] * mirror_sign[None, :]).astype(jnp.bfloat16)
    return rounded[:, :, None, None] * factor[None, None]

def combine_halves(projected, leading, parity):
    first_part = projected[:, :, 0, 0] + parity * projected[:, :, 0, 1]
    second_part = projected[:, :, 1, 0] + parity * projected[:, :, 1, 1]
    return leading * first_part + (1.0 - leading) * second_part

def latitude_terms(sin_lat, first_row, count):
    mirrored = jnp.concatenate([sin_lat, -sin_lat])
    local_sine = lax.dynamic_slice_in_dim(mirrored, first_row, count)
    weights = math.pi * jnp.sqrt(1.0 - local_sine * local_sine) / mirrored.shape[0]
    return (2.0 * local_sine, weights)

def tendencies(physical_grid_samples, coriolis):
    local_spin_spectrum = physical_grid_samples[:, 0:2]
    spreading_rate_spectrum = physical_grid_samples[:, 2:4]
    thermal_spectrum = physical_grid_samples[:, 4:6]
    planetary_spin_spectrum = local_spin_spectrum + coriolis[:, None]
    average_heat_level = 0.5 * (thermal_spectrum[:, 0:1] + thermal_spectrum[:, 1:2])
    return jnp.concatenate([-planetary_spin_spectrum * spreading_rate_spectrum, planetary_spin_spectrum * local_spin_spectrum - 0.5 * spreading_rate_spectrum * spreading_rate_spectrum, -(thermal_spectrum + average_heat_level) * spreading_rate_spectrum], axis=1)

def semi_implicit(spectra, tendency, degree, gravity, stability):
    trajectory_count, comp_count, pair_count, row_length = spectra.shape
    truncation = row_length - 1
    shaped = spectra.reshape(trajectory_count, comp_count // 2, 2, pair_count, row_length)
    forcing = tendency.reshape(trajectory_count, comp_count // 2, 2, pair_count, row_length)
    eigen_value = wave_scale * (degree * (degree + 1)).astype(jnp.float32) / float(truncation * truncation)
    damping = 1.0 / (1.0 + diffusion * eigen_value * eigen_value)
    coupling = time_step * time_step * eigen_value
    product = jnp.dot(gravity, stability, precision=lax.Precision.HIGHEST)
    new_zeta = damping * (shaped[:, 0:2] + time_step * forcing[:, 0:2])
    t_star = shaped[:, 4:6] + time_step * forcing[:, 4:6]
    d_star = shaped[:, 2:4] + time_step * forcing[:, 2:4]
    right_one = d_star[:, 0] + time_step * eigen_value * (gravity[0, 0] * t_star[:, 0] + gravity[0, 1] * t_star[:, 1])
    right_two = d_star[:, 1] + time_step * eigen_value * (gravity[1, 0] * t_star[:, 0] + gravity[1, 1] * t_star[:, 1])
    diag_one = 1.0 + coupling * product[0, 0]
    diag_two = 1.0 + coupling * product[1, 1]
    cross_one = coupling * product[0, 1]
    cross_two = coupling * product[1, 0]
    determ = diag_one * diag_two - cross_one * cross_two
    div_one = (diag_two * right_one - cross_one * right_two) / determ
    div_two = (diag_one * right_two - cross_two * right_one) / determ
    temp_one = damping * (t_star[:, 0] - time_step * (stability[0, 0] * div_one + stability[0, 1] * div_two))
    temp_two = damping * (t_star[:, 1] - time_step * (stability[1, 0] * div_one + stability[1, 1] * div_two))
    new_div = damping * jnp.stack([div_one, div_two], axis=1)
    new_temp = jnp.stack([temp_one, temp_two], axis=1)
    result = jnp.concatenate([new_zeta, new_div, new_temp], axis=1)
    return result.reshape(spectra.shape)

def reference(spectra, legendre, sin_lat, gravity, stability, clones):
    leading, parity, degree = pair_layout(jnp.arange(PAIRS, dtype=jnp.int32), NW + 1, NW)
    zonal_table = fourier_table(PAIRS, NW, NLON).astype(jnp.float32)
    coriolis, weights = latitude_terms(sin_lat, 0, NLAT)
    legendre_wide = legendre.astype(jnp.float32)

    def advance_one(spectrum):
        spectrum = spectrum[None]
        inputs_wide = legendre_input(spectrum, leading, parity).astype(jnp.float32)
        fourier = jnp.einsum('tchqpj,pjl->tchpql', inputs_wide, legendre_wide)
        fourier = fourier.reshape(1, 12, 2, PAIRS, NLAT).astype(jnp.bfloat16)
        banded = fourier.astype(jnp.float32).reshape(1, 6, 2, 2, PAIRS, NLAT)
        physical_grid_samples = jnp.einsum('tfrhpl,rhpk->tflk', banded, zonal_table) * (1.0 / NW)
        forcing = tendencies(physical_grid_samples, coriolis).astype(jnp.bfloat16)
        weighted = jnp.einsum('tflk,rhpk->tfrhpl', forcing.astype(jnp.float32), zonal_table) * weights
        weighted = weighted.astype(jnp.bfloat16).astype(jnp.float32)
        returned = weighted.reshape(1, 12, 2, PAIRS, 2, NHALF)
        projected = jnp.einsum('tchpql,pjl->tchqpj', returned, legendre_wide)
        tendency = combine_halves(projected, leading, parity)
        return semi_implicit(spectrum, tendency, degree, gravity, stability)[0]
    advanced_states = lax.map(advance_one, spectra)
    return advanced_states.at[clones[:, 0]].set(advanced_states[clones[:, 1]])
```

```python
import functools
import math

import jax
import jax.numpy as jnp
import numpy as np
from jax import lax
from jax.experimental import pallas as pl
from jax.experimental.pallas import tpu as pltpu
from jax.sharding import PartitionSpec as P

NW = 640
WIDTH = NW + 1
NLON = 1280
NLAT = 768
NHALF = 384
PAIRS = 320
TRAJ = 4
FIELDS = 6
LOCAL = 20
SPACE = 16
GROUP = 4
GROUPS = LOCAL // GROUP
ROWS = 4 * LOCAL
FULL = 128 * FIELDS
LANES = FULL + 64 * FIELDS
DT = 0.25
WAVE_SCALE = 16.0
DIFFUSION = 0.02
F32 = jnp.float32
BF16 = jnp.bfloat16


@functools.cache
def zonal_tables():
    pair = np.arange(PAIRS)
    order = np.stack([pair, NW - 1 - pair], axis=1)
    phase = (order[:, :, None] * np.arange(NLON)) % NLON
    angle = phase * (2.0 * math.pi / NLON)
    table = np.stack([np.cos(angle), -np.sin(angle)], axis=2).reshape(4 * PAIRS, NLON)
    table = table.astype(jnp.bfloat16)
    return table, np.ascontiguousarray(table.T)


def row_col(rows, width):
    return (
        lax.broadcasted_iota(jnp.int32, (rows, width), 0),
        lax.broadcasted_iota(jnp.int32, (rows, width), 1),
    )


def sign_mask(pair):
    row, col = row_col(8, WIDTH)
    leading = (col < NW - pair).astype(jnp.int32)
    offset = jnp.where(leading == 1, col, col - (NW - pair))
    parity = (1 - 2 * (offset & 1)).astype(F32)
    sign = jnp.where(row >= 4, parity, 1.0)
    return jnp.where(((row >> 1) & 1) + leading == 1, sign, 0.0)


def swap4(value):
    return pltpu.roll(value, 4, 1)


def legendre_group(group, first_pair, x_ref, leg_ref, put):
    row8, _ = row_col(8, WIDTH)
    odd = (row8 & 1) == 1
    results = []
    for k in range(GROUP):
        local = group * GROUP + k
        mask = sign_mask(first_pair + local)
        pieces = []
        for t in range(TRAJ):
            for f in range(FIELDS):
                real = x_ref[t, 2 * f, pl.ds(local, 1), :]
                imag = x_ref[t, 2 * f + 1, pl.ds(local, 1), :]
                pieces.append(jnp.where(odd, imag, real) * mask)
        lhs = jnp.concatenate(pieces, axis=0).astype(BF16)
        dots = jnp.dot(lhs, leg_ref[k], preferred_element_type=F32)
        results.append(dots.reshape(TRAJ * FIELDS, 8, NHALF))
    upper = lax.broadcasted_iota(jnp.int32, (TRAJ * FIELDS, 8, NHALF), 1) < 4
    hemispheres = ([], [])
    for k in range(0, GROUP, 2):
        first, second = results[k], results[k + 1]
        hemispheres[0].append(jnp.where(upper, first, swap4(second)))
        hemispheres[1].append(jnp.where(upper, swap4(first), second))
    low = lax.broadcasted_iota(jnp.int32, (16, 128), 1) < 64
    for side in range(2):
        one, two = hemispheres[side]
        for t in range(TRAJ):
            for level in range(FIELDS // 2):
                tiles = []
                for f in (2 * level, 2 * level + 1):
                    tile = jnp.concatenate([one[t * FIELDS + f], two[t * FIELDS + f]], axis=0)
                    put(4 * t + 2 * side, 128 * f, tile[:, 0:128].astype(BF16))
                    put(4 * t + 2 * side + 1, 128 * f, tile[:, 128:256].astype(BF16))
                    tiles.append(tile[:, 256:384])
                a, b = tiles
                lane = FULL + 128 * level
                put(4 * t + 2 * side, lane, jnp.where(low, a, pltpu.roll(b, 64, 1)).astype(BF16))
                put(
                    4 * t + 2 * side + 1, lane, jnp.where(low, pltpu.roll(a, 64, 1), b).astype(BF16)
                )


def legendre_kernel(x_ref, leg_ref, out_ref):
    group = pl.program_id(0)
    first_pair = lax.axis_index("space") * LOCAL

    def put(block, lane, value):
        out_ref[block, :, lane : lane + 128] = value

    legendre_group(group, first_pair, x_ref, leg_ref, put)


def latitude_rows(sin_ref, place):
    low = lax.broadcasted_iota(jnp.int32, (1, 128), 1) < 64
    zero, one, two = (sin_ref[:, 128 * i : 128 * i + 128] for i in range(3))
    swapped = pltpu.roll(two, 64, 1)
    second = (place & 1) == 1
    sign = jnp.where((place & 3) >= 2, -1.0, 1.0).astype(F32)
    full = jnp.where(second, one, zero) * sign
    half = jnp.where(second, jnp.where(low, swapped, two), jnp.where(low, two, swapped)) * sign
    return full, half


def forcing_of(spin, spread, heat, heat_swapped, coriolis):
    spun = spin + coriolis
    return (
        -spun * spread,
        spun * spin - 0.5 * spread * spread,
        -(heat + 0.5 * (heat + heat_swapped)) * spread,
    )


def grid_kernel(f_ref, tall_ref, wide_ref, sin_ref, out_ref, forcing_ref):
    place = lax.axis_index("space")
    full, half = latitude_rows(sin_ref, place)
    tile = 256

    def forward(i, _):
        rows = pl.ds(pl.multiple_of(i * tile, tile), tile)
        basis = wide_ref[rows, :]
        part = jnp.dot(basis, f_ref[:, 0:FULL], preferred_element_type=F32) * (1.0 / NW)
        field = [part[:, 128 * f : 128 * f + 128] for f in range(FIELDS)]
        for a in range(2):
            made = forcing_of(field[a], field[2 + a], field[4 + a], field[5 - a], 2.0 * full)
            for g in range(3):
                lane = 128 * (2 * g + a)
                forcing_ref[rows, lane : lane + 128] = made[g].astype(BF16)
        part = jnp.dot(basis, f_ref[:, FULL:LANES], preferred_element_type=F32) * (1.0 / NW)
        field = [part[:, 128 * f : 128 * f + 128] for f in range(3)]
        made = forcing_of(*field, pltpu.roll(field[2], 64, 1), 2.0 * half)
        for g in range(3):
            lane = FULL + 128 * g
            forcing_ref[rows, lane : lane + 128] = made[g].astype(BF16)
        return 0

    lax.fori_loop(0, NLON // tile, forward, 0)
    weight_full = math.pi * jnp.sqrt(1.0 - full * full) / NLAT
    weight_half = math.pi * jnp.sqrt(1.0 - half * half) / NLAT
    weights = jnp.concatenate([weight_full] * FIELDS + [weight_half] * 3, axis=1)

    def backward(i, _):
        rows = pl.ds(pl.multiple_of(i * tile, tile), tile)
        basis = tall_ref[rows, :]
        part = jnp.dot(basis, forcing_ref[:, 0:FULL], preferred_element_type=F32)
        out_ref[rows, 0:FULL] = (part * weights[:, 0:FULL]).astype(BF16)
        part = jnp.dot(basis, forcing_ref[:, FULL:LANES], preferred_element_type=F32)
        out_ref[rows, FULL:LANES] = (part * weights[:, FULL:LANES]).astype(BF16)
        return 0

    lax.fori_loop(0, 4 * PAIRS // tile, backward, 0)


def project_group(group, first_pair, get, leg_ref, tend_ref):
    low = lax.broadcasted_iota(jnp.int32, (16, 128), 1) < 64
    hemispheres = ([], [])
    for side in range(2):
        for t in range(TRAJ):
            for level in range(FIELDS // 2):
                lane = FULL + 128 * level
                a = get(4 * t + 2 * side, lane).astype(F32)
                b = get(4 * t + 2 * side + 1, lane).astype(F32)
                last = (
                    jnp.where(low, a, pltpu.roll(b, 64, 1)),
                    jnp.where(low, pltpu.roll(a, 64, 1), b),
                )
                for h in range(2):
                    f = 2 * level + h
                    hemispheres[side].append(
                        jnp.concatenate(
                            [
                                get(4 * t + 2 * side, 128 * f).astype(F32),
                                get(4 * t + 2 * side + 1, 128 * f).astype(F32),
                                last[h],
                            ],
                            axis=1,
                        )
                    )
    north = jnp.stack(hemispheres[0])
    south = jnp.stack(hemispheres[1])
    upper = lax.broadcasted_iota(jnp.int32, (TRAJ * FIELDS, 8, NHALF), 1) < 4
    row8, _ = row_col(8, WIDTH)
    odd = ((row8 & 1) == 1)[None]
    sums = []
    for k in range(GROUP):
        rows = slice(8 * (k // 2), 8 * (k // 2) + 8)
        n, s = north[:, rows], south[:, rows]
        lhs = jnp.where(upper, n, swap4(s)) if k % 2 == 0 else jnp.where(upper, swap4(n), s)
        lhs = lhs.reshape(8 * TRAJ * FIELDS, NHALF).astype(BF16)
        dots = lax.dot_general(
            lhs, leg_ref[k], (((1,), (1,)), ((), ())), preferred_element_type=F32
        ).reshape(TRAJ * FIELDS, 8, WIDTH)
        dots = dots * sign_mask(first_pair + group * GROUP + k)[None]
        dots = dots + pltpu.roll(dots, 4, 1)
        sums.append(dots + pltpu.roll(dots, 2, 1))
    place = (row8 & 3)[None]
    here = (row8 >> 2) == (group & 1)
    for part in range(2):
        mixed = None
        for k in range(GROUP):
            turned = pltpu.roll(sums[k], 1, 1)
            every = jnp.where(odd, turned, sums[k]) if part == 0 else jnp.where(odd, sums[k], turned)
            mixed = every if k == 0 else jnp.where(place == k, every, mixed)
        for i in range(TRAJ * FIELDS):
            slot = tend_ref.at[2 * i + part, group >> 1]
            slot[...] = jnp.where(here, mixed[i], slot[...])


def semi_implicit(first_pair, x_ref, tend_ref, grav_ref, stab_ref, out_ref):
    g = [[grav_ref[a, b] for b in range(2)] for a in range(2)]
    s = [[stab_ref[a, b] for b in range(2)] for a in range(2)]
    k = [[g[a][0] * s[0][b] + g[a][1] * s[1][b] for b in range(2)] for a in range(2)]
    for tile in range(3):
        count = min(8, LOCAL - 8 * tile)
        row, col = row_col(count, WIDTH)
        pair = row + (first_pair + 8 * tile)
        leading = col < NW - pair
        degree = jnp.where(leading, col + pair, (NW - 1 - pair) + col - (NW - pair))
        lam = WAVE_SCALE * (degree * (degree + 1)).astype(F32) / float(NW * NW)
        damp = 1.0 / (1.0 + DIFFUSION * lam * lam)
        coupling = DT * DT * lam
        diag = [1.0 + coupling * k[a][a] for a in range(2)]
        cross = [coupling * k[0][1], coupling * k[1][0]]
        inverse = 1.0 / (diag[0] * diag[1] - cross[0] * cross[1])
        rows = slice(8 * tile, 8 * tile + count)

        def one(t, _):
            for part in range(2):
                def moved(f):
                    c = 2 * f + part
                    return x_ref[t, c, rows, :] + DT * tend_ref[12 * t + c, tile, 0:count, :]

                for a in range(2):
                    out_ref[t, 2 * a + part, rows, :] = damp * moved(a)
                heat = [moved(4), moved(5)]
                right = [
                    moved(2 + a) + DT * lam * (g[a][0] * heat[0] + g[a][1] * heat[1])
                    for a in range(2)
                ]
                new = [
                    (diag[1] * right[0] - cross[0] * right[1]) * inverse,
                    (diag[0] * right[1] - cross[1] * right[0]) * inverse,
                ]
                for a in range(2):
                    out_ref[t, 4 + 2 * a + part, rows, :] = damp * new[a]
                    out_ref[t, 8 + 2 * a + part, rows, :] = damp * (
                        heat[a] - DT * (s[a][0] * new[0] + s[a][1] * new[1])
                    )
            return 0

        lax.fori_loop(0, TRAJ, one, 0)


def project_kernel(back_ref, leg_ref, x_ref, grav_ref, stab_ref, out_ref, tend_ref):
    group = pl.program_id(0)
    first_pair = lax.axis_index("space") * LOCAL

    def get(block, lane):
        return back_ref[block, :, lane : lane + 128]

    project_group(group, first_pair, get, leg_ref, tend_ref)

    @pl.when(group == GROUPS - 1)
    def _():
        semi_implicit(first_pair, x_ref, tend_ref, grav_ref, stab_ref, out_ref)


def resident(shape):
    return pl.BlockSpec(shape, lambda *_: (0,) * len(shape))


STATE = (TRAJ, 2 * FIELDS, LOCAL, WIDTH)
LEG_BLOCK = pl.BlockSpec((GROUP, WIDTH, NHALF), lambda g: (g, 0, 0))
BAND_BLOCK = pl.BlockSpec((SPACE, 16, LANES), lambda g: (0, g, 0))
PARAMS = pltpu.CompilerParams(vmem_limit_bytes=56 * 1024 * 1024)


def to_fourier(state, legendre):
    return pl.pallas_call(
        legendre_kernel,
        grid=(GROUPS,),
        in_specs=[resident(STATE), LEG_BLOCK],
        out_specs=BAND_BLOCK,
        out_shape=jax.ShapeDtypeStruct((SPACE, ROWS, LANES), BF16),
        compiler_params=PARAMS,
        name="legendre",
    )(state, legendre)


def on_grid(fourier, sin_lat):
    tall, wide = zonal_tables()
    return pl.pallas_call(
        grid_kernel,
        out_shape=jax.ShapeDtypeStruct((4 * PAIRS, LANES), BF16),
        scratch_shapes=[pltpu.VMEM((NLON, LANES), BF16)],
        compiler_params=PARAMS,
        name="on_grid",
    )(fourier, jnp.asarray(tall), jnp.asarray(wide), sin_lat.reshape(1, NHALF))


def to_spectral(back, legendre, state, gravity, stability):
    smem = pl.BlockSpec(memory_space=pltpu.SMEM)
    return pl.pallas_call(
        project_kernel,
        grid=(GROUPS,),
        in_specs=[BAND_BLOCK, LEG_BLOCK, resident(STATE), smem, smem],
        out_specs=resident(STATE),
        out_shape=jax.ShapeDtypeStruct(STATE, F32),
        scratch_shapes=[pltpu.VMEM((TRAJ * 2 * FIELDS, 3, 8, WIDTH), F32)],
        compiler_params=PARAMS,
        name="project",
    )(back, legendre, state, gravity, stability)


def with_clones(state, clones):
    me = lax.axis_index("member")
    killed, source = clones[:, 0], clones[:, 1]
    picked = state[source % TRAJ]
    mine = (source // TRAJ == me)[:, None, None, None]
    received = lax.psum(jnp.where(mine, picked, 0.0), "member")
    rows = me * TRAJ + jnp.arange(TRAJ, dtype=jnp.int32)
    for entry in range(clones.shape[0]):
        here = (rows == killed[entry])[:, None, None, None]
        state = jnp.where(here, received[entry][None], state)
    return state


def exchange(blocks):
    return lax.all_to_all(blocks, "space", split_axis=0, concat_axis=0, tiled=True)


def shards(spectra, legendre, sin_lat, gravity, stability, clones):
    state = with_clones(spectra, clones)
    fourier = exchange(to_fourier(state, legendre))
    weighted = on_grid(fourier.reshape(SPACE * ROWS, LANES), sin_lat)
    back = exchange(weighted.reshape(SPACE, ROWS, LANES))
    return to_spectral(back, legendre, state, gravity, stability)


def solution(mesh):
    placed = (P("member", None, "space", None), P("space", None, None), P(), P(), P(), P())
    return jax.shard_map(
        shards,
        mesh=mesh,
        in_specs=placed,
        out_specs=P("member", None, "space", None),
        check_vma=False,
    )
```

```python
import functools
import math

import jax
import jax.numpy as jnp
import numpy as np
from jax import lax
from jax.experimental import pallas as pl
from jax.experimental.pallas import tpu as pltpu
from jax.sharding import PartitionSpec as P

NW = 640
WIDTH = NW + 1
NLON = 1280
NLAT = 768
NHALF = 384
PAIRS = 320
TRAJ = 4
FIELDS = 6
LOCAL = 20
SPACE = 16
GROUP = 4
GROUPS = LOCAL // GROUP
ROWS = 4 * LOCAL
FULL = 128 * FIELDS
LANES = FULL + 64 * FIELDS
PART = ((0, FULL), (FULL, LANES))
MEMBERS = 8
KILLED = 4
WIDE = 768
GROUPED = (GROUPS, TRAJ, 2 * FIELDS * GROUP, WIDE)
MESH = pl.DeviceIdType.MESH
DT = 0.25
WAVE_SCALE = 16.0
DIFFUSION = 0.02
F32 = jnp.float32
BF16 = jnp.bfloat16


@functools.cache
def zonal_tables():
    pair = np.arange(PAIRS)
    order = np.stack([pair, NW - 1 - pair], axis=1)
    phase = (order[:, :, None] * np.arange(NLON)) % NLON
    angle = phase * (2.0 * math.pi / NLON)
    table = np.stack([np.cos(angle), -np.sin(angle)], axis=2).reshape(4 * PAIRS, NLON)
    table = table.astype(jnp.bfloat16)
    return table, np.ascontiguousarray(table.T)


def row_col(rows, width):
    return (
        lax.broadcasted_iota(jnp.int32, (rows, width), 0),
        lax.broadcasted_iota(jnp.int32, (rows, width), 1),
    )


def sign_mask(pair):
    row, col = row_col(8, WIDTH)
    leading = (col < NW - pair).astype(jnp.int32)
    offset = jnp.where(leading == 1, col, col - (NW - pair))
    parity = (1 - 2 * (offset & 1)).astype(F32)
    sign = jnp.where(row >= 4, parity, 1.0)
    return jnp.where(((row >> 1) & 1) + leading == 1, sign, 0.0)


def swap4(value):
    return pltpu.roll(value, 4, 1)


def legendre_group(pair, xg_ref, leg_ref, put):
    row8, _ = row_col(8, WIDTH)
    odd = (row8 & 1) == 1
    results = []
    for k in range(GROUP):
        mask = sign_mask(pair + k)
        pieces = []
        for t in range(TRAJ):
            for f in range(FIELDS):
                real, imag = (
                    xg_ref[t, GROUP * c + k : GROUP * c + k + 1, 0:WIDTH] for c in (2 * f, 2 * f + 1)
                )
                pieces.append(jnp.where(odd, imag, real) * mask)
        lhs = jnp.concatenate(pieces, axis=0).astype(BF16)
        dots = jnp.dot(lhs, leg_ref[k], preferred_element_type=F32)
        results.append(dots.reshape(TRAJ * FIELDS, 8, NHALF))
    upper = lax.broadcasted_iota(jnp.int32, (TRAJ * FIELDS, 8, NHALF), 1) < 4
    hemispheres = ([], [])
    for k in range(0, GROUP, 2):
        first, second = results[k], results[k + 1]
        hemispheres[0].append(jnp.where(upper, first, swap4(second)))
        hemispheres[1].append(jnp.where(upper, swap4(first), second))
    low = lax.broadcasted_iota(jnp.int32, (16, 128), 1) < 64
    for side in range(2):
        one, two = hemispheres[side]
        for t in range(TRAJ):
            for level in range(FIELDS // 2):
                tiles = []
                for f in (2 * level, 2 * level + 1):
                    tile = jnp.concatenate([one[t * FIELDS + f], two[t * FIELDS + f]], axis=0)
                    put(4 * t + 2 * side, 128 * f, tile[:, 0:128].astype(BF16))
                    put(4 * t + 2 * side + 1, 128 * f, tile[:, 128:256].astype(BF16))
                    tiles.append(tile[:, 256:384])
                a, b = tiles
                lane = FULL + 128 * level
                put(4 * t + 2 * side, lane, jnp.where(low, a, pltpu.roll(b, 64, 1)).astype(BF16))
                put(
                    4 * t + 2 * side + 1, lane, jnp.where(low, pltpu.roll(a, 64, 1), b).astype(BF16)
                )


def latitude_rows(sin_ref, place):
    low = lax.broadcasted_iota(jnp.int32, (1, 128), 1) < 64
    zero, one, two = (sin_ref[:, 128 * i : 128 * i + 128] for i in range(3))
    swapped = pltpu.roll(two, 64, 1)
    second = (place & 1) == 1
    sign = jnp.where((place & 3) >= 2, -1.0, 1.0).astype(F32)
    full = jnp.where(second, one, zero) * sign
    half = jnp.where(second, jnp.where(low, swapped, two), jnp.where(low, two, swapped)) * sign
    return full, half


def forcing_of(spin, spread, heat, heat_swapped, coriolis):
    spun = spin + coriolis
    return (
        -spun * spread,
        spun * spin - 0.5 * spread * spread,
        -(heat + 0.5 * (heat + heat_swapped)) * spread,
    )


def grid_forward(part, sines, f_ref, wide_ref, forcing_ref):
    start, stop = PART[part]
    tile = 256

    def step(i, _):
        rows = pl.ds(pl.multiple_of(i * tile, tile), tile)
        sums = jnp.dot(wide_ref[rows, :], f_ref[:, start:stop], preferred_element_type=F32)
        sums = sums * (1.0 / NW)
        field = [sums[:, lane : lane + 128] for lane in range(0, stop - start, 128)]
        if part == 0:
            sets = [(field[a], field[2 + a], field[4 + a], field[5 - a]) for a in range(2)]
        else:
            sets = [(*field, pltpu.roll(field[2], 64, 1))]
        for a, fields in enumerate(sets):
            for g, made in enumerate(forcing_of(*fields, 2.0 * sines)):
                lane = start + 128 * (len(sets) * g + a)
                forcing_ref[rows, lane : lane + 128] = made.astype(BF16)
        return 0

    lax.fori_loop(0, NLON // tile, step, 0)


def grid_backward(part, sines, rows, forcing_ref, tall_ref, out_ref):
    start, stop = PART[part]
    weights = math.pi * jnp.sqrt(1.0 - sines * sines) / NLAT
    weights = jnp.concatenate([weights] * ((stop - start) // 128), axis=1)
    sums = jnp.dot(tall_ref[rows, :], forcing_ref[:, start:stop], preferred_element_type=F32)
    out_ref[rows, start:stop] = (sums * weights).astype(BF16)


def spread(axis, count, body):
    me = lax.axis_index(axis)

    def one(d, _):
        body(lax.rem(me + d, count))
        return 0

    lax.fori_loop(1, count, one, 0)


def main_kernel(
    clones_ref,
    x_ref,
    leg_any,
    tall_any,
    wide_any,
    sin_ref,
    back_ref,
    state_ref,
    leg_ref,
    tall_ref,
    wide_ref,
    xg_ref,
    hand_ref,
    landed_ref,
    shared_ref,
    send_ref,
    fourier_ref,
    forcing_ref,
    give_ref,
    leg_sem,
    table_sem,
    state_sem,
    own_sem,
    rs_send,
    rs_recv,
    ag_send,
    ag_recv,
    out_send,
    out_recv,
    half_send,
    half_recv,
    back_send,
    back_recv,
):
    member = lax.axis_index("member")
    place = lax.axis_index("space")
    sines = latitude_rows(sin_ref, place)
    leg_copies = []
    for g in range(GROUPS):
        some = pl.ds(g * GROUP, GROUP)
        leg_copies.append(
            pltpu.make_async_copy(leg_any.at[some], leg_ref.at[some], leg_sem.at[g])
        )
        leg_copies[-1].start()
    wide_copy = pltpu.make_async_copy(wide_any, wide_ref, table_sem.at[0])
    tall_copy = pltpu.make_async_copy(tall_any, tall_ref, table_sem.at[1])
    wide_copy.start()
    tall_copy.start()

    barrier = pltpu.get_barrier_semaphore()
    spread(
        "space",
        SPACE,
        lambda peer: pl.semaphore_signal(
            barrier, inc=1, device_id={"space": peer}, device_id_type=MESH
        ),
    )
    spread(
        "member",
        MEMBERS,
        lambda peer: pl.semaphore_signal(
            barrier, inc=1, device_id={"member": peer}, device_id_type=MESH
        ),
    )

    def scatter(q, g, peer, source):
        return pltpu.make_async_remote_copy(
            src_ref=hand_ref.at[q, g, peer],
            dst_ref=landed_ref.at[q, g, source],
            send_sem=rs_send.at[q, g, peer],
            recv_sem=rs_recv.at[q, g, source],
            device_id={"member": peer},
            device_id_type=MESH,
        )

    def gather(q, g, peer, source):
        return pltpu.make_async_remote_copy(
            src_ref=shared_ref.at[q, g, source],
            dst_ref=shared_ref.at[q, g, source],
            send_sem=ag_send.at[q, g, peer],
            recv_sem=ag_recv.at[q, g, source],
            device_id={"member": peer},
            device_id_type=MESH,
        )

    def regroup(g):
        some = slice(g * GROUP, g * GROUP + GROUP)
        for t in range(TRAJ):
            rows = jnp.concatenate([x_ref[t, c, some, :] for c in range(2 * FIELDS)], axis=0)
            xg_ref[g, t, :, 0:WIDTH] = rows
            xg_ref[g, t, :, NW:WIDE] = jnp.where(
                lax.broadcasted_iota(jnp.int32, (48, 128), 1) < 1, rows[:, NW:WIDTH], 0.0
            )

    def offer(q, g):
        for entry in range(KILLED):
            source = clones_ref[entry, 1]
            value = xg_ref[g, source & (TRAJ - 1)]
            high = value.astype(BF16)
            value = high if q == 0 else (value - high.astype(F32)).astype(BF16)
            value = jnp.where((source >> 2) == member, value.astype(F32), 0.0).astype(BF16)
            hand_ref[q, g, 2 * entry] = value[:, 0 : WIDE // 2]
            hand_ref[q, g, 2 * entry + 1] = value[:, WIDE // 2 : WIDE]
        spread("member", MEMBERS, lambda peer: scatter(q, g, peer, member).start())

    def settle(q, g):
        spread("member", MEMBERS, lambda peer: scatter(q, g, peer, peer).wait_recv())

        def add(d, total):
            return total + landed_ref[q, g, lax.rem(member + d, MEMBERS)].astype(F32)

        total = lax.fori_loop(1, MEMBERS, add, hand_ref[q, g, member].astype(F32))
        shared_ref[q, g, member] = total.astype(BF16)
        spread("member", MEMBERS, lambda peer: gather(q, g, peer, member).start())

    def arrived(q, g):
        spread("member", MEMBERS, lambda peer: gather(q, g, peer, peer).wait_recv())

    def adopt(g, parts):
        for entry in range(KILLED):
            value = None
            for q in range(parts):
                piece = jnp.concatenate(
                    [shared_ref[q, g, 2 * entry], shared_ref[q, g, 2 * entry + 1]], axis=1
                ).astype(F32)
                value = piece if value is None else value + piece
            for t in range(TRAJ):
                killed = clones_ref[entry, 0] == member * TRAJ + t
                xg_ref[g, t] = jnp.where(killed, value, xg_ref[g, t])

    def outward(g, peer, source):
        lanes = pl.ds(0, FULL)
        return pltpu.make_async_remote_copy(
            src_ref=send_ref.at[peer, pl.ds(g * 16, 16), lanes],
            dst_ref=fourier_ref.at[pl.ds(source * ROWS + g * 16, 16), lanes],
            send_sem=out_send.at[g, peer],
            recv_sem=out_recv.at[g, source],
            device_id={"space": peer},
            device_id_type=MESH,
        )

    def outward_half(peer, source):
        lanes = pl.ds(FULL, LANES - FULL)
        return pltpu.make_async_remote_copy(
            src_ref=send_ref.at[peer, :, lanes],
            dst_ref=fourier_ref.at[pl.ds(source * ROWS, ROWS), lanes],
            send_sem=half_send.at[peer],
            recv_sem=half_recv.at[source],
            device_id={"space": peer},
            device_id_type=MESH,
        )

    def homeward(part, peer, source):
        start, stop = PART[part]
        lanes = pl.ds(start, stop - start)
        return pltpu.make_async_remote_copy(
            src_ref=give_ref.at[pl.ds(peer * ROWS, ROWS), lanes],
            dst_ref=back_ref.at[source, :, lanes],
            send_sem=back_send.at[part, peer],
            recv_sem=back_recv.at[part, source],
            device_id={"space": peer},
            device_id_type=MESH,
        )

    for g in range(GROUPS):
        regroup(g)
        if g == 0:
            pl.semaphore_wait(barrier, SPACE + MEMBERS - 2)
        offer(0, g)
    settle(0, 0)

    def legendre_step(g, _):
        @pl.when(g + 1 < GROUPS)
        def _():
            settle(0, g + 1)

        arrived(0, g)
        adopt(g, 1)
        some = pl.ds(g * GROUP, GROUP)
        pltpu.make_async_copy(leg_any.at[some], leg_ref.at[some], leg_sem.at[g]).wait()

        def put(block, lane, value):
            send_ref[block, pl.ds(pl.multiple_of(g * 16, 16), 16), lane : lane + 128] = value

        legendre_group(
            place * LOCAL + g * GROUP, xg_ref.at[g], leg_ref.at[pl.ds(g * GROUP, GROUP)], put
        )
        spread("space", SPACE, lambda peer: outward(g, peer, place).start())
        return 0

    lax.fori_loop(0, GROUPS, legendre_step, 0)
    own_out = pltpu.make_async_copy(
        send_ref.at[place], fourier_ref.at[pl.ds(place * ROWS, ROWS)], own_sem.at[0]
    )
    own_out.start()
    spread("space", SPACE, lambda peer: outward_half(peer, place).start())

    def each_group(body):
        def one(g, _):
            body(g)
            return 0

        lax.fori_loop(0, GROUPS, one, 0)

    each_group(lambda g: offer(1, g))
    wide_copy.wait()
    tall_copy.wait()
    own_out.wait()
    each_group(
        lambda g: spread("space", SPACE, lambda peer: outward(g, peer, peer).wait_recv())
    )
    quarter = 4 * ROWS
    for part in range(2):
        if part == 1:
            spread("space", SPACE, lambda peer: outward_half(peer, peer).wait_recv())
        grid_forward(part, sines[part], fourier_ref, wide_ref, forcing_ref)

        def backward(i, _, part=part):
            block = lax.rem((place >> 2) + i, 4)
            rows = pl.ds(pl.multiple_of(block * quarter, quarter), quarter)
            grid_backward(part, sines[part], rows, forcing_ref, tall_ref, give_ref)

            def one(j, _):
                peer = block * 4 + lax.rem((place & 3) + j, 4)

                @pl.when(peer != place)
                def _():
                    homeward(part, peer, place).start()

                return 0

            lax.fori_loop(0, 4, one, 0)
            return 0

        lax.fori_loop(0, 4, backward, 0)
        if part == 0:
            each_group(lambda g: settle(1, g))
    own_back = pltpu.make_async_copy(
        give_ref.at[pl.ds(place * ROWS, ROWS)], back_ref.at[place], own_sem.at[1]
    )
    own_back.start()

    def complete(g):
        arrived(1, g)
        adopt(g, 2)

    each_group(complete)
    state_copy = pltpu.make_async_copy(xg_ref, state_ref, state_sem)
    state_copy.start()
    for q in range(2):
        each_group(
            lambda g: spread("member", MEMBERS, lambda peer: scatter(q, g, peer, peer).wait_send())
        )
        each_group(
            lambda g: spread("member", MEMBERS, lambda peer: gather(q, g, peer, member).wait_send())
        )
    each_group(
        lambda g: spread("space", SPACE, lambda peer: outward(g, peer, place).wait_send())
    )
    spread("space", SPACE, lambda peer: outward_half(peer, place).wait_send())
    for part in range(2):
        spread("space", SPACE, lambda peer: homeward(part, peer, place).wait_send())
        spread("space", SPACE, lambda peer: homeward(part, peer, peer).wait_recv())
    own_back.wait()
    state_copy.wait()


def project_group(group, first_pair, get, leg_ref):
    low = lax.broadcasted_iota(jnp.int32, (16, 128), 1) < 64
    hemispheres = ([], [])
    for side in range(2):
        for t in range(TRAJ):
            for level in range(FIELDS // 2):
                lane = FULL + 128 * level
                a = get(4 * t + 2 * side, lane).astype(F32)
                b = get(4 * t + 2 * side + 1, lane).astype(F32)
                last = (
                    jnp.where(low, a, pltpu.roll(b, 64, 1)),
                    jnp.where(low, pltpu.roll(a, 64, 1), b),
                )
                for h in range(2):
                    f = 2 * level + h
                    hemispheres[side].append(
                        jnp.concatenate(
                            [
                                get(4 * t + 2 * side, 128 * f).astype(F32),
                                get(4 * t + 2 * side + 1, 128 * f).astype(F32),
                                last[h],
                            ],
                            axis=1,
                        )
                    )
    north = jnp.stack(hemispheres[0])
    south = jnp.stack(hemispheres[1])
    upper = lax.broadcasted_iota(jnp.int32, (TRAJ * FIELDS, 8, NHALF), 1) < 4
    row8, _ = row_col(8, WIDTH)
    odd = ((row8 & 1) == 1)[None]
    sums = []
    for k in range(GROUP):
        rows = slice(8 * (k // 2), 8 * (k // 2) + 8)
        n, s = north[:, rows], south[:, rows]
        lhs = jnp.where(upper, n, swap4(s)) if k % 2 == 0 else jnp.where(upper, swap4(n), s)
        lhs = lhs.reshape(8 * TRAJ * FIELDS, NHALF).astype(BF16)
        dots = lax.dot_general(
            lhs, leg_ref[k], (((1,), (1,)), ((), ())), preferred_element_type=F32
        ).reshape(TRAJ * FIELDS, 8, WIDTH)
        dots = dots * sign_mask(first_pair + group * GROUP + k)[None]
        dots = dots + pltpu.roll(dots, 4, 1)
        sums.append(dots + pltpu.roll(dots, 2, 1))
    place = (row8 & 3)[None]
    upper = (row8 < 4)[None]
    mixed = []
    for part in range(2):
        some = None
        for k in range(GROUP):
            turned = pltpu.roll(sums[k], 1, 1)
            every = jnp.where(odd, turned, sums[k]) if part == 0 else jnp.where(odd, sums[k], turned)
            some = every if k == 0 else jnp.where(place == k, every, some)
        mixed.append(some)
    return jnp.where(upper, mixed[0], mixed[1])


def semi_implicit(pair, group, state_ref, tend, grav_ref, stab_ref, new_ref):
    g = [[grav_ref[a, b] for b in range(2)] for a in range(2)]
    s = [[stab_ref[a, b] for b in range(2)] for a in range(2)]
    k = [[g[a][0] * s[0][b] + g[a][1] * s[1][b] for b in range(2)] for a in range(2)]
    row, col = row_col(8, WIDTH)
    pair = pair + (row & 3)
    degree = jnp.where(col < NW - pair, col + pair, (NW - 1 - pair) + col - (NW - pair))
    lam = WAVE_SCALE * (degree * (degree + 1)).astype(F32) / float(NW * NW)
    damp = 1.0 / (1.0 + DIFFUSION * lam * lam)
    coupling = DT * DT * lam
    diag = [1.0 + coupling * k[a][a] for a in range(2)]
    cross = [coupling * k[0][1], coupling * k[1][0]]
    inverse = 1.0 / (diag[0] * diag[1] - cross[0] * cross[1])
    upper = row < 4
    here = (row >> 2) == (group & 1)
    for t in range(TRAJ):

        def moved(f):
            return state_ref[0, t, 8 * f : 8 * f + 8, 0:WIDTH] + DT * tend[t * FIELDS + f]

        def place(f, value):
            turned = pltpu.roll(value, 4, 0)
            for part in range(2):
                both = jnp.where(upper, turned, value) if part else jnp.where(upper, value, turned)
                slot = new_ref.at[2 * (t * FIELDS + f) + part, group >> 1]
                slot[...] = jnp.where(here, both, slot[...])

        for a in range(2):
            place(a, damp * moved(a))
        heat = [moved(4), moved(5)]
        right = [
            moved(2 + a) + DT * lam * (g[a][0] * heat[0] + g[a][1] * heat[1]) for a in range(2)
        ]
        new = [
            (diag[1] * right[0] - cross[0] * right[1]) * inverse,
            (diag[0] * right[1] - cross[1] * right[0]) * inverse,
        ]
        for a in range(2):
            place(2 + a, damp * new[a])
            place(4 + a, damp * (heat[a] - DT * (s[a][0] * new[0] + s[a][1] * new[1])))


def project_kernel(back_ref, leg_ref, state_ref, grav_ref, stab_ref, out_ref, new_ref):
    group = pl.program_id(0)
    first_pair = lax.axis_index("space") * LOCAL

    def get(block, lane):
        return back_ref[block, :, lane : lane + 128]

    tend = project_group(group, first_pair, get, leg_ref)
    semi_implicit(first_pair + group * GROUP, group, state_ref, tend, grav_ref, stab_ref, new_ref)

    @pl.when(group == GROUPS - 1)
    def _():
        def finish(t, _):
            for c in range(2 * FIELDS):
                for tile in range(3):
                    rows = min(8, LOCAL - 8 * tile)
                    value = new_ref[2 * FIELDS * t + c, tile, 0:rows, :]
                    out_ref[t, c, 8 * tile : 8 * tile + rows, :] = value
            return 0

        lax.fori_loop(0, TRAJ, finish, 0)


def resident(shape):
    return pl.BlockSpec(shape, lambda *_: (0,) * len(shape))


STATE = (TRAJ, 2 * FIELDS, LOCAL, WIDTH)
LEG_BLOCK = pl.BlockSpec((GROUP, WIDTH, NHALF), lambda g: (g, 0, 0))
BAND_BLOCK = pl.BlockSpec((SPACE, 16, LANES), lambda g: (0, g, 0))


def to_bands(spectra, legendre, sin_lat, clones):
    tall, wide = zonal_tables()
    anywhere = pl.BlockSpec(memory_space=pl.ANY)
    vmem = pl.BlockSpec(memory_space=pltpu.VMEM)
    smem = pl.BlockSpec(memory_space=pltpu.SMEM)
    dma = pltpu.SemaphoreType.DMA
    pieces = (2, GROUPS, MEMBERS, 2 * FIELDS * GROUP, WIDE // 2)
    band = (4 * PAIRS, LANES)
    return pl.pallas_call(
        main_kernel,
        in_specs=[smem, vmem, anywhere, anywhere, anywhere, vmem],
        out_specs=[anywhere, anywhere],
        out_shape=[
            jax.ShapeDtypeStruct((SPACE, ROWS, LANES), BF16),
            jax.ShapeDtypeStruct(GROUPED, F32),
        ],
        scratch_shapes=[
            pltpu.VMEM((LOCAL, WIDTH, NHALF), BF16),
            pltpu.VMEM((4 * PAIRS, NLON), BF16),
            pltpu.VMEM((NLON, 4 * PAIRS), BF16),
            pltpu.VMEM(GROUPED, F32),
            pltpu.VMEM(pieces, BF16),
            pltpu.VMEM(pieces, BF16),
            pltpu.VMEM(pieces, BF16),
            pltpu.VMEM((SPACE, ROWS, LANES), BF16),
            pltpu.VMEM(band, BF16),
            pltpu.VMEM(band, BF16),
            pltpu.VMEM(band, BF16),
            dma((GROUPS,)),
            dma((2,)),
            dma,
            dma((2,)),
            dma((2, GROUPS, MEMBERS)),
            dma((2, GROUPS, MEMBERS)),
            dma((2, GROUPS, MEMBERS)),
            dma((2, GROUPS, MEMBERS)),
            dma((GROUPS, SPACE)),
            dma((GROUPS, SPACE)),
            dma((SPACE,)),
            dma((SPACE,)),
            dma((2, SPACE)),
            dma((2, SPACE)),
        ],
        compiler_params=pltpu.CompilerParams(
            vmem_limit_bytes=60 * 1024 * 1024, collective_id=0, has_side_effects=True
        ),
        name="bands",
    )(clones, spectra, legendre, jnp.asarray(tall), jnp.asarray(wide), sin_lat.reshape(1, NHALF))


def to_spectral(back, legendre, state, gravity, stability):
    smem = pl.BlockSpec(memory_space=pltpu.SMEM)
    return pl.pallas_call(
        project_kernel,
        grid=(GROUPS,),
        in_specs=[
            BAND_BLOCK,
            LEG_BLOCK,
            pl.BlockSpec((1,) + GROUPED[1:], lambda g: (g, 0, 0, 0)),
            smem,
            smem,
        ],
        out_specs=resident(STATE),
        out_shape=jax.ShapeDtypeStruct(STATE, F32),
        scratch_shapes=[pltpu.VMEM((TRAJ * 2 * FIELDS, 3, 8, WIDTH), F32)],
        compiler_params=pltpu.CompilerParams(vmem_limit_bytes=56 * 1024 * 1024),
        name="project",
    )(back, legendre, state, gravity, stability)


def shards(spectra, legendre, sin_lat, gravity, stability, clones):
    back, state = to_bands(spectra, legendre, sin_lat, clones)
    return to_spectral(back, legendre, state, gravity, stability)


def solution(mesh):
    placed = (P("member", None, "space", None), P("space", None, None), P(), P(), P(), P())
    return jax.shard_map(
        shards,
        mesh=mesh,
        in_specs=placed,
        out_specs=P("member", None, "space", None),
        check_vma=False,
    )
```

```python
import functools
import math

import jax
import jax.numpy as jnp
import numpy as np
from jax import lax
from jax.experimental import pallas as pl
from jax.experimental.pallas import tpu as pltpu
from jax.sharding import PartitionSpec as P

NW = 640
WIDTH = NW + 1
NLON = 1280
NLAT = 768
NHALF = 384
PAIRS = 320
TRAJ = 4
FIELDS = 6
LOCAL = 20
SPACE = 16
GROUP = 4
GROUPS = LOCAL // GROUP
ROWS = 4 * LOCAL
FULL = 128 * FIELDS
LANES = FULL + 64 * FIELDS
PART = ((0, FULL), (FULL, LANES))
MEMBERS = 8
KILLED = 4
WIDE = 768
GROUPED = (GROUPS, 2 * FIELDS, GROUP, TRAJ, WIDTH)
MIX = 2 * FIELDS * GROUP
MESH = pl.DeviceIdType.MESH
DT = 0.25
WAVE_SCALE = 16.0
DIFFUSION = 0.02
F32 = jnp.float32
BF16 = jnp.bfloat16


@functools.cache
def zonal_tables():
    pair = np.arange(PAIRS)
    order = np.stack([pair, NW - 1 - pair], axis=1)
    phase = (order[:, :, None] * np.arange(NLON)) % NLON
    angle = phase * (2.0 * math.pi / NLON)
    table = np.stack([np.cos(angle), -np.sin(angle)], axis=2).reshape(4 * PAIRS, NLON)
    table = table.astype(jnp.bfloat16)
    return table, np.ascontiguousarray(table.T)


def row_col(rows, width):
    return (
        lax.broadcasted_iota(jnp.int32, (rows, width), 0),
        lax.broadcasted_iota(jnp.int32, (rows, width), 1),
    )


def sign_mask(pair):
    row, col = row_col(8, WIDTH)
    leading = (col < NW - pair).astype(jnp.int32)
    offset = jnp.where(leading == 1, col, col - (NW - pair))
    parity = (1 - 2 * (offset & 1)).astype(F32)
    sign = jnp.where(row >= 4, parity, 1.0)
    return jnp.where(((row >> 1) & 1) + leading == 1, sign, 0.0)


def swap4(value):
    return pltpu.roll(value, 4, 1)


def legendre_group(pair, now_ref, leg_ref, put):
    row8, _ = row_col(8, WIDTH)
    odd = (row8 & 1) == 1
    results = []
    for k in range(GROUP):
        mask = sign_mask(pair + k)
        pieces = []
        for t in range(TRAJ):
            for f in range(FIELDS):
                first = MIX * t + 2 * GROUP * f + k
                real, imag = (now_ref[row : row + 1, 0:WIDTH] for row in (first, first + GROUP))
                pieces.append(jnp.where(odd, imag, real) * mask)
        lhs = jnp.concatenate(pieces, axis=0).astype(BF16)
        dots = jnp.dot(lhs, leg_ref[k], preferred_element_type=F32)
        results.append(dots.reshape(TRAJ * FIELDS, 8, NHALF))
    upper = lax.broadcasted_iota(jnp.int32, (TRAJ * FIELDS, 8, NHALF), 1) < 4
    hemispheres = ([], [])
    for k in range(0, GROUP, 2):
        first, second = results[k], results[k + 1]
        hemispheres[0].append(jnp.where(upper, first, swap4(second)))
        hemispheres[1].append(jnp.where(upper, swap4(first), second))
    low = lax.broadcasted_iota(jnp.int32, (16, 128), 1) < 64
    for side in range(2):
        one, two = hemispheres[side]
        for t in range(TRAJ):
            for level in range(FIELDS // 2):
                tiles = []
                for f in (2 * level, 2 * level + 1):
                    tile = jnp.concatenate([one[t * FIELDS + f], two[t * FIELDS + f]], axis=0)
                    put(4 * t + 2 * side, 128 * f, tile[:, 0:128].astype(BF16))
                    put(4 * t + 2 * side + 1, 128 * f, tile[:, 128:256].astype(BF16))
                    tiles.append(tile[:, 256:384])
                a, b = tiles
                lane = FULL + 128 * level
                put(4 * t + 2 * side, lane, jnp.where(low, a, pltpu.roll(b, 64, 1)).astype(BF16))
                put(
                    4 * t + 2 * side + 1, lane, jnp.where(low, pltpu.roll(a, 64, 1), b).astype(BF16)
                )


def latitude_rows(sin_ref, place):
    low = lax.broadcasted_iota(jnp.int32, (1, 128), 1) < 64
    zero, one, two = (sin_ref[:, 128 * i : 128 * i + 128] for i in range(3))
    swapped = pltpu.roll(two, 64, 1)
    second = (place & 1) == 1
    sign = jnp.where((place & 3) >= 2, -1.0, 1.0).astype(F32)
    full = jnp.where(second, one, zero) * sign
    half = jnp.where(second, jnp.where(low, swapped, two), jnp.where(low, two, swapped)) * sign
    return full, half


def forcing_of(spin, spread, heat, heat_swapped, coriolis):
    spun = spin + coriolis
    return (
        -spun * spread,
        spun * spin - 0.5 * spread * spread,
        -(heat + 0.5 * (heat + heat_swapped)) * spread,
    )


def grid_forward(part, sines, f_ref, wide_ref, forcing_ref):
    start, stop = PART[part]
    tile = 256

    def step(i, _):
        rows = pl.ds(pl.multiple_of(i * tile, tile), tile)
        sums = jnp.dot(wide_ref[rows, :], f_ref[:, start:stop], preferred_element_type=F32)
        sums = sums * (1.0 / NW)
        field = [sums[:, lane : lane + 128] for lane in range(0, stop - start, 128)]
        if part == 0:
            sets = [(field[a], field[2 + a], field[4 + a], field[5 - a]) for a in range(2)]
        else:
            sets = [(*field, pltpu.roll(field[2], 64, 1))]
        for a, fields in enumerate(sets):
            for g, made in enumerate(forcing_of(*fields, 2.0 * sines)):
                lane = start + 128 * (len(sets) * g + a)
                forcing_ref[rows, lane : lane + 128] = made.astype(BF16)
        return 0

    lax.fori_loop(0, NLON // tile, step, 0)


def grid_backward(part, sines, rows, forcing_ref, tall_ref, out_ref):
    start, stop = PART[part]
    weights = math.pi * jnp.sqrt(1.0 - sines * sines) / NLAT
    weights = jnp.concatenate([weights] * ((stop - start) // 128), axis=1)
    sums = jnp.dot(tall_ref[rows, :], forcing_ref[:, start:stop], preferred_element_type=F32)
    out_ref[rows, start:stop] = (sums * weights).astype(BF16)


def one_hot(condition):
    return jnp.where(condition, 1.0, 0.0).astype(BF16)


def square(rows):
    return row_col(rows, TRAJ * MIX)


def select_rows(clones_ref, member):
    row, col = square(MIX)
    parts = []
    for entry in range(KILLED):
        source = clones_ref[1, entry]
        wanted = jnp.where((source >> 2) == member, source & (TRAJ - 1), TRAJ)
        parts.append(one_hot((row == (col >> 2)) & ((col & 3) == wanted)))
    return jnp.concatenate(parts, axis=0)


def entry_of(clones_ref, number):
    found = KILLED
    for entry in range(KILLED):
        found = jnp.where(clones_ref[0, entry] == number, entry, found)
    return found


def entry_columns(col):
    return sum((col >= MIX * i).astype(jnp.int32) for i in range(1, KILLED))


def keep_and_put(clones_ref, member):
    row, col = square(MIX)
    entry = entry_columns(col)
    keep, put = [], []
    for t in range(TRAJ):
        found = entry_of(clones_ref, member * TRAJ + t)
        own = jnp.where(found == KILLED, t, TRAJ)
        keep.append(one_hot((row == (col >> 2)) & ((col & 3) == own)))
        put.append(one_hot((row == col - MIX * entry) & (entry == found)))
    return jnp.concatenate(keep, axis=0), jnp.concatenate(put, axis=0)


def by_trajectory(values, row):
    mixed = values[0]
    for t in range(1, TRAJ):
        mixed = jnp.where(row == t, values[t], mixed)
    return mixed


def place_rows(clones_ref, member):
    row, col = square(TRAJ * MIX)
    entry = entry_columns(col)
    found = [entry_of(clones_ref, member * TRAJ + t) for t in range(TRAJ)]
    return one_hot((entry == by_trajectory(found, row & 3)) & ((row >> 2) == col - MIX * entry))


def spread(axis, count, body):
    me = lax.axis_index(axis)

    def one(d, _):
        body(lax.rem(me + d, count))
        return 0

    lax.fori_loop(1, count, one, 0)


def main_kernel(
    clones_ref,
    x_any,
    leg_any,
    tall_any,
    wide_any,
    sin_ref,
    back_ref,
    state_ref,
    leg_ref,
    tall_ref,
    wide_ref,
    xg_ref,
    half_ref,
    now_ref,
    hand_ref,
    landed_ref,
    shared_ref,
    send_ref,
    fourier_ref,
    forcing_ref,
    give_ref,
    x_sem,
    leg_sem,
    table_sem,
    state_sem,
    own_sem,
    rs_send,
    rs_recv,
    ag_send,
    ag_recv,
    out_send,
    out_recv,
    half_send,
    half_recv,
    back_send,
    back_recv,
):
    member = lax.axis_index("member")
    place = lax.axis_index("space")
    sines = latitude_rows(sin_ref, place)

    def x_copy(g):
        some = pl.ds(g * GROUP, GROUP)
        return pltpu.make_async_copy(x_any.at[:, some], xg_ref.at[g], x_sem.at[g])

    def leg_copy(g):
        some = pl.ds(g * GROUP, GROUP)
        return pltpu.make_async_copy(leg_any.at[some], leg_ref.at[some], leg_sem.at[g])

    for copy in (x_copy, leg_copy):
        for g in range(GROUPS):
            copy(g).start()
    wide_copy = pltpu.make_async_copy(wide_any, wide_ref, table_sem.at[0])
    tall_copy = pltpu.make_async_copy(tall_any, tall_ref, table_sem.at[1])
    wide_copy.start()
    tall_copy.start()

    barrier = pltpu.get_barrier_semaphore()
    spread(
        "space",
        SPACE,
        lambda peer: pl.semaphore_signal(
            barrier, inc=1, device_id={"space": peer}, device_id_type=MESH
        ),
    )
    spread(
        "member",
        MEMBERS,
        lambda peer: pl.semaphore_signal(
            barrier, inc=1, device_id={"member": peer}, device_id_type=MESH
        ),
    )

    def scatter(q, g, peer, source):
        return pltpu.make_async_remote_copy(
            src_ref=hand_ref.at[q, g, peer],
            dst_ref=landed_ref.at[q, g, source],
            send_sem=rs_send.at[q, g, peer],
            recv_sem=rs_recv.at[q, g, source],
            device_id={"member": peer},
            device_id_type=MESH,
        )

    def gather(q, g, peer, source):
        return pltpu.make_async_remote_copy(
            src_ref=shared_ref.at[q, g, source],
            dst_ref=shared_ref.at[q, g, source],
            send_sem=ag_send.at[q, g, peer],
            recv_sem=ag_recv.at[q, g, source],
            device_id={"member": peer},
            device_id_type=MESH,
        )

    def regroup(g):
        rows = jnp.concatenate(
            [xg_ref[g, c, p] for c in range(2 * FIELDS) for p in range(GROUP)], axis=0
        )
        _, lane = row_col(TRAJ * MIX, 128)
        value = jnp.concatenate(
            [rows[:, 0:NW], jnp.where(lane < 1, rows[:, NW:WIDTH], 0.0)], axis=1
        )
        high = value.astype(BF16)
        half_ref[0, g] = high
        half_ref[1, g] = (value - high.astype(F32)).astype(BF16)

    selection = select_rows(clones_ref, member)

    def offer(q, g):
        value = jnp.dot(selection, half_ref[q, g], preferred_element_type=F32).astype(BF16)
        for entry in range(KILLED):
            rows = slice(MIX * entry, MIX * entry + MIX)
            hand_ref[q, g, 2 * entry] = value[rows, 0 : WIDE // 2]
            hand_ref[q, g, 2 * entry + 1] = value[rows, WIDE // 2 : WIDE]
        spread("member", MEMBERS, lambda peer: scatter(q, g, peer, member).start())

    def settle(q, g):
        spread("member", MEMBERS, lambda peer: scatter(q, g, peer, peer).wait_recv())

        def add(d, total):
            return total + landed_ref[q, g, lax.rem(member + d, MEMBERS)].astype(F32)

        total = lax.fori_loop(1, MEMBERS, add, hand_ref[q, g, member].astype(F32))
        shared_ref[q, g, member] = total.astype(BF16)
        spread("member", MEMBERS, lambda peer: gather(q, g, peer, member).start())

    def arrived(q, g):
        spread("member", MEMBERS, lambda peer: gather(q, g, peer, peer).wait_recv())

    def received(q, g):
        return jnp.concatenate(
            [
                jnp.concatenate([shared_ref[q, g, 2 * e], shared_ref[q, g, 2 * e + 1]], axis=1)
                for e in range(KILLED)
            ],
            axis=0,
        )

    def outward(g, peer, source):
        lanes = pl.ds(0, FULL)
        return pltpu.make_async_remote_copy(
            src_ref=send_ref.at[peer, pl.ds(g * 16, 16), lanes],
            dst_ref=fourier_ref.at[pl.ds(source * ROWS + g * 16, 16), lanes],
            send_sem=out_send.at[g, peer],
            recv_sem=out_recv.at[g, source],
            device_id={"space": peer},
            device_id_type=MESH,
        )

    def outward_half(peer, source):
        lanes = pl.ds(FULL, LANES - FULL)
        return pltpu.make_async_remote_copy(
            src_ref=send_ref.at[peer, :, lanes],
            dst_ref=fourier_ref.at[pl.ds(source * ROWS, ROWS), lanes],
            send_sem=half_send.at[peer],
            recv_sem=half_recv.at[source],
            device_id={"space": peer},
            device_id_type=MESH,
        )

    def homeward(part, peer, source):
        start, stop = PART[part]
        lanes = pl.ds(start, stop - start)
        return pltpu.make_async_remote_copy(
            src_ref=give_ref.at[pl.ds(peer * ROWS, ROWS), lanes],
            dst_ref=back_ref.at[source, :, lanes],
            send_sem=back_send.at[part, peer],
            recv_sem=back_recv.at[part, source],
            device_id={"space": peer},
            device_id_type=MESH,
        )

    x_copy(0).wait()
    regroup(0)
    pl.semaphore_wait(barrier, SPACE + MEMBERS - 2)
    offer(0, 0)

    def rest(g, _):
        x_copy(g).wait()
        regroup(g)
        offer(0, g)
        return 0

    lax.fori_loop(1, GROUPS, rest, 0)
    keep, put_rows = keep_and_put(clones_ref, member)
    settle(0, 0)

    def legendre_step(g, _):
        @pl.when(g + 1 < GROUPS)
        def _():
            settle(0, g + 1)

        arrived(0, g)
        now = jnp.dot(keep, half_ref[0, g], preferred_element_type=F32)
        now_ref[...] = now + jnp.dot(put_rows, received(0, g), preferred_element_type=F32)
        leg_copy(g).wait()

        def put(block, lane, value):
            send_ref[block, pl.ds(pl.multiple_of(g * 16, 16), 16), lane : lane + 128] = value

        legendre_group(
            place * LOCAL + g * GROUP, now_ref, leg_ref.at[pl.ds(g * GROUP, GROUP)], put
        )
        spread("space", SPACE, lambda peer: outward(g, peer, place).start())
        return 0

    lax.fori_loop(0, GROUPS, legendre_step, 0)
    own_out = pltpu.make_async_copy(
        send_ref.at[place], fourier_ref.at[pl.ds(place * ROWS, ROWS)], own_sem.at[0]
    )
    own_out.start()
    spread("space", SPACE, lambda peer: outward_half(peer, place).start())

    def each_group(body):
        def one(g, _):
            body(g)
            return 0

        lax.fori_loop(0, GROUPS, one, 0)

    each_group(lambda g: offer(1, g))
    wide_copy.wait()
    tall_copy.wait()
    own_out.wait()
    each_group(
        lambda g: spread("space", SPACE, lambda peer: outward(g, peer, peer).wait_recv())
    )
    quarter = 4 * ROWS
    for part in range(2):
        if part == 1:
            spread("space", SPACE, lambda peer: outward_half(peer, peer).wait_recv())
        grid_forward(part, sines[part], fourier_ref, wide_ref, forcing_ref)

        def backward(i, _, part=part):
            block = lax.rem((place >> 2) + i, 4)
            rows = pl.ds(pl.multiple_of(block * quarter, quarter), quarter)
            grid_backward(part, sines[part], rows, forcing_ref, tall_ref, give_ref)

            def one(j, _):
                peer = block * 4 + lax.rem((place & 3) + j, 4)

                @pl.when(peer != place)
                def _():
                    homeward(part, peer, place).start()

                return 0

            lax.fori_loop(0, 4, one, 0)
            return 0

        lax.fori_loop(0, 4, backward, 0)
        if part == 0:
            each_group(lambda g: settle(1, g))
    own_back = pltpu.make_async_copy(
        give_ref.at[pl.ds(place * ROWS, ROWS)], back_ref.at[place], own_sem.at[1]
    )
    own_back.start()

    placing = place_rows(clones_ref, member)
    row, _ = row_col(TRAJ, WIDTH)
    killed = by_trajectory(
        [entry_of(clones_ref, member * TRAJ + t) for t in range(TRAJ)], row
    )

    def complete(g):
        arrived(1, g)
        value = sum(
            jnp.dot(placing, received(q, g), preferred_element_type=F32) for q in range(2)
        )
        for c in range(2 * FIELDS):
            for p in range(GROUP):
                first = (c * GROUP + p) * TRAJ
                new = value[first : first + TRAJ, 0:WIDTH]
                xg_ref[g, c, p] = jnp.where(killed < KILLED, new, xg_ref[g, c, p])

    each_group(complete)
    state_copy = pltpu.make_async_copy(xg_ref, state_ref, state_sem)
    state_copy.start()
    for q in range(2):
        each_group(
            lambda g: spread("member", MEMBERS, lambda peer: scatter(q, g, peer, peer).wait_send())
        )
        each_group(
            lambda g: spread("member", MEMBERS, lambda peer: gather(q, g, peer, member).wait_send())
        )
    each_group(
        lambda g: spread("space", SPACE, lambda peer: outward(g, peer, place).wait_send())
    )
    spread("space", SPACE, lambda peer: outward_half(peer, place).wait_send())
    for part in range(2):
        spread("space", SPACE, lambda peer: homeward(part, peer, place).wait_send())
        spread("space", SPACE, lambda peer: homeward(part, peer, peer).wait_recv())
    own_back.wait()
    state_copy.wait()


def unmix():
    row, col = row_col(128, 128)
    t, half, side, part, pair = row & 3, (row >> 2) & 1, (row >> 3) & 1, (row >> 4) & 1, row >> 5
    return one_hot(col == 32 * t + 16 * side + 4 * pair + 2 * half + part)


def project_rows(back_ref):
    low = lax.broadcasted_iota(jnp.int32, (128, 128), 1) < 64
    order = unmix()

    def column(odd, lane):
        return jnp.concatenate(
            [
                back_ref[4 * t + 2 * side + odd, :, lane : lane + 128]
                for t in range(TRAJ)
                for side in range(2)
            ],
            axis=0,
        )

    fields = []
    for level in range(FIELDS // 2):
        lanes = [256 * level, 256 * level + 128, FULL + 128 * level]
        mixed = jnp.concatenate([column(odd, lane) for lane in lanes for odd in range(2)], axis=1)
        rows = jnp.dot(order, mixed, preferred_element_type=F32)
        a, b = rows[:, 512:640], rows[:, 640:768]
        last = (
            jnp.where(low, a, pltpu.roll(b, 64, 1)),
            jnp.where(low, pltpu.roll(a, 64, 1), b),
        )
        for h in range(2):
            fields.append(
                jnp.concatenate([rows[:, 256 * h : 256 * h + 256], last[h]], axis=1).astype(BF16)
            )
    return fields


def project_kernel(back_ref, leg_ref, state_ref, grav_ref, stab_ref, out_ref):
    g = [[grav_ref[a, b] for b in range(2)] for a in range(2)]
    s = [[stab_ref[a, b] for b in range(2)] for a in range(2)]
    gs = [[g[a][0] * s[0][b] + g[a][1] * s[1][b] for b in range(2)] for a in range(2)]
    first_pair = lax.axis_index("space") * LOCAL + pl.program_id(0) * GROUP
    fields = project_rows(back_ref)
    row8, _ = row_col(8, WIDTH)
    upper = row8 < 4
    _, col = row_col(1, WIDTH)
    for k in range(GROUP):
        pair = first_pair + k
        lhs = jnp.concatenate([rows[32 * k : 32 * k + 32] for rows in fields], axis=0)
        sums = lax.dot_general(
            lhs, leg_ref[k], (((1,), (1,)), ((), ())), preferred_element_type=F32
        )
        leading = col < NW - pair
        offset = jnp.where(leading, col, col - (NW - pair))
        parity = (1 - 2 * (offset & 1)).astype(F32)
        degree = jnp.where(leading, pair, NW - 1 - pair) + offset
        lam = WAVE_SCALE * (degree * (degree + 1)).astype(F32) / float(NW * NW)
        damp = 1.0 / (1.0 + DIFFUSION * lam * lam)
        coupling = DT * DT * lam
        diag = [1.0 + coupling * gs[a][a] for a in range(2)]
        cross = [coupling * gs[0][1], coupling * gs[1][0]]
        inverse = 1.0 / (diag[0] * diag[1] - cross[0] * cross[1])
        weight = [[DT * lam * g[a][b] for b in range(2)] for a in range(2)]
        left = jnp.broadcast_to(leading, (8, WIDTH))

        def moved(f):
            part = []
            for r in range(2):
                first = 32 * f + 16 * r
                part.append(sums[first : first + 8] + parity * sums[first + 8 : first + 16])
            near = jnp.where(upper, part[0], pltpu.roll(part[1], 4, 0))
            far = jnp.where(upper, pltpu.roll(part[0], 4, 0), part[1])
            old = jnp.concatenate([state_ref[0, 2 * f, k], state_ref[0, 2 * f + 1, k]], axis=0)
            return old + DT * jnp.where(left, near, far)

        def store(f, value):
            out_ref[2 * f, k] = value[0:4]
            out_ref[2 * f + 1, k] = value[4:8]

        for a in range(2):
            store(a, damp * moved(a))
        heat = [moved(4), moved(5)]
        right = [moved(2 + a) + (weight[a][0] * heat[0] + weight[a][1] * heat[1]) for a in range(2)]
        new = [
            (diag[1] * right[0] - cross[0] * right[1]) * inverse,
            (diag[0] * right[1] - cross[1] * right[0]) * inverse,
        ]
        for a in range(2):
            store(2 + a, damp * new[a])
            store(4 + a, damp * (heat[a] - DT * (s[a][0] * new[0] + s[a][1] * new[1])))


STATE = (2 * FIELDS, LOCAL, TRAJ, WIDTH)
LEG_BLOCK = pl.BlockSpec((GROUP, WIDTH, NHALF), lambda g: (g, 0, 0))
BAND_BLOCK = pl.BlockSpec((SPACE, 16, LANES), lambda g: (0, g, 0))


def to_bands(spectra, legendre, sin_lat, clones):
    tall, wide = zonal_tables()
    anywhere = pl.BlockSpec(memory_space=pl.ANY)
    vmem = pl.BlockSpec(memory_space=pltpu.VMEM)
    smem = pl.BlockSpec(memory_space=pltpu.SMEM)
    dma = pltpu.SemaphoreType.DMA
    pieces = (2, GROUPS, MEMBERS, MIX, WIDE // 2)
    band = (4 * PAIRS, LANES)
    return pl.pallas_call(
        main_kernel,
        in_specs=[smem, anywhere, anywhere, anywhere, anywhere, vmem],
        out_specs=[anywhere, anywhere],
        out_shape=[
            jax.ShapeDtypeStruct((SPACE, ROWS, LANES), BF16),
            jax.ShapeDtypeStruct(GROUPED, F32),
        ],
        scratch_shapes=[
            pltpu.VMEM((LOCAL, WIDTH, NHALF), BF16),
            pltpu.VMEM((4 * PAIRS, NLON), BF16),
            pltpu.VMEM((NLON, 4 * PAIRS), BF16),
            pltpu.VMEM(GROUPED, F32),
            pltpu.VMEM((2, GROUPS, TRAJ * MIX, WIDE), BF16),
            pltpu.VMEM((TRAJ * MIX, WIDE), F32),
            pltpu.VMEM(pieces, BF16),
            pltpu.VMEM(pieces, BF16),
            pltpu.VMEM(pieces, BF16),
            pltpu.VMEM((SPACE, ROWS, LANES), BF16),
            pltpu.VMEM(band, BF16),
            pltpu.VMEM(band, BF16),
            pltpu.VMEM(band, BF16),
            dma((GROUPS,)),
            dma((GROUPS,)),
            dma((2,)),
            dma,
            dma((2,)),
            dma((2, GROUPS, MEMBERS)),
            dma((2, GROUPS, MEMBERS)),
            dma((2, GROUPS, MEMBERS)),
            dma((2, GROUPS, MEMBERS)),
            dma((GROUPS, SPACE)),
            dma((GROUPS, SPACE)),
            dma((SPACE,)),
            dma((SPACE,)),
            dma((2, SPACE)),
            dma((2, SPACE)),
        ],
        compiler_params=pltpu.CompilerParams(
            vmem_limit_bytes=60 * 1024 * 1024, collective_id=0, has_side_effects=True
        ),
        name="bands",
    )(clones.T, spectra, legendre, jnp.asarray(tall), jnp.asarray(wide), sin_lat.reshape(1, NHALF))


def to_spectral(back, legendre, state, gravity, stability):
    smem = pl.BlockSpec(memory_space=pltpu.SMEM)
    return pl.pallas_call(
        project_kernel,
        grid=(GROUPS,),
        in_specs=[
            BAND_BLOCK,
            LEG_BLOCK,
            pl.BlockSpec((1,) + GROUPED[1:], lambda g: (g, 0, 0, 0, 0)),
            smem,
            smem,
        ],
        out_specs=pl.BlockSpec((2 * FIELDS, GROUP, TRAJ, WIDTH), lambda g: (0, g, 0, 0)),
        out_shape=jax.ShapeDtypeStruct(STATE, F32),
        compiler_params=pltpu.CompilerParams(vmem_limit_bytes=56 * 1024 * 1024),
        name="project",
    )(back, legendre, state, gravity, stability)


def shards(spectra, legendre, sin_lat, gravity, stability, clones):
    back, state = to_bands(spectra.transpose(1, 2, 0, 3), legendre, sin_lat, clones)
    return to_spectral(back, legendre, state, gravity, stability).transpose(2, 0, 1, 3)


def solution(mesh):
    placed = (P("member", None, "space", None), P("space", None, None), P(), P(), P(), P())
    return jax.shard_map(
        shards,
        mesh=mesh,
        in_specs=placed,
        out_specs=P("member", None, "space", None),
        check_vma=False,
    )
```

```python
import functools
import math

import jax
import jax.numpy as jnp
import numpy as np
from jax import lax
from jax.experimental import pallas as pl
from jax.experimental.pallas import tpu as pltpu
from jax.sharding import PartitionSpec as P

NW = 640
WIDTH = NW + 1
NLON = 1280
NLAT = 768
NHALF = 384
PAIRS = 320
TRAJ = 4
FIELDS = 6
LOCAL = 20
SPACE = 16
GROUP = 4
GROUPS = LOCAL // GROUP
FULL = 128 * FIELDS
LANES = FULL + 64 * FIELDS
PART = ((0, FULL), (FULL, LANES))
MEMBERS = 8
KILLED = 4
WIDE = 768
GROUPED = (GROUPS, 2 * FIELDS, GROUP, TRAJ, WIDTH)
MIX = 2 * FIELDS * GROUP
TILE = 16 * SPACE
EARLY = 2
MESH = pl.DeviceIdType.MESH
DT = 0.25
WAVE_SCALE = 16.0
DIFFUSION = 0.02
F32 = jnp.float32
BF16 = jnp.bfloat16


@functools.cache
def zonal_tables():
    pair = np.arange(PAIRS).reshape(SPACE, GROUPS, GROUP).transpose(1, 0, 2).reshape(-1)
    order = np.stack([pair, NW - 1 - pair], axis=1)
    phase = (order[:, :, None] * np.arange(NLON)) % NLON
    angle = phase * (2.0 * math.pi / NLON)
    table = np.stack([np.cos(angle), -np.sin(angle)], axis=2).reshape(4 * PAIRS, NLON)
    table = table.astype(jnp.bfloat16)
    return table, np.ascontiguousarray(table.T)


def row_col(rows, width):
    return (
        lax.broadcasted_iota(jnp.int32, (rows, width), 0),
        lax.broadcasted_iota(jnp.int32, (rows, width), 1),
    )


def sign_mask(pair):
    row, col = row_col(8, WIDTH)
    leading = (col < NW - pair).astype(jnp.int32)
    offset = jnp.where(leading == 1, col, col - (NW - pair))
    parity = (1 - 2 * (offset & 1)).astype(F32)
    sign = jnp.where(row >= 4, parity, 1.0)
    return jnp.where(((row >> 1) & 1) + leading == 1, sign, 0.0)


def swap4(value):
    return pltpu.roll(value, 4, 1)


def legendre_group(pair, now_ref, leg_ref, put):
    row8, _ = row_col(8, WIDTH)
    odd = (row8 & 1) == 1
    results = []
    for k in range(GROUP):
        mask = sign_mask(pair + k)
        pieces = []
        for t in range(TRAJ):
            for f in range(FIELDS):
                first = MIX * t + 2 * GROUP * f + k
                real, imag = (now_ref[row : row + 1, 0:WIDTH] for row in (first, first + GROUP))
                pieces.append(jnp.where(odd, imag, real) * mask)
        lhs = jnp.concatenate(pieces, axis=0).astype(BF16)
        dots = jnp.dot(lhs, leg_ref[k], preferred_element_type=F32)
        results.append(dots.reshape(TRAJ * FIELDS, 8, NHALF))
    upper = lax.broadcasted_iota(jnp.int32, (TRAJ * FIELDS, 8, NHALF), 1) < 4
    hemispheres = ([], [])
    for k in range(0, GROUP, 2):
        first, second = results[k], results[k + 1]
        hemispheres[0].append(jnp.where(upper, first, swap4(second)))
        hemispheres[1].append(jnp.where(upper, swap4(first), second))
    low = lax.broadcasted_iota(jnp.int32, (16, 128), 1) < 64
    for side in range(2):
        one, two = hemispheres[side]
        for t in range(TRAJ):
            for level in range(FIELDS // 2):
                tiles = []
                for f in (2 * level, 2 * level + 1):
                    tile = jnp.concatenate([one[t * FIELDS + f], two[t * FIELDS + f]], axis=0)
                    put(4 * t + 2 * side, 128 * f, tile[:, 0:128].astype(BF16))
                    put(4 * t + 2 * side + 1, 128 * f, tile[:, 128:256].astype(BF16))
                    tiles.append(tile[:, 256:384])
                a, b = tiles
                lane = FULL + 128 * level
                put(4 * t + 2 * side, lane, jnp.where(low, a, pltpu.roll(b, 64, 1)).astype(BF16))
                put(
                    4 * t + 2 * side + 1, lane, jnp.where(low, pltpu.roll(a, 64, 1), b).astype(BF16)
                )


def latitude_rows(sin_ref, place):
    low = lax.broadcasted_iota(jnp.int32, (1, 128), 1) < 64
    zero, one, two = (sin_ref[128 * i : 128 * i + 128].reshape(1, 128) for i in range(3))
    swapped = pltpu.roll(two, 64, 1)
    second = (place & 1) == 1
    sign = jnp.where((place & 3) >= 2, -1.0, 1.0).astype(F32)
    full = jnp.where(second, one, zero) * sign
    half = jnp.where(second, jnp.where(low, swapped, two), jnp.where(low, two, swapped)) * sign
    return full, half


def forcing_of(spin, spread, heat, heat_swapped, coriolis):
    spun = spin + coriolis
    return (
        -spun * spread,
        spun * spin - 0.5 * spread * spread,
        -(heat + 0.5 * (heat + heat_swapped)) * spread,
    )


def grid_forward(part, sines, f_ref, wide_ref, forcing_ref):
    start, stop = PART[part]
    tile = TILE

    def step(i, _):
        rows = pl.ds(pl.multiple_of(i * tile, tile), tile)
        sums = jnp.dot(wide_ref[rows, :], f_ref[:, start:stop], preferred_element_type=F32)
        sums = sums * (1.0 / NW)
        field = [sums[:, lane : lane + 128] for lane in range(0, stop - start, 128)]
        if part == 0:
            sets = [(field[a], field[2 + a], field[4 + a], field[5 - a]) for a in range(2)]
        else:
            sets = [(*field, pltpu.roll(field[2], 64, 1))]
        for a, fields in enumerate(sets):
            for g, made in enumerate(forcing_of(*fields, 2.0 * sines)):
                lane = start + 128 * (len(sets) * g + a)
                forcing_ref[rows, lane : lane + 128] = made.astype(BF16)
        return 0

    lax.fori_loop(0, NLON // tile, step, 0)


def grid_backward(part, sines, rows, forcing_ref, tall_ref, out_ref):
    start, stop = PART[part]
    weights = math.pi * jnp.sqrt(1.0 - sines * sines) / NLAT
    weights = jnp.concatenate([weights] * ((stop - start) // 128), axis=1)
    sums = jnp.dot(tall_ref[rows, :], forcing_ref[:, start:stop], preferred_element_type=F32)
    out_ref[rows, start:stop] = (sums * weights).astype(BF16)


def one_hot(condition):
    return jnp.where(condition, 1.0, 0.0).astype(BF16)


def square(rows):
    return row_col(rows, TRAJ * MIX)


def select_rows(clones_ref, member):
    row, col = square(MIX)
    parts = []
    for entry in range(KILLED):
        source = clones_ref[1, entry]
        wanted = jnp.where((source >> 2) == member, source & (TRAJ - 1), TRAJ)
        parts.append(one_hot((row == (col >> 2)) & ((col & 3) == wanted)))
    return jnp.concatenate(parts, axis=0)


def entry_of(clones_ref, number):
    found = KILLED
    for entry in range(KILLED):
        found = jnp.where(clones_ref[0, entry] == number, entry, found)
    return found


def entry_columns(col):
    return sum((col >= MIX * i).astype(jnp.int32) for i in range(1, KILLED))


def keep_and_put(clones_ref, member):
    row, col = square(MIX)
    entry = entry_columns(col)
    keep, put = [], []
    for t in range(TRAJ):
        found = entry_of(clones_ref, member * TRAJ + t)
        own = jnp.where(found == KILLED, t, TRAJ)
        keep.append(one_hot((row == (col >> 2)) & ((col & 3) == own)))
        put.append(one_hot((row == col - MIX * entry) & (entry == found)))
    return jnp.concatenate(keep, axis=0), jnp.concatenate(put, axis=0)


def by_trajectory(values, row):
    mixed = values[0]
    for t in range(1, TRAJ):
        mixed = jnp.where(row == t, values[t], mixed)
    return mixed


def place_rows(clones_ref, member):
    row, col = square(TRAJ * MIX)
    entry = entry_columns(col)
    found = [entry_of(clones_ref, member * TRAJ + t) for t in range(TRAJ)]
    return one_hot((entry == by_trajectory(found, row & 3)) & ((row >> 2) == col - MIX * entry))


def spread(axis, count, body):
    me = lax.axis_index(axis)

    def one(d, _):
        body(lax.rem(me + d, count))
        return 0

    lax.fori_loop(1, count, one, 0)


def main_kernel(
    clones_ref,
    x_any,
    leg_any,
    tall_any,
    wide_any,
    sin_ref,
    back_ref,
    state_ref,
    leg_ref,
    tall_ref,
    wide_ref,
    xg_ref,
    half_ref,
    now_ref,
    hand_ref,
    landed_ref,
    shared_ref,
    send_ref,
    fourier_ref,
    forcing_ref,
    give_ref,
    x_sem,
    leg_sem,
    table_sem,
    state_sem,
    own_sem,
    rs_send,
    rs_recv,
    ag_send,
    ag_recv,
    out_send,
    out_recv,
    back_send,
    back_recv,
):
    member = lax.axis_index("member")
    place = lax.axis_index("space")
    sines = latitude_rows(sin_ref, place)

    def x_copy(g):
        some = pl.ds(g * GROUP, GROUP)
        return pltpu.make_async_copy(x_any.at[:, some], xg_ref.at[g], x_sem.at[g])

    def leg_copy(g):
        some = pl.ds(g * GROUP, GROUP)
        return pltpu.make_async_copy(leg_any.at[some], leg_ref.at[some], leg_sem.at[g])

    for copy in (x_copy, leg_copy):
        for g in range(GROUPS):
            copy(g).start()
    wide_copy = pltpu.make_async_copy(wide_any, wide_ref, table_sem.at[0])
    tall_copy = pltpu.make_async_copy(tall_any, tall_ref, table_sem.at[1])
    wide_copy.start()
    tall_copy.start()

    barrier = pltpu.get_barrier_semaphore()
    spread(
        "space",
        SPACE,
        lambda peer: pl.semaphore_signal(
            barrier, inc=1, device_id={"space": peer}, device_id_type=MESH
        ),
    )
    spread(
        "member",
        MEMBERS,
        lambda peer: pl.semaphore_signal(
            barrier, inc=1, device_id={"member": peer}, device_id_type=MESH
        ),
    )

    def scatter(q, g, peer, source):
        return pltpu.make_async_remote_copy(
            src_ref=hand_ref.at[q, g, peer],
            dst_ref=landed_ref.at[q, g, source],
            send_sem=rs_send.at[q, g, peer],
            recv_sem=rs_recv.at[q, g, source],
            device_id={"member": peer},
            device_id_type=MESH,
        )

    def gather(q, g, peer, source):
        return pltpu.make_async_remote_copy(
            src_ref=shared_ref.at[q, g, source],
            dst_ref=shared_ref.at[q, g, source],
            send_sem=ag_send.at[q, g, peer],
            recv_sem=ag_recv.at[q, g, source],
            device_id={"member": peer},
            device_id_type=MESH,
        )

    def regroup(g):
        rows = jnp.concatenate(
            [xg_ref[g, c, p] for c in range(2 * FIELDS) for p in range(GROUP)], axis=0
        )
        _, lane = row_col(TRAJ * MIX, 128)
        value = jnp.concatenate(
            [rows[:, 0:NW], jnp.where(lane < 1, rows[:, NW:WIDTH], 0.0)], axis=1
        )
        high = value.astype(BF16)
        half_ref[0, g] = high
        half_ref[1, g] = (value - high.astype(F32)).astype(BF16)

    selection = select_rows(clones_ref, member)

    def offer(q, g):
        value = jnp.dot(selection, half_ref[q, g], preferred_element_type=F32).astype(BF16)
        for entry in range(KILLED):
            rows = slice(MIX * entry, MIX * entry + MIX)
            hand_ref[q, g, 2 * entry] = value[rows, 0 : WIDE // 2]
            hand_ref[q, g, 2 * entry + 1] = value[rows, WIDE // 2 : WIDE]
        spread("member", MEMBERS, lambda peer: scatter(q, g, peer, member).start())

    def settle(q, g):
        spread("member", MEMBERS, lambda peer: scatter(q, g, peer, peer).wait_recv())

        def add(d, total):
            return total + landed_ref[q, g, lax.rem(member + d, MEMBERS)].astype(F32)

        total = lax.fori_loop(1, MEMBERS, add, hand_ref[q, g, member].astype(F32))
        shared_ref[q, g, member] = total.astype(BF16)
        spread("member", MEMBERS, lambda peer: gather(q, g, peer, member).start())

    def arrived(q, g):
        spread("member", MEMBERS, lambda peer: gather(q, g, peer, peer).wait_recv())

    def received(q, g):
        return jnp.concatenate(
            [
                jnp.concatenate([shared_ref[q, g, 2 * e], shared_ref[q, g, 2 * e + 1]], axis=1)
                for e in range(KILLED)
            ],
            axis=0,
        )

    def outward(part, g, peer, source):
        start, stop = PART[part]
        lanes = pl.ds(start, stop - start)
        return pltpu.make_async_remote_copy(
            src_ref=send_ref.at[g, peer, :, lanes],
            dst_ref=fourier_ref.at[pl.ds(g * TILE + source * 16, 16), lanes],
            send_sem=out_send.at[part, g, peer],
            recv_sem=out_recv.at[part, g, source],
            device_id={"space": peer},
            device_id_type=MESH,
        )

    def homeward(part, g, peer, source):
        start, stop = PART[part]
        lanes = pl.ds(start, stop - start)
        return pltpu.make_async_remote_copy(
            src_ref=give_ref.at[pl.ds(g * TILE + peer * 16, 16), lanes],
            dst_ref=back_ref.at[g, source, :, lanes],
            send_sem=back_send.at[part, g, peer],
            recv_sem=back_recv.at[part, g, source],
            device_id={"space": peer},
            device_id_type=MESH,
        )

    def own_out(g):
        rows = pl.ds(g * TILE + place * 16, 16)
        return pltpu.make_async_copy(send_ref.at[g, place], fourier_ref.at[rows], own_sem.at[0, g])

    def own_back(g):
        rows = pl.ds(g * TILE + place * 16, 16)
        return pltpu.make_async_copy(give_ref.at[rows], back_ref.at[g, place], own_sem.at[1, g])

    def each_group(body):
        def one(g, _):
            body(g)
            return 0

        lax.fori_loop(0, GROUPS, one, 0)

    def send_out(part, g):
        spread("space", SPACE, lambda peer: outward(part, g, peer, place).start())

    x_copy(0).wait()
    regroup(0)
    pl.semaphore_wait(barrier, SPACE + MEMBERS - 2)
    offer(0, 0)

    x_copy(1).wait()
    regroup(1)
    settle(0, 0)
    offer(0, 1)
    keep, put_rows = keep_and_put(clones_ref, member)

    def legendre_step(g, _):
        @pl.when(g + 2 < GROUPS)
        def _():
            x_copy(g + 2).wait()
            regroup(g + 2)

        arrived(0, g)

        @pl.when((g > 0) & (g + 1 < GROUPS))
        def _():
            settle(0, g + 1)

        @pl.when((g > 0) & (g + 2 < GROUPS))
        def _():
            offer(0, g + 2)

        now = jnp.dot(keep, half_ref[0, g], preferred_element_type=F32)
        now_ref[...] = now + jnp.dot(put_rows, received(0, g), preferred_element_type=F32)
        leg_copy(g).wait()

        def put(block, lane, value):
            send_ref[g, block, :, lane : lane + 128] = value

        legendre_group(
            place * LOCAL + g * GROUP, now_ref, leg_ref.at[pl.ds(g * GROUP, GROUP)], put
        )
        send_out(0, g)
        own_out(g).start()

        @pl.when(g < EARLY)
        def _():
            send_out(1, g)

        @pl.when(g == 0)
        def _():
            settle(0, 1)
            offer(0, 2)

        return 0

    lax.fori_loop(0, GROUPS, legendre_step, 0)

    def send_late(g, _):
        send_out(1, g)
        return 0

    lax.fori_loop(EARLY, GROUPS, send_late, 0)
    each_group(lambda g: offer(1, g))
    wide_copy.wait()
    tall_copy.wait()
    each_group(lambda g: own_out(g).wait())

    for part in range(2):
        each_group(
            lambda g: spread(
                "space", SPACE, lambda peer: outward(part, g, peer, peer).wait_recv()
            )
        )
        grid_forward(part, sines[part], fourier_ref, wide_ref, forcing_ref)

        def backward(g):
            rows = pl.ds(pl.multiple_of(g * TILE, TILE), TILE)
            grid_backward(part, sines[part], rows, forcing_ref, tall_ref, give_ref)
            spread("space", SPACE, lambda peer: homeward(part, g, peer, place).start())

        each_group(backward)
        if part == 0:
            each_group(lambda g: settle(1, g))
    each_group(lambda g: own_back(g).start())

    placing = place_rows(clones_ref, member)
    row, _ = row_col(TRAJ, WIDTH)
    killed = by_trajectory(
        [entry_of(clones_ref, member * TRAJ + t) for t in range(TRAJ)], row
    )

    def complete(g):
        arrived(1, g)
        value = sum(
            jnp.dot(placing, received(q, g), preferred_element_type=F32) for q in range(2)
        )
        for c in range(2 * FIELDS):
            for p in range(GROUP):
                first = (c * GROUP + p) * TRAJ
                new = value[first : first + TRAJ, 0:WIDTH]
                xg_ref[g, c, p] = jnp.where(killed < KILLED, new, xg_ref[g, c, p])

    each_group(complete)
    state_copy = pltpu.make_async_copy(xg_ref, state_ref, state_sem)
    state_copy.start()
    for q in range(2):
        each_group(
            lambda g: spread("member", MEMBERS, lambda peer: scatter(q, g, peer, peer).wait_send())
        )
        each_group(
            lambda g: spread("member", MEMBERS, lambda peer: gather(q, g, peer, member).wait_send())
        )
    for part in range(2):
        each_group(
            lambda g: spread(
                "space", SPACE, lambda peer: outward(part, g, peer, place).wait_send()
            )
        )
        each_group(
            lambda g: spread(
                "space", SPACE, lambda peer: homeward(part, g, peer, place).wait_send()
            )
        )
        each_group(
            lambda g: spread(
                "space", SPACE, lambda peer: homeward(part, g, peer, peer).wait_recv()
            )
        )
    each_group(lambda g: own_back(g).wait())
    state_copy.wait()


def unmix():
    row, col = row_col(128, 128)
    t, half, side, part, pair = row & 3, (row >> 2) & 1, (row >> 3) & 1, (row >> 4) & 1, row >> 5
    return one_hot(col == 32 * t + 16 * side + 4 * pair + 2 * half + part)


def project_rows(back_ref):
    low = lax.broadcasted_iota(jnp.int32, (128, 128), 1) < 64
    order = unmix()

    def column(odd, lane):
        return jnp.concatenate(
            [
                back_ref[0, 4 * t + 2 * side + odd, :, lane : lane + 128]
                for t in range(TRAJ)
                for side in range(2)
            ],
            axis=0,
        )

    fields = []
    for level in range(FIELDS // 2):
        lanes = [256 * level, 256 * level + 128, FULL + 128 * level]
        mixed = jnp.concatenate([column(odd, lane) for lane in lanes for odd in range(2)], axis=1)
        rows = jnp.dot(order, mixed, preferred_element_type=F32)
        a, b = rows[:, 512:640], rows[:, 640:768]
        last = (
            jnp.where(low, a, pltpu.roll(b, 64, 1)),
            jnp.where(low, pltpu.roll(a, 64, 1), b),
        )
        for h in range(2):
            fields.append(
                jnp.concatenate([rows[:, 256 * h : 256 * h + 256], last[h]], axis=1).astype(BF16)
            )
    return fields


def project_kernel(back_ref, leg_ref, state_ref, grav_ref, stab_ref, out_ref):
    g = [[grav_ref[a, b] for b in range(2)] for a in range(2)]
    s = [[stab_ref[a, b] for b in range(2)] for a in range(2)]
    gs = [[g[a][0] * s[0][b] + g[a][1] * s[1][b] for b in range(2)] for a in range(2)]
    first_pair = lax.axis_index("space") * LOCAL + pl.program_id(0) * GROUP
    fields = project_rows(back_ref)
    row8, _ = row_col(8, WIDTH)
    upper = row8 < 4
    _, col = row_col(1, WIDTH)
    for k in range(GROUP):
        pair = first_pair + k
        lhs = jnp.concatenate([rows[32 * k : 32 * k + 32] for rows in fields], axis=0)
        sums = lax.dot_general(
            lhs, leg_ref[k], (((1,), (1,)), ((), ())), preferred_element_type=F32
        )
        leading = col < NW - pair
        offset = jnp.where(leading, col, col - (NW - pair))
        parity = (1 - 2 * (offset & 1)).astype(F32)
        degree = jnp.where(leading, pair, NW - 1 - pair) + offset
        lam = WAVE_SCALE * (degree * (degree + 1)).astype(F32) / float(NW * NW)
        damp = 1.0 / (1.0 + DIFFUSION * lam * lam)
        coupling = DT * DT * lam
        diag = [1.0 + coupling * gs[a][a] for a in range(2)]
        cross = [coupling * gs[0][1], coupling * gs[1][0]]
        inverse = 1.0 / (diag[0] * diag[1] - cross[0] * cross[1])
        weight = [[DT * lam * g[a][b] for b in range(2)] for a in range(2)]
        left = jnp.broadcast_to(leading, (8, WIDTH))

        def moved(f):
            part = []
            for r in range(2):
                first = 32 * f + 16 * r
                part.append(sums[first : first + 8] + parity * sums[first + 8 : first + 16])
            near = jnp.where(upper, part[0], pltpu.roll(part[1], 4, 0))
            far = jnp.where(upper, pltpu.roll(part[0], 4, 0), part[1])
            old = jnp.concatenate([state_ref[0, 2 * f, k], state_ref[0, 2 * f + 1, k]], axis=0)
            return old + DT * jnp.where(left, near, far)

        def store(f, value):
            out_ref[2 * f, k] = value[0:4]
            out_ref[2 * f + 1, k] = value[4:8]

        for a in range(2):
            store(a, damp * moved(a))
        heat = [moved(4), moved(5)]
        right = [moved(2 + a) + (weight[a][0] * heat[0] + weight[a][1] * heat[1]) for a in range(2)]
        new = [
            (diag[1] * right[0] - cross[0] * right[1]) * inverse,
            (diag[0] * right[1] - cross[1] * right[0]) * inverse,
        ]
        for a in range(2):
            store(2 + a, damp * new[a])
            store(4 + a, damp * (heat[a] - DT * (s[a][0] * new[0] + s[a][1] * new[1])))


STATE = (2 * FIELDS, LOCAL, TRAJ, WIDTH)
LEG_BLOCK = pl.BlockSpec((GROUP, WIDTH, NHALF), lambda g: (g, 0, 0))
BAND_BLOCK = pl.BlockSpec((1, SPACE, 16, LANES), lambda g: (g, 0, 0, 0))


def to_bands(spectra, legendre, sin_lat, clones):
    tall, wide = zonal_tables()
    anywhere = pl.BlockSpec(memory_space=pl.ANY)
    vmem = pl.BlockSpec(memory_space=pltpu.VMEM)
    smem = pl.BlockSpec(memory_space=pltpu.SMEM)
    dma = pltpu.SemaphoreType.DMA
    pieces = (2, GROUPS, MEMBERS, MIX, WIDE // 2)
    band = (4 * PAIRS, LANES)
    return pl.pallas_call(
        main_kernel,
        in_specs=[smem, anywhere, anywhere, anywhere, anywhere, vmem],
        out_specs=[anywhere, anywhere],
        out_shape=[
            jax.ShapeDtypeStruct((GROUPS, SPACE, 16, LANES), BF16),
            jax.ShapeDtypeStruct(GROUPED, F32),
        ],
        scratch_shapes=[
            pltpu.VMEM((LOCAL, WIDTH, NHALF), BF16),
            pltpu.VMEM((4 * PAIRS, NLON), BF16),
            pltpu.VMEM((NLON, 4 * PAIRS), BF16),
            pltpu.VMEM(GROUPED, F32),
            pltpu.VMEM((2, GROUPS, TRAJ * MIX, WIDE), BF16),
            pltpu.VMEM((TRAJ * MIX, WIDE), F32),
            pltpu.VMEM(pieces, BF16),
            pltpu.VMEM(pieces, BF16),
            pltpu.VMEM(pieces, BF16),
            pltpu.VMEM((GROUPS, SPACE, 16, LANES), BF16),
            pltpu.VMEM(band, BF16),
            pltpu.VMEM(band, BF16),
            pltpu.VMEM(band, BF16),
            dma((GROUPS,)),
            dma((GROUPS,)),
            dma((2,)),
            dma,
            dma((2, GROUPS)),
            dma((2, GROUPS, MEMBERS)),
            dma((2, GROUPS, MEMBERS)),
            dma((2, GROUPS, MEMBERS)),
            dma((2, GROUPS, MEMBERS)),
            dma((2, GROUPS, SPACE)),
            dma((2, GROUPS, SPACE)),
            dma((2, GROUPS, SPACE)),
            dma((2, GROUPS, SPACE)),
        ],
        compiler_params=pltpu.CompilerParams(
            vmem_limit_bytes=60 * 1024 * 1024, collective_id=0, has_side_effects=True
        ),
        name="bands",
    )(clones.T, spectra, legendre, jnp.asarray(tall), jnp.asarray(wide), sin_lat)


def to_spectral(back, legendre, state, gravity, stability):
    smem = pl.BlockSpec(memory_space=pltpu.SMEM)
    return pl.pallas_call(
        project_kernel,
        grid=(GROUPS,),
        in_specs=[
            BAND_BLOCK,
            LEG_BLOCK,
            pl.BlockSpec((1,) + GROUPED[1:], lambda g: (g, 0, 0, 0, 0)),
            smem,
            smem,
        ],
        out_specs=pl.BlockSpec((2 * FIELDS, GROUP, TRAJ, WIDTH), lambda g: (0, g, 0, 0)),
        out_shape=jax.ShapeDtypeStruct(STATE, F32),
        compiler_params=pltpu.CompilerParams(vmem_limit_bytes=56 * 1024 * 1024),
        name="project",
    )(back, legendre, state, gravity, stability)


def shards(spectra, legendre, sin_lat, gravity, stability, clones):
    back, state = to_bands(spectra.transpose(1, 2, 0, 3), legendre, sin_lat, clones)
    return to_spectral(back, legendre, state, gravity, stability).transpose(2, 0, 1, 3)


def solution(mesh):
    placed = (P("member", None, "space", None), P("space", None, None), P(), P(), P(), P())
    return jax.shard_map(
        shards,
        mesh=mesh,
        in_specs=placed,
        out_specs=P("member", None, "space", None),
        check_vma=False,
    )
```

```python
import functools
import math

import jax
import jax.numpy as jnp
import numpy as np
from jax import lax
from jax.experimental import pallas as pl
from jax.experimental.pallas import tpu as pltpu
from jax.sharding import PartitionSpec as P

NW = 640
WIDTH = NW + 1
NLON = 1280
NLAT = 768
NHALF = 384
PAIRS = 320
TRAJ = 4
FIELDS = 6
LOCAL = 20
SPACE = 16
GROUP = 4
GROUPS = LOCAL // GROUP
FULL = 128 * FIELDS
LANES = FULL + 64 * FIELDS
PART = ((0, FULL), (FULL, LANES))
MEMBERS = 8
CHIPS = 4
KILLED = 4
WIDE = 768
GROUPED = (GROUPS, 2 * FIELDS, GROUP, TRAJ, WIDTH)
MIX = 2 * FIELDS * GROUP
TILE = 16 * SPACE
EARLY = 2
MESH = pl.DeviceIdType.MESH
DT = 0.25
WAVE_SCALE = 16.0
DIFFUSION = 0.02
F32 = jnp.float32
BF16 = jnp.bfloat16


@functools.cache
def zonal_tables():
    pair = np.arange(PAIRS).reshape(SPACE, GROUPS, GROUP).transpose(1, 0, 2).reshape(-1)
    order = np.stack([pair, NW - 1 - pair], axis=1)
    phase = (order[:, :, None] * np.arange(NLON)) % NLON
    angle = phase * (2.0 * math.pi / NLON)
    table = np.stack([np.cos(angle), -np.sin(angle)], axis=2).reshape(4 * PAIRS, NLON)
    table = table.astype(jnp.bfloat16)
    return table, np.ascontiguousarray(table.T)


def row_col(rows, width):
    return (
        lax.broadcasted_iota(jnp.int32, (rows, width), 0),
        lax.broadcasted_iota(jnp.int32, (rows, width), 1),
    )


def sign_mask(pair):
    row, col = row_col(8, WIDTH)
    leading = (col < NW - pair).astype(jnp.int32)
    offset = jnp.where(leading == 1, col, col - (NW - pair))
    parity = (1 - 2 * (offset & 1)).astype(F32)
    sign = jnp.where(row >= 4, parity, 1.0)
    return jnp.where(((row >> 1) & 1) + leading == 1, sign, 0.0)


def swap4(value):
    return pltpu.roll(value, 4, 1)


def legendre_group(pair, now_ref, leg_ref, put):
    row8, _ = row_col(8, WIDTH)
    odd = (row8 & 1) == 1
    results = []
    for k in range(GROUP):
        mask = sign_mask(pair + k)
        pieces = []
        for t in range(TRAJ):
            for f in range(FIELDS):
                first = MIX * t + 2 * GROUP * f + k
                real, imag = (now_ref[row : row + 1, 0:WIDTH] for row in (first, first + GROUP))
                pieces.append(jnp.where(odd, imag, real) * mask)
        lhs = jnp.concatenate(pieces, axis=0).astype(BF16)
        dots = jnp.dot(lhs, leg_ref[k], preferred_element_type=F32)
        results.append(dots.reshape(TRAJ * FIELDS, 8, NHALF))
    upper = lax.broadcasted_iota(jnp.int32, (TRAJ * FIELDS, 8, NHALF), 1) < 4
    hemispheres = ([], [])
    for k in range(0, GROUP, 2):
        first, second = results[k], results[k + 1]
        hemispheres[0].append(jnp.where(upper, first, swap4(second)))
        hemispheres[1].append(jnp.where(upper, swap4(first), second))
    low = lax.broadcasted_iota(jnp.int32, (16, 128), 1) < 64
    for side in range(2):
        one, two = hemispheres[side]
        for t in range(TRAJ):
            for level in range(FIELDS // 2):
                tiles = []
                for f in (2 * level, 2 * level + 1):
                    tile = jnp.concatenate([one[t * FIELDS + f], two[t * FIELDS + f]], axis=0)
                    put(4 * t + 2 * side, 128 * f, tile[:, 0:128].astype(BF16))
                    put(4 * t + 2 * side + 1, 128 * f, tile[:, 128:256].astype(BF16))
                    tiles.append(tile[:, 256:384])
                a, b = tiles
                lane = FULL + 128 * level
                put(4 * t + 2 * side, lane, jnp.where(low, a, pltpu.roll(b, 64, 1)).astype(BF16))
                put(
                    4 * t + 2 * side + 1, lane, jnp.where(low, pltpu.roll(a, 64, 1), b).astype(BF16)
                )


def latitude_rows(sin_ref, place):
    low = lax.broadcasted_iota(jnp.int32, (1, 128), 1) < 64
    zero, one, two = (sin_ref[128 * i : 128 * i + 128].reshape(1, 128) for i in range(3))
    swapped = pltpu.roll(two, 64, 1)
    second = (place & 1) == 1
    sign = jnp.where((place & 3) >= 2, -1.0, 1.0).astype(F32)
    full = jnp.where(second, one, zero) * sign
    half = jnp.where(second, jnp.where(low, swapped, two), jnp.where(low, two, swapped)) * sign
    return full, half


def forcing_of(spin, spread, heat, heat_swapped, coriolis):
    spun = spin + coriolis
    return (
        -spun * spread,
        spun * spin - 0.5 * spread * spread,
        -(heat + 0.5 * (heat + heat_swapped)) * spread,
    )


def grid_forward(part, sines, f_ref, wide_ref, forcing_ref):
    start, stop = PART[part]
    tile = TILE

    def step(i, _):
        rows = pl.ds(pl.multiple_of(i * tile, tile), tile)
        sums = jnp.dot(wide_ref[rows, :], f_ref[:, start:stop], preferred_element_type=F32)
        sums = sums * (1.0 / NW)
        field = [sums[:, lane : lane + 128] for lane in range(0, stop - start, 128)]
        if part == 0:
            sets = [(field[a], field[2 + a], field[4 + a], field[5 - a]) for a in range(2)]
        else:
            sets = [(*field, pltpu.roll(field[2], 64, 1))]
        for a, fields in enumerate(sets):
            for g, made in enumerate(forcing_of(*fields, 2.0 * sines)):
                lane = start + 128 * (len(sets) * g + a)
                forcing_ref[rows, lane : lane + 128] = made.astype(BF16)
        return 0

    lax.fori_loop(0, NLON // tile, step, 0)


def grid_backward(part, sines, rows, forcing_ref, tall_ref, out_ref):
    start, stop = PART[part]
    weights = math.pi * jnp.sqrt(1.0 - sines * sines) / NLAT
    weights = jnp.concatenate([weights] * ((stop - start) // 128), axis=1)
    sums = jnp.dot(tall_ref[rows, :], forcing_ref[:, start:stop], preferred_element_type=F32)
    out_ref[rows, start:stop] = (sums * weights).astype(BF16)


def one_hot(condition):
    return jnp.where(condition, 1.0, 0.0).astype(BF16)


def square(rows):
    return row_col(rows, TRAJ * MIX)


def select_rows(clones_ref, member):
    row, col = square(MIX)
    parts = []
    for entry in range(KILLED):
        source = clones_ref[1, entry]
        wanted = jnp.where((source >> 2) == member, source & (TRAJ - 1), TRAJ)
        parts.append(one_hot((row == (col >> 2)) & ((col & 3) == wanted)))
    return jnp.concatenate(parts, axis=0)


def entry_of(clones_ref, number):
    found = KILLED
    for entry in range(KILLED):
        found = jnp.where(clones_ref[0, entry] == number, entry, found)
    return found


def entry_columns(col):
    return sum((col >= MIX * i).astype(jnp.int32) for i in range(1, KILLED))


def keep_and_put(clones_ref, member):
    row, col = square(MIX)
    entry = entry_columns(col)
    keep, put = [], []
    for t in range(TRAJ):
        found = entry_of(clones_ref, member * TRAJ + t)
        own = jnp.where(found == KILLED, t, TRAJ)
        keep.append(one_hot((row == (col >> 2)) & ((col & 3) == own)))
        put.append(one_hot((row == col - MIX * entry) & (entry == found)))
    return jnp.concatenate(keep, axis=0), jnp.concatenate(put, axis=0)


def by_trajectory(values, row):
    mixed = values[0]
    for t in range(1, TRAJ):
        mixed = jnp.where(row == t, values[t], mixed)
    return mixed


def place_rows(clones_ref, member):
    row, col = square(TRAJ * MIX)
    entry = entry_columns(col)
    found = [entry_of(clones_ref, member * TRAJ + t) for t in range(TRAJ)]
    return one_hot((entry == by_trajectory(found, row & 3)) & ((row >> 2) == col - MIX * entry))


def spread(axis, count, body):
    me = lax.axis_index(axis)

    def one(d, _):
        body(lax.rem(me + d, count))
        return 0

    lax.fori_loop(1, count, one, 0)


def main_kernel(
    clones_ref,
    x_any,
    leg_any,
    tall_any,
    wide_any,
    sin_ref,
    back_ref,
    state_ref,
    leg_ref,
    tall_ref,
    wide_ref,
    xg_ref,
    half_ref,
    now_ref,
    hand_ref,
    core_ref,
    pair_ref,
    landed_ref,
    shared_ref,
    send_ref,
    fourier_ref,
    forcing_ref,
    give_ref,
    x_sem,
    leg_sem,
    table_sem,
    state_sem,
    own_sem,
    core_send,
    core_recv,
    rs_send,
    rs_recv,
    ag_send,
    ag_recv,
    out_send,
    out_recv,
    back_send,
    back_recv,
):
    member = lax.axis_index("member")
    place = lax.axis_index("space")
    core = member & 1
    chip = member >> 1
    partner = member + 1 - 2 * core
    sines = latitude_rows(sin_ref, place)

    def x_copy(g):
        some = pl.ds(g * GROUP, GROUP)
        return pltpu.make_async_copy(x_any.at[:, some], xg_ref.at[g], x_sem.at[g])

    def leg_copy(g):
        some = pl.ds(g * GROUP, GROUP)
        return pltpu.make_async_copy(leg_any.at[some], leg_ref.at[some], leg_sem.at[g])

    for copy in (x_copy, leg_copy):
        for g in range(GROUPS):
            copy(g).start()
    wide_copy = pltpu.make_async_copy(wide_any, wide_ref, table_sem.at[0])
    tall_copy = pltpu.make_async_copy(tall_any, tall_ref, table_sem.at[1])
    wide_copy.start()
    tall_copy.start()

    barrier = pltpu.get_barrier_semaphore()
    spread(
        "space",
        SPACE,
        lambda peer: pl.semaphore_signal(
            barrier, inc=1, device_id={"space": peer}, device_id_type=MESH
        ),
    )
    spread(
        "member",
        MEMBERS,
        lambda peer: pl.semaphore_signal(
            barrier, inc=1, device_id={"member": peer}, device_id_type=MESH
        ),
    )

    def across(q, g):
        return pltpu.make_async_remote_copy(
            src_ref=hand_ref.at[q, g, 1 - core],
            dst_ref=core_ref.at[q, g],
            send_sem=core_send.at[q, g],
            recv_sem=core_recv.at[q, g],
            device_id={"member": partner},
            device_id_type=MESH,
        )

    def scatter(q, g, peer, source):
        return pltpu.make_async_remote_copy(
            src_ref=pair_ref.at[q, g, peer],
            dst_ref=landed_ref.at[q, g, source],
            send_sem=rs_send.at[q, g, peer],
            recv_sem=rs_recv.at[q, g, source],
            device_id={"member": 2 * peer + core},
            device_id_type=MESH,
        )

    def gather(q, g, peer, source):
        return pltpu.make_async_remote_copy(
            src_ref=shared_ref.at[q, g, source & 1, source >> 1],
            dst_ref=shared_ref.at[q, g, source & 1, source >> 1],
            send_sem=ag_send.at[q, g, peer],
            recv_sem=ag_recv.at[q, g, source],
            device_id={"member": peer},
            device_id_type=MESH,
        )

    def other_chips(body):
        def one(d, _):
            body(lax.rem(chip + d, CHIPS))
            return 0

        lax.fori_loop(1, CHIPS, one, 0)

    def regroup(g):
        rows = jnp.concatenate(
            [xg_ref[g, c, p] for c in range(2 * FIELDS) for p in range(GROUP)], axis=0
        )
        _, lane = row_col(TRAJ * MIX, 128)
        value = jnp.concatenate(
            [rows[:, 0:NW], jnp.where(lane < 1, rows[:, NW:WIDTH], 0.0)], axis=1
        )
        high = value.astype(BF16)
        half_ref[0, g] = high
        half_ref[1, g] = (value - high.astype(F32)).astype(BF16)

    selection = select_rows(clones_ref, member)

    def offer(q, g):
        value = jnp.dot(selection, half_ref[q, g], preferred_element_type=F32).astype(BF16)
        for entry in range(KILLED):
            rows = slice(MIX * entry, MIX * entry + MIX)
            hand_ref[q, g, 0, entry] = value[rows, 0 : WIDE // 2]
            hand_ref[q, g, 1, entry] = value[rows, WIDE // 2 : WIDE]
        across(q, g).start()

    def combine(q, g):
        across(q, g).wait_recv()
        total = hand_ref[q, g, core].astype(F32) + core_ref[q, g].astype(F32)
        pair_ref[q, g] = total.astype(BF16)
        other_chips(lambda peer: scatter(q, g, peer, chip).start())

    def settle(q, g):
        other_chips(lambda peer: scatter(q, g, peer, peer).wait_recv())
        total = pair_ref[q, g, chip].astype(F32)
        for d in range(1, CHIPS):
            total = total + landed_ref[q, g, lax.rem(chip + d, CHIPS)].astype(F32)
        shared_ref[q, g, core, chip] = total.astype(BF16)
        spread("member", MEMBERS, lambda peer: gather(q, g, peer, member).start())

    def arrived(q, g):
        spread("member", MEMBERS, lambda peer: gather(q, g, peer, peer).wait_recv())

    def received(q, g):
        return jnp.concatenate(
            [
                jnp.concatenate([shared_ref[q, g, 0, e], shared_ref[q, g, 1, e]], axis=1)
                for e in range(KILLED)
            ],
            axis=0,
        )

    def outward(part, g, peer, source):
        start, stop = PART[part]
        lanes = pl.ds(start, stop - start)
        return pltpu.make_async_remote_copy(
            src_ref=send_ref.at[g, peer, :, lanes],
            dst_ref=fourier_ref.at[pl.ds(g * TILE + source * 16, 16), lanes],
            send_sem=out_send.at[part, g, peer],
            recv_sem=out_recv.at[part, g, source],
            device_id={"space": peer},
            device_id_type=MESH,
        )

    def homeward(part, g, peer, source):
        start, stop = PART[part]
        lanes = pl.ds(start, stop - start)
        return pltpu.make_async_remote_copy(
            src_ref=give_ref.at[pl.ds(g * TILE + peer * 16, 16), lanes],
            dst_ref=back_ref.at[g, source, :, lanes],
            send_sem=back_send.at[part, g, peer],
            recv_sem=back_recv.at[part, g, source],
            device_id={"space": peer},
            device_id_type=MESH,
        )

    def own_out(g):
        rows = pl.ds(g * TILE + place * 16, 16)
        return pltpu.make_async_copy(send_ref.at[g, place], fourier_ref.at[rows], own_sem.at[0, g])

    def own_back(g):
        rows = pl.ds(g * TILE + place * 16, 16)
        return pltpu.make_async_copy(give_ref.at[rows], back_ref.at[g, place], own_sem.at[1, g])

    def each_group(body):
        def one(g, _):
            body(g)
            return 0

        lax.fori_loop(0, GROUPS, one, 0)

    def send_out(part, g):
        spread("space", SPACE, lambda peer: outward(part, g, peer, place).start())

    x_copy(0).wait()
    regroup(0)
    pl.semaphore_wait(barrier, SPACE + MEMBERS - 2)
    offer(0, 0)

    x_copy(1).wait()
    regroup(1)
    offer(0, 1)
    combine(0, 0)
    x_copy(2).wait()
    regroup(2)
    offer(0, 2)
    combine(0, 1)
    keep, put_rows = keep_and_put(clones_ref, member)
    settle(0, 0)

    def legendre_step(g, _):
        @pl.when(g + 3 < GROUPS)
        def _():
            x_copy(g + 3).wait()
            regroup(g + 3)
            offer(0, g + 3)

        @pl.when(g + 2 < GROUPS)
        def _():
            combine(0, g + 2)

        @pl.when(g + 1 < GROUPS)
        def _():
            settle(0, g + 1)

        arrived(0, g)
        now = jnp.dot(keep, half_ref[0, g], preferred_element_type=F32)
        now_ref[...] = now + jnp.dot(put_rows, received(0, g), preferred_element_type=F32)
        leg_copy(g).wait()

        def put(block, lane, value):
            send_ref[g, block, :, lane : lane + 128] = value

        legendre_group(
            place * LOCAL + g * GROUP, now_ref, leg_ref.at[pl.ds(g * GROUP, GROUP)], put
        )
        send_out(0, g)
        own_out(g).start()

        @pl.when(g < EARLY)
        def _():
            send_out(1, g)

        return 0

    lax.fori_loop(0, GROUPS, legendre_step, 0)

    def send_late(g, _):
        send_out(1, g)
        return 0

    lax.fori_loop(EARLY, GROUPS, send_late, 0)
    each_group(lambda g: offer(1, g))
    each_group(lambda g: combine(1, g))
    wide_copy.wait()
    tall_copy.wait()
    each_group(lambda g: own_out(g).wait())

    for part in range(2):
        each_group(
            lambda g: spread(
                "space", SPACE, lambda peer: outward(part, g, peer, peer).wait_recv()
            )
        )
        grid_forward(part, sines[part], fourier_ref, wide_ref, forcing_ref)

        def backward(g):
            rows = pl.ds(pl.multiple_of(g * TILE, TILE), TILE)
            grid_backward(part, sines[part], rows, forcing_ref, tall_ref, give_ref)
            spread("space", SPACE, lambda peer: homeward(part, g, peer, place).start())

        each_group(backward)
        if part == 0:
            each_group(lambda g: settle(1, g))
    each_group(lambda g: own_back(g).start())

    placing = place_rows(clones_ref, member)
    row, _ = row_col(TRAJ, WIDTH)
    killed = by_trajectory(
        [entry_of(clones_ref, member * TRAJ + t) for t in range(TRAJ)], row
    )

    def complete(g):
        arrived(1, g)
        value = sum(
            jnp.dot(placing, received(q, g), preferred_element_type=F32) for q in range(2)
        )
        for c in range(2 * FIELDS):
            for p in range(GROUP):
                first = (c * GROUP + p) * TRAJ
                new = value[first : first + TRAJ, 0:WIDTH]
                xg_ref[g, c, p] = jnp.where(killed < KILLED, new, xg_ref[g, c, p])

    each_group(complete)
    state_copy = pltpu.make_async_copy(xg_ref, state_ref, state_sem)
    state_copy.start()
    for q in range(2):
        each_group(lambda g: across(q, g).wait_send())
        each_group(lambda g: other_chips(lambda peer: scatter(q, g, peer, chip).wait_send()))
        each_group(
            lambda g: spread("member", MEMBERS, lambda peer: gather(q, g, peer, member).wait_send())
        )
    for part in range(2):
        each_group(
            lambda g: spread(
                "space", SPACE, lambda peer: outward(part, g, peer, place).wait_send()
            )
        )
        each_group(
            lambda g: spread(
                "space", SPACE, lambda peer: homeward(part, g, peer, place).wait_send()
            )
        )
        each_group(
            lambda g: spread(
                "space", SPACE, lambda peer: homeward(part, g, peer, peer).wait_recv()
            )
        )
    each_group(lambda g: own_back(g).wait())
    state_copy.wait()


def unmix():
    row, col = row_col(128, 128)
    t, half, side, part, pair = row & 3, (row >> 2) & 1, (row >> 3) & 1, (row >> 4) & 1, row >> 5
    return one_hot(col == 32 * t + 16 * side + 4 * pair + 2 * half + part)


def project_rows(back_ref):
    low = lax.broadcasted_iota(jnp.int32, (128, 128), 1) < 64
    order = unmix()

    def column(odd, lane):
        return jnp.concatenate(
            [
                back_ref[0, 4 * t + 2 * side + odd, :, lane : lane + 128]
                for t in range(TRAJ)
                for side in range(2)
            ],
            axis=0,
        )

    fields = []
    for level in range(FIELDS // 2):
        lanes = [256 * level, 256 * level + 128, FULL + 128 * level]
        mixed = jnp.concatenate([column(odd, lane) for lane in lanes for odd in range(2)], axis=1)
        rows = jnp.dot(order, mixed, preferred_element_type=F32)
        a, b = rows[:, 512:640], rows[:, 640:768]
        last = (
            jnp.where(low, a, pltpu.roll(b, 64, 1)),
            jnp.where(low, pltpu.roll(a, 64, 1), b),
        )
        for h in range(2):
            fields.append(
                jnp.concatenate([rows[:, 256 * h : 256 * h + 256], last[h]], axis=1).astype(BF16)
            )
    return fields


def project_kernel(back_ref, leg_ref, state_ref, grav_ref, stab_ref, out_ref):
    g = [[grav_ref[a, b] for b in range(2)] for a in range(2)]
    s = [[stab_ref[a, b] for b in range(2)] for a in range(2)]
    gs = [[g[a][0] * s[0][b] + g[a][1] * s[1][b] for b in range(2)] for a in range(2)]
    first_pair = lax.axis_index("space") * LOCAL + pl.program_id(0) * GROUP
    fields = project_rows(back_ref)
    row8, _ = row_col(8, WIDTH)
    upper = row8 < 4
    _, col = row_col(1, WIDTH)
    for k in range(GROUP):
        pair = first_pair + k
        lhs = jnp.concatenate([rows[32 * k : 32 * k + 32] for rows in fields], axis=0)
        sums = lax.dot_general(
            lhs, leg_ref[k], (((1,), (1,)), ((), ())), preferred_element_type=F32
        )
        leading = col < NW - pair
        offset = jnp.where(leading, col, col - (NW - pair))
        parity = (1 - 2 * (offset & 1)).astype(F32)
        degree = jnp.where(leading, pair, NW - 1 - pair) + offset
        lam = WAVE_SCALE * (degree * (degree + 1)).astype(F32) / float(NW * NW)
        damp = 1.0 / (1.0 + DIFFUSION * lam * lam)
        coupling = DT * DT * lam
        diag = [1.0 + coupling * gs[a][a] for a in range(2)]
        cross = [coupling * gs[0][1], coupling * gs[1][0]]
        inverse = 1.0 / (diag[0] * diag[1] - cross[0] * cross[1])
        weight = [[DT * lam * g[a][b] for b in range(2)] for a in range(2)]
        left = jnp.broadcast_to(leading, (8, WIDTH))

        def moved(f):
            part = []
            for r in range(2):
                first = 32 * f + 16 * r
                part.append(sums[first : first + 8] + parity * sums[first + 8 : first + 16])
            near = jnp.where(upper, part[0], pltpu.roll(part[1], 4, 0))
            far = jnp.where(upper, pltpu.roll(part[0], 4, 0), part[1])
            old = jnp.concatenate([state_ref[0, 2 * f, k], state_ref[0, 2 * f + 1, k]], axis=0)
            return old + DT * jnp.where(left, near, far)

        def store(f, value):
            out_ref[2 * f, k] = value[0:4]
            out_ref[2 * f + 1, k] = value[4:8]

        for a in range(2):
            store(a, damp * moved(a))
        heat = [moved(4), moved(5)]
        right = [moved(2 + a) + (weight[a][0] * heat[0] + weight[a][1] * heat[1]) for a in range(2)]
        new = [
            (diag[1] * right[0] - cross[0] * right[1]) * inverse,
            (diag[0] * right[1] - cross[1] * right[0]) * inverse,
        ]
        for a in range(2):
            store(2 + a, damp * new[a])
            store(4 + a, damp * (heat[a] - DT * (s[a][0] * new[0] + s[a][1] * new[1])))


STATE = (2 * FIELDS, LOCAL, TRAJ, WIDTH)
LEG_BLOCK = pl.BlockSpec((GROUP, WIDTH, NHALF), lambda g: (g, 0, 0))
BAND_BLOCK = pl.BlockSpec((1, SPACE, 16, LANES), lambda g: (g, 0, 0, 0))


def to_bands(spectra, legendre, sin_lat, clones):
    tall, wide = zonal_tables()
    anywhere = pl.BlockSpec(memory_space=pl.ANY)
    vmem = pl.BlockSpec(memory_space=pltpu.VMEM)
    smem = pl.BlockSpec(memory_space=pltpu.SMEM)
    dma = pltpu.SemaphoreType.DMA
    pieces = (KILLED, MIX, WIDE // 2)
    band = (4 * PAIRS, LANES)
    return pl.pallas_call(
        main_kernel,
        in_specs=[smem, anywhere, anywhere, anywhere, anywhere, vmem],
        out_specs=[anywhere, anywhere],
        out_shape=[
            jax.ShapeDtypeStruct((GROUPS, SPACE, 16, LANES), BF16),
            jax.ShapeDtypeStruct(GROUPED, F32),
        ],
        scratch_shapes=[
            pltpu.VMEM((LOCAL, WIDTH, NHALF), BF16),
            pltpu.VMEM((4 * PAIRS, NLON), BF16),
            pltpu.VMEM((NLON, 4 * PAIRS), BF16),
            pltpu.VMEM(GROUPED, F32),
            pltpu.VMEM((2, GROUPS, TRAJ * MIX, WIDE), BF16),
            pltpu.VMEM((TRAJ * MIX, WIDE), F32),
            pltpu.VMEM((2, GROUPS, 2) + pieces, BF16),
            pltpu.VMEM((2, GROUPS) + pieces, BF16),
            pltpu.VMEM((2, GROUPS) + pieces, BF16),
            pltpu.VMEM((2, GROUPS) + pieces, BF16),
            pltpu.VMEM((2, GROUPS, 2) + pieces, BF16),
            pltpu.VMEM((GROUPS, SPACE, 16, LANES), BF16),
            pltpu.VMEM(band, BF16),
            pltpu.VMEM(band, BF16),
            pltpu.VMEM(band, BF16),
            dma((GROUPS,)),
            dma((GROUPS,)),
            dma((2,)),
            dma,
            dma((2, GROUPS)),
            dma((2, GROUPS)),
            dma((2, GROUPS)),
            dma((2, GROUPS, CHIPS)),
            dma((2, GROUPS, CHIPS)),
            dma((2, GROUPS, MEMBERS)),
            dma((2, GROUPS, MEMBERS)),
            dma((2, GROUPS, SPACE)),
            dma((2, GROUPS, SPACE)),
            dma((2, GROUPS, SPACE)),
            dma((2, GROUPS, SPACE)),
        ],
        compiler_params=pltpu.CompilerParams(
            vmem_limit_bytes=60 * 1024 * 1024, collective_id=0, has_side_effects=True
        ),
        name="bands",
    )(clones.T, spectra, legendre, jnp.asarray(tall), jnp.asarray(wide), sin_lat)


def to_spectral(back, legendre, state, gravity, stability):
    smem = pl.BlockSpec(memory_space=pltpu.SMEM)
    return pl.pallas_call(
        project_kernel,
        grid=(GROUPS,),
        in_specs=[
            BAND_BLOCK,
            LEG_BLOCK,
            pl.BlockSpec((1,) + GROUPED[1:], lambda g: (g, 0, 0, 0, 0)),
            smem,
            smem,
        ],
        out_specs=pl.BlockSpec((2 * FIELDS, GROUP, TRAJ, WIDTH), lambda g: (0, g, 0, 0)),
        out_shape=jax.ShapeDtypeStruct(STATE, F32),
        compiler_params=pltpu.CompilerParams(vmem_limit_bytes=56 * 1024 * 1024),
        name="project",
    )(back, legendre, state, gravity, stability)


def shards(spectra, legendre, sin_lat, gravity, stability, clones):
    back, state = to_bands(spectra.transpose(1, 2, 0, 3), legendre, sin_lat, clones)
    return to_spectral(back, legendre, state, gravity, stability).transpose(2, 0, 1, 3)


def solution(mesh):
    placed = (P("member", None, "space", None), P("space", None, None), P(), P(), P(), P())
    return jax.shard_map(
        shards,
        mesh=mesh,
        in_specs=placed,
        out_specs=P("member", None, "space", None),
        check_vma=False,
    )
```

```python
import functools
import math

import jax
import jax.numpy as jnp
import numpy as np
from jax import lax
from jax.experimental import pallas as pl
from jax.experimental.pallas import tpu as pltpu
from jax.sharding import PartitionSpec as P

NW = 640
WIDTH = NW + 1
NLON = 1280
NLAT = 768
NHALF = 384
PAIRS = 320
TRAJ = 4
FIELDS = 6
LOCAL = 20
SPACE = 16
GROUP = 4
GROUPS = LOCAL // GROUP
FULL = 128 * FIELDS
LANES = FULL + 64 * FIELDS
PART = ((0, FULL), (FULL, LANES))
MEMBERS = 8
CHIPS = 4
KILLED = 4
WIDE = 768
GROUPED = (GROUPS, 2 * FIELDS, GROUP, TRAJ, WIDTH)
MIX = 2 * FIELDS * GROUP
TILE = 16 * SPACE
EARLY = 2
MESH = pl.DeviceIdType.MESH
DT = 0.25
WAVE_SCALE = 16.0
DIFFUSION = 0.02
F32 = jnp.float32
BF16 = jnp.bfloat16


@functools.cache
def zonal_tables():
    pair = np.arange(PAIRS).reshape(SPACE, GROUPS, GROUP).transpose(1, 0, 2).reshape(-1)
    order = np.stack([pair, NW - 1 - pair], axis=1)
    phase = (order[:, :, None] * np.arange(NLON)) % NLON
    angle = phase * (2.0 * math.pi / NLON)
    table = np.stack([np.cos(angle), -np.sin(angle)], axis=2).reshape(4 * PAIRS, NLON)
    table = table.astype(jnp.bfloat16)
    return table, np.ascontiguousarray(table.T)


def row_col(rows, width):
    return (
        lax.broadcasted_iota(jnp.int32, (rows, width), 0),
        lax.broadcasted_iota(jnp.int32, (rows, width), 1),
    )


def sign_mask(pair):
    row, col = row_col(8, WIDTH)
    leading = (col < NW - pair).astype(jnp.int32)
    offset = jnp.where(leading == 1, col, col - (NW - pair))
    parity = (1 - 2 * (offset & 1)).astype(F32)
    sign = jnp.where(row >= 4, parity, 1.0)
    return jnp.where(((row >> 1) & 1) + leading == 1, sign, 0.0)


def swap4(value):
    return pltpu.roll(value, 4, 1)


def legendre_group(pair, now_ref, leg_ref, put):
    row8, _ = row_col(8, WIDTH)
    odd = (row8 & 1) == 1
    results = []
    for k in range(GROUP):
        mask = sign_mask(pair + k)
        pieces = []
        for t in range(TRAJ):
            for f in range(FIELDS):
                first = MIX * t + 2 * GROUP * f + k
                real, imag = (now_ref[row : row + 1, 0:WIDTH] for row in (first, first + GROUP))
                pieces.append(jnp.where(odd, imag, real) * mask)
        lhs = jnp.concatenate(pieces, axis=0).astype(BF16)
        dots = jnp.dot(lhs, leg_ref[k], preferred_element_type=F32)
        results.append(dots.reshape(TRAJ * FIELDS, 8, NHALF))
    upper = lax.broadcasted_iota(jnp.int32, (TRAJ * FIELDS, 8, NHALF), 1) < 4
    hemispheres = ([], [])
    for k in range(0, GROUP, 2):
        first, second = results[k], results[k + 1]
        hemispheres[0].append(jnp.where(upper, first, swap4(second)))
        hemispheres[1].append(jnp.where(upper, swap4(first), second))
    low = lax.broadcasted_iota(jnp.int32, (16, 128), 1) < 64
    for side in range(2):
        one, two = hemispheres[side]
        for t in range(TRAJ):
            for level in range(FIELDS // 2):
                tiles = []
                for f in (2 * level, 2 * level + 1):
                    tile = jnp.concatenate([one[t * FIELDS + f], two[t * FIELDS + f]], axis=0)
                    put(4 * t + 2 * side, 128 * f, tile[:, 0:128].astype(BF16))
                    put(4 * t + 2 * side + 1, 128 * f, tile[:, 128:256].astype(BF16))
                    tiles.append(tile[:, 256:384])
                a, b = tiles
                lane = FULL + 128 * level
                put(4 * t + 2 * side, lane, jnp.where(low, a, pltpu.roll(b, 64, 1)).astype(BF16))
                put(
                    4 * t + 2 * side + 1, lane, jnp.where(low, pltpu.roll(a, 64, 1), b).astype(BF16)
                )


def latitude_rows(sin_ref, place):
    low = lax.broadcasted_iota(jnp.int32, (1, 128), 1) < 64
    zero, one, two = (sin_ref[128 * i : 128 * i + 128].reshape(1, 128) for i in range(3))
    swapped = pltpu.roll(two, 64, 1)
    second = (place & 1) == 1
    sign = jnp.where((place & 3) >= 2, -1.0, 1.0).astype(F32)
    full = jnp.where(second, one, zero) * sign
    half = jnp.where(second, jnp.where(low, swapped, two), jnp.where(low, two, swapped)) * sign
    return full, half


def forcing_of(spin, spread, heat, heat_swapped, coriolis):
    spun = spin + coriolis
    return (
        -spun * spread,
        spun * spin - 0.5 * spread * spread,
        -(heat + 0.5 * (heat + heat_swapped)) * spread,
    )


def grid_forward(part, sines, f_ref, wide_ref, forcing_ref):
    start, stop = PART[part]
    tile = TILE

    def step(i, _):
        rows = pl.ds(pl.multiple_of(i * tile, tile), tile)
        sums = jnp.dot(wide_ref[rows, :], f_ref[:, start:stop], preferred_element_type=F32)
        sums = sums * (1.0 / NW)
        field = [sums[:, lane : lane + 128] for lane in range(0, stop - start, 128)]
        if part == 0:
            sets = [(field[a], field[2 + a], field[4 + a], field[5 - a]) for a in range(2)]
        else:
            sets = [(*field, pltpu.roll(field[2], 64, 1))]
        for a, fields in enumerate(sets):
            for g, made in enumerate(forcing_of(*fields, 2.0 * sines)):
                lane = start + 128 * (len(sets) * g + a)
                forcing_ref[rows, lane : lane + 128] = made.astype(BF16)
        return 0

    lax.fori_loop(0, NLON // tile, step, 0)


def grid_backward(part, sines, rows, forcing_ref, tall_ref, out_ref):
    start, stop = PART[part]
    weights = math.pi * jnp.sqrt(1.0 - sines * sines) / NLAT
    weights = jnp.concatenate([weights] * ((stop - start) // 128), axis=1)
    sums = jnp.dot(tall_ref[rows, :], forcing_ref[:, start:stop], preferred_element_type=F32)
    out_ref[rows, start:stop] = (sums * weights).astype(BF16)


def one_hot(condition):
    return jnp.where(condition, 1.0, 0.0).astype(BF16)


def square(rows):
    return row_col(rows, TRAJ * MIX)


def select_rows(clones_ref, member):
    row, col = square(MIX)
    parts = []
    for entry in range(KILLED):
        source = clones_ref[1, entry]
        wanted = jnp.where((source >> 2) == member, source & (TRAJ - 1), TRAJ)
        parts.append(one_hot((row == (col >> 2)) & ((col & 3) == wanted)))
    return jnp.concatenate(parts, axis=0)


def entry_of(clones_ref, number):
    found = KILLED
    for entry in range(KILLED):
        found = jnp.where(clones_ref[0, entry] == number, entry, found)
    return found


def entry_columns(col):
    return sum((col >= MIX * i).astype(jnp.int32) for i in range(1, KILLED))


def keep_and_put(clones_ref, member):
    row, col = square(MIX)
    entry = entry_columns(col)
    keep, put = [], []
    for t in range(TRAJ):
        found = entry_of(clones_ref, member * TRAJ + t)
        own = jnp.where(found == KILLED, t, TRAJ)
        keep.append(one_hot((row == (col >> 2)) & ((col & 3) == own)))
        put.append(one_hot((row == col - MIX * entry) & (entry == found)))
    return jnp.concatenate(keep, axis=0), jnp.concatenate(put, axis=0)


def by_trajectory(values, row):
    mixed = values[0]
    for t in range(1, TRAJ):
        mixed = jnp.where(row == t, values[t], mixed)
    return mixed


def place_rows(clones_ref, member):
    row, col = square(TRAJ * MIX)
    entry = entry_columns(col)
    found = [entry_of(clones_ref, member * TRAJ + t) for t in range(TRAJ)]
    return one_hot((entry == by_trajectory(found, row & 3)) & ((row >> 2) == col - MIX * entry))


def unmix():
    row, col = row_col(128, 128)
    t, half, side, part, pair = row & 3, (row >> 2) & 1, (row >> 3) & 1, (row >> 4) & 1, row >> 5
    return one_hot(col == 32 * t + 16 * side + 4 * pair + 2 * half + part)


def project_rows(back_ref):
    low = lax.broadcasted_iota(jnp.int32, (128, 128), 1) < 64
    order = unmix()

    def column(odd, lane):
        return jnp.concatenate(
            [
                back_ref[4 * t + 2 * side + odd, :, lane : lane + 128]
                for t in range(TRAJ)
                for side in range(2)
            ],
            axis=0,
        )

    fields = []
    for level in range(FIELDS // 2):
        lanes = [256 * level, 256 * level + 128, FULL + 128 * level]
        mixed = jnp.concatenate([column(odd, lane) for lane in lanes for odd in range(2)], axis=1)
        rows = jnp.dot(order, mixed, preferred_element_type=F32)
        a, b = rows[:, 512:640], rows[:, 640:768]
        last = (
            jnp.where(low, a, pltpu.roll(b, 64, 1)),
            jnp.where(low, pltpu.roll(a, 64, 1), b),
        )
        for h in range(2):
            fields.append(
                jnp.concatenate([rows[:, 256 * h : 256 * h + 256], last[h]], axis=1).astype(BF16)
            )
    return fields


def project_group(first_pair, back_ref, leg_ref, state_ref, grav_ref, stab_ref):
    g = [[grav_ref[a, b] for b in range(2)] for a in range(2)]
    s = [[stab_ref[a, b] for b in range(2)] for a in range(2)]
    gs = [[g[a][0] * s[0][b] + g[a][1] * s[1][b] for b in range(2)] for a in range(2)]
    fields = project_rows(back_ref)
    row8, _ = row_col(8, WIDTH)
    upper = row8 < 4
    _, col = row_col(1, WIDTH)
    for k in range(GROUP):
        pair = first_pair + k
        lhs = jnp.concatenate([rows[32 * k : 32 * k + 32] for rows in fields], axis=0)
        sums = lax.dot_general(
            lhs, leg_ref[k], (((1,), (1,)), ((), ())), preferred_element_type=F32
        )
        leading = col < NW - pair
        offset = jnp.where(leading, col, col - (NW - pair))
        parity = (1 - 2 * (offset & 1)).astype(F32)
        degree = jnp.where(leading, pair, NW - 1 - pair) + offset
        lam = WAVE_SCALE * (degree * (degree + 1)).astype(F32) / float(NW * NW)
        damp = 1.0 / (1.0 + DIFFUSION * lam * lam)
        coupling = DT * DT * lam
        diag = [1.0 + coupling * gs[a][a] for a in range(2)]
        cross = [coupling * gs[0][1], coupling * gs[1][0]]
        inverse = 1.0 / (diag[0] * diag[1] - cross[0] * cross[1])
        weight = [[DT * lam * g[a][b] for b in range(2)] for a in range(2)]
        left = jnp.broadcast_to(leading, (8, WIDTH))

        def moved(f):
            part = []
            for r in range(2):
                first = 32 * f + 16 * r
                part.append(sums[first : first + 8] + parity * sums[first + 8 : first + 16])
            near = jnp.where(upper, part[0], pltpu.roll(part[1], 4, 0))
            far = jnp.where(upper, pltpu.roll(part[0], 4, 0), part[1])
            old = jnp.concatenate([state_ref[2 * f, k], state_ref[2 * f + 1, k]], axis=0)
            return old + DT * jnp.where(left, near, far)

        def store(f, value):
            state_ref[2 * f, k] = value[0:4]
            state_ref[2 * f + 1, k] = value[4:8]

        for a in range(2):
            store(a, damp * moved(a))
        heat = [moved(4), moved(5)]
        right = [moved(2 + a) + (weight[a][0] * heat[0] + weight[a][1] * heat[1]) for a in range(2)]
        new = [
            (diag[1] * right[0] - cross[0] * right[1]) * inverse,
            (diag[0] * right[1] - cross[1] * right[0]) * inverse,
        ]
        for a in range(2):
            store(2 + a, damp * new[a])
            store(4 + a, damp * (heat[a] - DT * (s[a][0] * new[0] + s[a][1] * new[1])))


def spread(axis, count, body):
    me = lax.axis_index(axis)

    def one(d, _):
        body(lax.rem(me + d, count))
        return 0

    lax.fori_loop(1, count, one, 0)


def main_kernel(
    clones_ref,
    x_any,
    leg_any,
    tall_any,
    wide_any,
    sin_ref,
    grav_ref,
    stab_ref,
    new_any,
    leg_ref,
    tall_ref,
    wide_ref,
    xg_ref,
    half_ref,
    now_ref,
    hand_ref,
    core_ref,
    pair_ref,
    landed_ref,
    shared_ref,
    send_ref,
    fourier_ref,
    forcing_ref,
    give_ref,
    back_ref,
    x_sem,
    leg_sem,
    table_sem,
    state_sem,
    own_sem,
    core_send,
    core_recv,
    rs_send,
    rs_recv,
    ag_send,
    ag_recv,
    out_send,
    out_recv,
    back_send,
    back_recv,
):
    member = lax.axis_index("member")
    place = lax.axis_index("space")
    core = member & 1
    chip = member >> 1
    partner = member + 1 - 2 * core
    sines = latitude_rows(sin_ref, place)

    def x_copy(g):
        some = pl.ds(g * GROUP, GROUP)
        return pltpu.make_async_copy(x_any.at[:, some], xg_ref.at[g], x_sem.at[g])

    def leg_copy(g):
        some = pl.ds(g * GROUP, GROUP)
        return pltpu.make_async_copy(leg_any.at[some], leg_ref.at[some], leg_sem.at[g])

    for copy in (x_copy, leg_copy):
        for g in range(GROUPS):
            copy(g).start()
    wide_copy = pltpu.make_async_copy(wide_any, wide_ref, table_sem.at[0])
    tall_copy = pltpu.make_async_copy(tall_any, tall_ref, table_sem.at[1])
    wide_copy.start()
    tall_copy.start()

    barrier = pltpu.get_barrier_semaphore()
    spread(
        "space",
        SPACE,
        lambda peer: pl.semaphore_signal(
            barrier, inc=1, device_id={"space": peer}, device_id_type=MESH
        ),
    )
    spread(
        "member",
        MEMBERS,
        lambda peer: pl.semaphore_signal(
            barrier, inc=1, device_id={"member": peer}, device_id_type=MESH
        ),
    )

    def across(q, g):
        return pltpu.make_async_remote_copy(
            src_ref=hand_ref.at[q, g, 1 - core],
            dst_ref=core_ref.at[q, g],
            send_sem=core_send.at[q, g],
            recv_sem=core_recv.at[q, g],
            device_id={"member": partner},
            device_id_type=MESH,
        )

    def scatter(q, g, peer, source):
        return pltpu.make_async_remote_copy(
            src_ref=pair_ref.at[q, g, peer],
            dst_ref=landed_ref.at[q, g, source],
            send_sem=rs_send.at[q, g, peer],
            recv_sem=rs_recv.at[q, g, source],
            device_id={"member": 2 * peer + core},
            device_id_type=MESH,
        )

    def gather(q, g, peer, source):
        return pltpu.make_async_remote_copy(
            src_ref=shared_ref.at[q, g, source & 1, source >> 1],
            dst_ref=shared_ref.at[q, g, source & 1, source >> 1],
            send_sem=ag_send.at[q, g, peer],
            recv_sem=ag_recv.at[q, g, source],
            device_id={"member": peer},
            device_id_type=MESH,
        )

    def other_chips(body):
        def one(d, _):
            body(lax.rem(chip + d, CHIPS))
            return 0

        lax.fori_loop(1, CHIPS, one, 0)

    def regroup(g):
        rows = jnp.concatenate(
            [xg_ref[g, c, p] for c in range(2 * FIELDS) for p in range(GROUP)], axis=0
        )
        _, lane = row_col(TRAJ * MIX, 128)
        value = jnp.concatenate(
            [rows[:, 0:NW], jnp.where(lane < 1, rows[:, NW:WIDTH], 0.0)], axis=1
        )
        high = value.astype(BF16)
        half_ref[0, g] = high
        half_ref[1, g] = (value - high.astype(F32)).astype(BF16)

    selection = select_rows(clones_ref, member)

    def offer(q, g):
        value = jnp.dot(selection, half_ref[q, g], preferred_element_type=F32).astype(BF16)
        for entry in range(KILLED):
            rows = slice(MIX * entry, MIX * entry + MIX)
            hand_ref[q, g, 0, entry] = value[rows, 0 : WIDE // 2]
            hand_ref[q, g, 1, entry] = value[rows, WIDE // 2 : WIDE]
        across(q, g).start()

    def combine(q, g):
        across(q, g).wait_recv()
        total = hand_ref[q, g, core].astype(F32) + core_ref[q, g].astype(F32)
        pair_ref[q, g] = total.astype(BF16)
        other_chips(lambda peer: scatter(q, g, peer, chip).start())

    def settle(q, g):
        other_chips(lambda peer: scatter(q, g, peer, peer).wait_recv())
        total = pair_ref[q, g, chip].astype(F32)
        for d in range(1, CHIPS):
            total = total + landed_ref[q, g, lax.rem(chip + d, CHIPS)].astype(F32)
        shared_ref[q, g, core, chip] = total.astype(BF16)
        spread("member", MEMBERS, lambda peer: gather(q, g, peer, member).start())

    def arrived(q, g):
        spread("member", MEMBERS, lambda peer: gather(q, g, peer, peer).wait_recv())

    def received(q, g):
        return jnp.concatenate(
            [
                jnp.concatenate([shared_ref[q, g, 0, e], shared_ref[q, g, 1, e]], axis=1)
                for e in range(KILLED)
            ],
            axis=0,
        )

    def outward(part, g, peer, source):
        start, stop = PART[part]
        lanes = pl.ds(start, stop - start)
        return pltpu.make_async_remote_copy(
            src_ref=send_ref.at[g, peer, :, lanes],
            dst_ref=fourier_ref.at[pl.ds(g * TILE + source * 16, 16), lanes],
            send_sem=out_send.at[part, g, peer],
            recv_sem=out_recv.at[part, g, source],
            device_id={"space": peer},
            device_id_type=MESH,
        )

    def homeward(part, g, peer, source):
        start, stop = PART[part]
        lanes = pl.ds(start, stop - start)
        return pltpu.make_async_remote_copy(
            src_ref=give_ref.at[pl.ds(g * TILE + peer * 16, 16), lanes],
            dst_ref=back_ref.at[g, source, :, lanes],
            send_sem=back_send.at[part, g, peer],
            recv_sem=back_recv.at[part, g, source],
            device_id={"space": peer},
            device_id_type=MESH,
        )

    def own_out(g):
        rows = pl.ds(g * TILE + place * 16, 16)
        return pltpu.make_async_copy(send_ref.at[g, place], fourier_ref.at[rows], own_sem.at[0, g])

    def own_back(g):
        rows = pl.ds(g * TILE + place * 16, 16)
        return pltpu.make_async_copy(give_ref.at[rows], back_ref.at[g, place], own_sem.at[1, g])

    def each_group(body):
        def one(g, _):
            body(g)
            return 0

        lax.fori_loop(0, GROUPS, one, 0)

    def send_out(part, g):
        spread("space", SPACE, lambda peer: outward(part, g, peer, place).start())

    x_copy(0).wait()
    regroup(0)
    pl.semaphore_wait(barrier, SPACE + MEMBERS - 2)
    offer(0, 0)

    x_copy(1).wait()
    regroup(1)
    offer(0, 1)
    combine(0, 0)
    x_copy(2).wait()
    regroup(2)
    offer(0, 2)
    combine(0, 1)
    keep, put_rows = keep_and_put(clones_ref, member)
    settle(0, 0)

    def legendre_step(g, _):
        @pl.when(g + 3 < GROUPS)
        def _():
            x_copy(g + 3).wait()
            regroup(g + 3)
            offer(0, g + 3)

        @pl.when(g + 2 < GROUPS)
        def _():
            combine(0, g + 2)

        @pl.when(g + 1 < GROUPS)
        def _():
            settle(0, g + 1)

        arrived(0, g)
        now = jnp.dot(keep, half_ref[0, g], preferred_element_type=F32)
        now_ref[...] = now + jnp.dot(put_rows, received(0, g), preferred_element_type=F32)
        leg_copy(g).wait()

        def put(block, lane, value):
            send_ref[g, block, :, lane : lane + 128] = value

        legendre_group(
            place * LOCAL + g * GROUP, now_ref, leg_ref.at[pl.ds(g * GROUP, GROUP)], put
        )
        send_out(0, g)
        own_out(g).start()

        @pl.when(g < EARLY)
        def _():
            send_out(1, g)

        return 0

    lax.fori_loop(0, GROUPS, legendre_step, 0)

    def send_late(g, _):
        send_out(1, g)
        return 0

    lax.fori_loop(EARLY, GROUPS, send_late, 0)
    each_group(lambda g: offer(1, g))
    each_group(lambda g: combine(1, g))
    wide_copy.wait()
    tall_copy.wait()
    each_group(lambda g: own_out(g).wait())

    for part in range(2):
        each_group(
            lambda g: spread(
                "space", SPACE, lambda peer: outward(part, g, peer, peer).wait_recv()
            )
        )
        grid_forward(part, sines[part], fourier_ref, wide_ref, forcing_ref)

        def backward(g):
            rows = pl.ds(pl.multiple_of(g * TILE, TILE), TILE)
            grid_backward(part, sines[part], rows, forcing_ref, tall_ref, give_ref)
            spread("space", SPACE, lambda peer: homeward(part, g, peer, place).start())

        each_group(backward)
        if part == 0:
            each_group(lambda g: settle(1, g))
    each_group(lambda g: own_back(g).start())

    placing = place_rows(clones_ref, member)
    row, _ = row_col(TRAJ, WIDTH)
    killed = by_trajectory(
        [entry_of(clones_ref, member * TRAJ + t) for t in range(TRAJ)], row
    )

    def complete(g):
        arrived(1, g)
        value = sum(
            jnp.dot(placing, received(q, g), preferred_element_type=F32) for q in range(2)
        )
        for c in range(2 * FIELDS):
            for p in range(GROUP):
                first = (c * GROUP + p) * TRAJ
                new = value[first : first + TRAJ, 0:WIDTH]
                xg_ref[g, c, p] = jnp.where(killed < KILLED, new, xg_ref[g, c, p])

    def new_copy(g):
        some = pl.ds(g * GROUP, GROUP)
        return pltpu.make_async_copy(xg_ref.at[g], new_any.at[:, some], state_sem.at[g])

    def project(g):
        complete(g)
        own_back(g).wait()
        for part in range(2):
            spread(
                "space", SPACE, lambda peer: homeward(part, g, peer, peer).wait_recv()
            )
        project_group(
            place * LOCAL + g * GROUP,
            back_ref.at[g],
            leg_ref.at[pl.ds(g * GROUP, GROUP)],
            xg_ref.at[g],
            grav_ref,
            stab_ref,
        )
        new_copy(g).start()

    each_group(project)
    for q in range(2):
        each_group(lambda g: across(q, g).wait_send())
        each_group(lambda g: other_chips(lambda peer: scatter(q, g, peer, chip).wait_send()))
        each_group(
            lambda g: spread("member", MEMBERS, lambda peer: gather(q, g, peer, member).wait_send())
        )
    for part in range(2):
        each_group(
            lambda g: spread(
                "space", SPACE, lambda peer: outward(part, g, peer, place).wait_send()
            )
        )
        each_group(
            lambda g: spread(
                "space", SPACE, lambda peer: homeward(part, g, peer, place).wait_send()
            )
        )
    each_group(lambda g: new_copy(g).wait())


STATE = (2 * FIELDS, LOCAL, TRAJ, WIDTH)


def step(state, legendre, sin_lat, gravity, stability, clones):
    tall, wide = zonal_tables()
    anywhere = pl.BlockSpec(memory_space=pl.ANY)
    vmem = pl.BlockSpec(memory_space=pltpu.VMEM)
    smem = pl.BlockSpec(memory_space=pltpu.SMEM)
    dma = pltpu.SemaphoreType.DMA
    pieces = (KILLED, MIX, WIDE // 2)
    band = (4 * PAIRS, LANES)
    return pl.pallas_call(
        main_kernel,
        in_specs=[smem, anywhere, anywhere, anywhere, anywhere, vmem, smem, smem],
        out_specs=anywhere,
        out_shape=jax.ShapeDtypeStruct(STATE, F32),
        scratch_shapes=[
            pltpu.VMEM((LOCAL, WIDTH, NHALF), BF16),
            pltpu.VMEM((4 * PAIRS, NLON), BF16),
            pltpu.VMEM((NLON, 4 * PAIRS), BF16),
            pltpu.VMEM(GROUPED, F32),
            pltpu.VMEM((2, GROUPS, TRAJ * MIX, WIDE), BF16),
            pltpu.VMEM((TRAJ * MIX, WIDE), F32),
            pltpu.VMEM((2, GROUPS, 2) + pieces, BF16),
            pltpu.VMEM((2, GROUPS) + pieces, BF16),
            pltpu.VMEM((2, GROUPS) + pieces, BF16),
            pltpu.VMEM((2, GROUPS) + pieces, BF16),
            pltpu.VMEM((2, GROUPS, 2) + pieces, BF16),
            pltpu.VMEM((GROUPS, SPACE, 16, LANES), BF16),
            pltpu.VMEM(band, BF16),
            pltpu.VMEM(band, BF16),
            pltpu.VMEM(band, BF16),
            pltpu.VMEM((GROUPS, SPACE, 16, LANES), BF16),
            dma((GROUPS,)),
            dma((GROUPS,)),
            dma((2,)),
            dma((GROUPS,)),
            dma((2, GROUPS)),
            dma((2, GROUPS)),
            dma((2, GROUPS)),
            dma((2, GROUPS, CHIPS)),
            dma((2, GROUPS, CHIPS)),
            dma((2, GROUPS, MEMBERS)),
            dma((2, GROUPS, MEMBERS)),
            dma((2, GROUPS, SPACE)),
            dma((2, GROUPS, SPACE)),
            dma((2, GROUPS, SPACE)),
            dma((2, GROUPS, SPACE)),
        ],
        compiler_params=pltpu.CompilerParams(
            vmem_limit_bytes=60 * 1024 * 1024, collective_id=0, has_side_effects=True
        ),
        name="step",
    )(
        clones.T,
        state,
        legendre,
        jnp.asarray(tall),
        jnp.asarray(wide),
        sin_lat,
        gravity,
        stability,
    )


def shards(spectra, legendre, sin_lat, gravity, stability, clones):
    state = spectra.transpose(1, 2, 0, 3)
    return step(state, legendre, sin_lat, gravity, stability, clones).transpose(2, 0, 1, 3)


def solution(mesh):
    placed = (P("member", None, "space", None), P("space", None, None), P(), P(), P(), P())
    return jax.shard_map(
        shards,
        mesh=mesh,
        in_specs=placed,
        out_specs=P("member", None, "space", None),
        check_vma=False,
    )
```

```python
import functools
import math

import jax
import jax.numpy as jnp
import numpy as np
from jax import lax
from jax.experimental import pallas as pl
from jax.experimental.pallas import tpu as pltpu
from jax.sharding import PartitionSpec as P

NW = 640
WIDTH = NW + 1
NLON = 1280
NLAT = 768
NHALF = 384
PAIRS = 320
TRAJ = 4
FIELDS = 6
LOCAL = 20
SPACE = 16
GROUP = 4
GROUPS = LOCAL // GROUP
FULL = 128 * FIELDS
LANES = FULL + 64 * FIELDS
PART = ((0, FULL), (FULL, LANES), (0, LANES))
BOTH = 2
MEMBERS = 8
CHIPS = 4
KILLED = 4
WIDE = 768
GROUPED = (GROUPS, 2 * FIELDS, GROUP, TRAJ, WIDTH)
MIX = 2 * FIELDS * GROUP
TILE = 16 * SPACE
EARLY = 2
MESH = pl.DeviceIdType.MESH
DT = 0.25
WAVE_SCALE = 16.0
DIFFUSION = 0.02
F32 = jnp.float32
BF16 = jnp.bfloat16


@functools.cache
def zonal_tables():
    pair = np.arange(PAIRS).reshape(SPACE, GROUPS, GROUP).transpose(1, 0, 2).reshape(-1)
    order = np.stack([pair, NW - 1 - pair], axis=1)
    phase = (order[:, :, None] * np.arange(NLON)) % NLON
    angle = phase * (2.0 * math.pi / NLON)
    table = np.stack([np.cos(angle), -np.sin(angle)], axis=2).reshape(4 * PAIRS, NLON)
    table = table.astype(jnp.bfloat16)
    return table, np.ascontiguousarray(table.T)


def row_col(rows, width):
    return (
        lax.broadcasted_iota(jnp.int32, (rows, width), 0),
        lax.broadcasted_iota(jnp.int32, (rows, width), 1),
    )


def sign_mask(pair):
    row, col = row_col(8, WIDTH)
    leading = (col < NW - pair).astype(jnp.int32)
    offset = jnp.where(leading == 1, col, col - (NW - pair))
    parity = (1 - 2 * (offset & 1)).astype(F32)
    sign = jnp.where(row >= 4, parity, 1.0)
    return jnp.where(((row >> 1) & 1) + leading == 1, sign, 0.0)


def swap4(value):
    return pltpu.roll(value, 4, 1)


def legendre_group(pair, now_ref, leg_ref, put):
    row8, _ = row_col(8, WIDTH)
    odd = (row8 & 1) == 1
    results = []
    for k in range(GROUP):
        mask = sign_mask(pair + k)
        pieces = []
        for t in range(TRAJ):
            for f in range(FIELDS):
                first = MIX * t + 2 * GROUP * f + k
                real, imag = (now_ref[row : row + 1, 0:WIDTH] for row in (first, first + GROUP))
                pieces.append(jnp.where(odd, imag, real) * mask)
        lhs = jnp.concatenate(pieces, axis=0).astype(BF16)
        dots = jnp.dot(lhs, leg_ref[k], preferred_element_type=F32)
        results.append(dots.reshape(TRAJ * FIELDS, 8, NHALF))
    upper = lax.broadcasted_iota(jnp.int32, (TRAJ * FIELDS, 8, NHALF), 1) < 4
    hemispheres = ([], [])
    for k in range(0, GROUP, 2):
        first, second = results[k], results[k + 1]
        hemispheres[0].append(jnp.where(upper, first, swap4(second)))
        hemispheres[1].append(jnp.where(upper, swap4(first), second))
    low = lax.broadcasted_iota(jnp.int32, (16, 128), 1) < 64
    for side in range(2):
        one, two = hemispheres[side]
        for t in range(TRAJ):
            for level in range(FIELDS // 2):
                tiles = []
                for f in (2 * level, 2 * level + 1):
                    tile = jnp.concatenate([one[t * FIELDS + f], two[t * FIELDS + f]], axis=0)
                    put(4 * t + 2 * side, 128 * f, tile[:, 0:128].astype(BF16))
                    put(4 * t + 2 * side + 1, 128 * f, tile[:, 128:256].astype(BF16))
                    tiles.append(tile[:, 256:384])
                a, b = tiles
                lane = FULL + 128 * level
                put(4 * t + 2 * side, lane, jnp.where(low, a, pltpu.roll(b, 64, 1)).astype(BF16))
                put(
                    4 * t + 2 * side + 1, lane, jnp.where(low, pltpu.roll(a, 64, 1), b).astype(BF16)
                )


def latitude_rows(sin_ref, place):
    low = lax.broadcasted_iota(jnp.int32, (1, 128), 1) < 64
    zero, one, two = (sin_ref[128 * i : 128 * i + 128].reshape(1, 128) for i in range(3))
    swapped = pltpu.roll(two, 64, 1)
    second = (place & 1) == 1
    sign = jnp.where((place & 3) >= 2, -1.0, 1.0).astype(F32)
    full = jnp.where(second, one, zero) * sign
    half = jnp.where(second, jnp.where(low, swapped, two), jnp.where(low, two, swapped)) * sign
    return full, half


def forcing_of(spin, spread, heat, heat_swapped, coriolis):
    spun = spin + coriolis
    return (
        -spun * spread,
        spun * spin - 0.5 * spread * spread,
        -(heat + 0.5 * (heat + heat_swapped)) * spread,
    )


def grid_forward(part, sines, f_ref, wide_ref, forcing_ref):
    start, stop = PART[part]
    tile = TILE

    def step(i, _):
        rows = pl.ds(pl.multiple_of(i * tile, tile), tile)
        sums = jnp.dot(wide_ref[rows, :], f_ref[:, start:stop], preferred_element_type=F32)
        sums = sums * (1.0 / NW)
        field = [sums[:, lane : lane + 128] for lane in range(0, stop - start, 128)]
        if part == 0:
            sets = [(field[a], field[2 + a], field[4 + a], field[5 - a]) for a in range(2)]
        else:
            sets = [(*field, pltpu.roll(field[2], 64, 1))]
        for a, fields in enumerate(sets):
            for g, made in enumerate(forcing_of(*fields, 2.0 * sines)):
                lane = start + 128 * (len(sets) * g + a)
                forcing_ref[rows, lane : lane + 128] = made.astype(BF16)
        return 0

    lax.fori_loop(0, NLON // tile, step, 0)


def grid_backward(part, sines, rows, forcing_ref, tall_ref, out_ref):
    start, stop = PART[part]
    weights = math.pi * jnp.sqrt(1.0 - sines * sines) / NLAT
    weights = jnp.concatenate([weights] * ((stop - start) // 128), axis=1)
    sums = jnp.dot(tall_ref[rows, :], forcing_ref[:, start:stop], preferred_element_type=F32)
    out_ref[rows, start:stop] = (sums * weights).astype(BF16)


def one_hot(condition):
    return jnp.where(condition, 1.0, 0.0).astype(BF16)


def square(rows):
    return row_col(rows, TRAJ * MIX)


def select_rows(clones_ref, member):
    row, col = square(MIX)
    parts = []
    for entry in range(KILLED):
        source = clones_ref[1, entry]
        wanted = jnp.where((source >> 2) == member, source & (TRAJ - 1), TRAJ)
        parts.append(one_hot((row == (col >> 2)) & ((col & 3) == wanted)))
    return jnp.concatenate(parts, axis=0)


def entry_of(clones_ref, number):
    found = KILLED
    for entry in range(KILLED):
        found = jnp.where(clones_ref[0, entry] == number, entry, found)
    return found


def entry_columns(col):
    return sum((col >= MIX * i).astype(jnp.int32) for i in range(1, KILLED))


def keep_and_put(clones_ref, member):
    row, col = square(MIX)
    entry = entry_columns(col)
    keep, put = [], []
    for t in range(TRAJ):
        found = entry_of(clones_ref, member * TRAJ + t)
        own = jnp.where(found == KILLED, t, TRAJ)
        keep.append(one_hot((row == (col >> 2)) & ((col & 3) == own)))
        put.append(one_hot((row == col - MIX * entry) & (entry == found)))
    return jnp.concatenate(keep, axis=0), jnp.concatenate(put, axis=0)


def by_trajectory(values, row):
    mixed = values[0]
    for t in range(1, TRAJ):
        mixed = jnp.where(row == t, values[t], mixed)
    return mixed


def place_rows(clones_ref, member):
    row, col = square(TRAJ * MIX)
    entry = entry_columns(col)
    found = [entry_of(clones_ref, member * TRAJ + t) for t in range(TRAJ)]
    return one_hot((entry == by_trajectory(found, row & 3)) & ((row >> 2) == col - MIX * entry))


def unmix():
    row, col = row_col(128, 128)
    t, half, side, part, pair = row & 3, (row >> 2) & 1, (row >> 3) & 1, (row >> 4) & 1, row >> 5
    return one_hot(col == 32 * t + 16 * side + 4 * pair + 2 * half + part)


def project_rows(back_ref):
    low = lax.broadcasted_iota(jnp.int32, (128, 128), 1) < 64
    order = unmix()

    def column(odd, lane):
        return jnp.concatenate(
            [
                back_ref[4 * t + 2 * side + odd, :, lane : lane + 128]
                for t in range(TRAJ)
                for side in range(2)
            ],
            axis=0,
        )

    fields = []
    for level in range(FIELDS // 2):
        lanes = [256 * level, 256 * level + 128, FULL + 128 * level]
        mixed = jnp.concatenate([column(odd, lane) for lane in lanes for odd in range(2)], axis=1)
        rows = jnp.dot(order, mixed, preferred_element_type=F32)
        a, b = rows[:, 512:640], rows[:, 640:768]
        last = (
            jnp.where(low, a, pltpu.roll(b, 64, 1)),
            jnp.where(low, pltpu.roll(a, 64, 1), b),
        )
        for h in range(2):
            fields.append(
                jnp.concatenate([rows[:, 256 * h : 256 * h + 256], last[h]], axis=1).astype(BF16)
            )
    return fields


def project_group(first_pair, back_ref, leg_ref, state_ref, grav_ref, stab_ref):
    g = [[grav_ref[a, b] for b in range(2)] for a in range(2)]
    s = [[stab_ref[a, b] for b in range(2)] for a in range(2)]
    gs = [[g[a][0] * s[0][b] + g[a][1] * s[1][b] for b in range(2)] for a in range(2)]
    fields = project_rows(back_ref)
    row8, _ = row_col(8, WIDTH)
    upper = row8 < 4
    _, col = row_col(1, WIDTH)
    for k in range(GROUP):
        pair = first_pair + k
        lhs = jnp.concatenate([rows[32 * k : 32 * k + 32] for rows in fields], axis=0)
        sums = lax.dot_general(
            lhs, leg_ref[k], (((1,), (1,)), ((), ())), preferred_element_type=F32
        )
        leading = col < NW - pair
        offset = jnp.where(leading, col, col - (NW - pair))
        parity = (1 - 2 * (offset & 1)).astype(F32)
        degree = jnp.where(leading, pair, NW - 1 - pair) + offset
        lam = WAVE_SCALE * (degree * (degree + 1)).astype(F32) / float(NW * NW)
        damp = 1.0 / (1.0 + DIFFUSION * lam * lam)
        coupling = DT * DT * lam
        diag = [1.0 + coupling * gs[a][a] for a in range(2)]
        cross = [coupling * gs[0][1], coupling * gs[1][0]]
        inverse = 1.0 / (diag[0] * diag[1] - cross[0] * cross[1])
        weight = [[DT * lam * g[a][b] for b in range(2)] for a in range(2)]
        left = jnp.broadcast_to(leading, (8, WIDTH))

        def moved(f):
            part = []
            for r in range(2):
                first = 32 * f + 16 * r
                part.append(sums[first : first + 8] + parity * sums[first + 8 : first + 16])
            near = jnp.where(upper, part[0], pltpu.roll(part[1], 4, 0))
            far = jnp.where(upper, pltpu.roll(part[0], 4, 0), part[1])
            old = jnp.concatenate([state_ref[2 * f, k], state_ref[2 * f + 1, k]], axis=0)
            return old + DT * jnp.where(left, near, far)

        def store(f, value):
            state_ref[2 * f, k] = value[0:4]
            state_ref[2 * f + 1, k] = value[4:8]

        for a in range(2):
            store(a, damp * moved(a))
        heat = [moved(4), moved(5)]
        right = [moved(2 + a) + (weight[a][0] * heat[0] + weight[a][1] * heat[1]) for a in range(2)]
        new = [
            (diag[1] * right[0] - cross[0] * right[1]) * inverse,
            (diag[0] * right[1] - cross[1] * right[0]) * inverse,
        ]
        for a in range(2):
            store(2 + a, damp * new[a])
            store(4 + a, damp * (heat[a] - DT * (s[a][0] * new[0] + s[a][1] * new[1])))


def spread(axis, count, body):
    me = lax.axis_index(axis)

    for d in range(1, count):
        body((me + d) & (count - 1))


def main_kernel(
    clones_ref,
    x_any,
    leg_any,
    tall_any,
    wide_any,
    sin_ref,
    grav_ref,
    stab_ref,
    new_any,
    leg_ref,
    tall_ref,
    wide_ref,
    xg_ref,
    half_ref,
    now_ref,
    hand_ref,
    core_ref,
    pair_ref,
    landed_ref,
    shared_ref,
    send_ref,
    fourier_ref,
    forcing_ref,
    give_ref,
    back_ref,
    x_sem,
    leg_sem,
    table_sem,
    state_sem,
    own_sem,
    core_send,
    core_recv,
    rs_send,
    rs_recv,
    ag_send,
    ag_recv,
    over_send,
    over_recv,
    out_send,
    out_recv,
    back_send,
    back_recv,
):
    member = lax.axis_index("member")
    place = lax.axis_index("space")
    core = member & 1
    chip = member >> 1
    partner = member + 1 - 2 * core
    sines = latitude_rows(sin_ref, place)

    def x_copy(g):
        some = pl.ds(g * GROUP, GROUP)
        return pltpu.make_async_copy(x_any.at[:, some], xg_ref.at[g], x_sem.at[g])

    def leg_copy(g):
        some = pl.ds(g * GROUP, GROUP)
        return pltpu.make_async_copy(leg_any.at[some], leg_ref.at[some], leg_sem.at[g])

    for copy in (x_copy, leg_copy):
        for g in range(GROUPS):
            copy(g).start()
    wide_copy = pltpu.make_async_copy(wide_any, wide_ref, table_sem.at[0])
    tall_copy = pltpu.make_async_copy(tall_any, tall_ref, table_sem.at[1])
    wide_copy.start()
    tall_copy.start()

    barrier = pltpu.get_barrier_semaphore()
    spread(
        "space",
        SPACE,
        lambda peer: pl.semaphore_signal(
            barrier, inc=1, device_id={"space": peer}, device_id_type=MESH
        ),
    )
    spread(
        "member",
        MEMBERS,
        lambda peer: pl.semaphore_signal(
            barrier, inc=1, device_id={"member": peer}, device_id_type=MESH
        ),
    )

    def across(q, g):
        return pltpu.make_async_remote_copy(
            src_ref=hand_ref.at[q, g, 1 - core],
            dst_ref=core_ref.at[q, g],
            send_sem=core_send.at[q, g],
            recv_sem=core_recv.at[q, g],
            device_id={"member": partner},
            device_id_type=MESH,
        )

    def scatter(q, g, peer, source):
        return pltpu.make_async_remote_copy(
            src_ref=pair_ref.at[q, g, peer],
            dst_ref=landed_ref.at[q, g, source],
            send_sem=rs_send.at[q, g, peer],
            recv_sem=rs_recv.at[q, g, source],
            device_id={"member": 2 * peer + core},
            device_id_type=MESH,
        )

    def gather(q, g, peer, source):
        return pltpu.make_async_remote_copy(
            src_ref=shared_ref.at[q, g, core, source],
            dst_ref=shared_ref.at[q, g, core, source],
            send_sem=ag_send.at[q, g, peer],
            recv_sem=ag_recv.at[q, g, source],
            device_id={"member": 2 * peer + core},
            device_id_type=MESH,
        )

    def hand_over(q, g, half):
        return pltpu.make_async_remote_copy(
            src_ref=shared_ref.at[q, g, half],
            dst_ref=shared_ref.at[q, g, half],
            send_sem=over_send.at[q, g],
            recv_sem=over_recv.at[q, g],
            device_id={"member": partner},
            device_id_type=MESH,
        )

    def other_chips(body):
        for d in range(1, CHIPS):
            body((chip + d) & (CHIPS - 1))

    def regroup(g):
        rows = jnp.concatenate(
            [xg_ref[g, c, p] for c in range(2 * FIELDS) for p in range(GROUP)], axis=0
        )
        _, lane = row_col(TRAJ * MIX, 128)
        value = jnp.concatenate(
            [rows[:, 0:NW], jnp.where(lane < 1, rows[:, NW:WIDTH], 0.0)], axis=1
        )
        high = value.astype(BF16)
        half_ref[0, g] = high
        half_ref[1, g] = (value - high.astype(F32)).astype(BF16)

    selection = select_rows(clones_ref, member)

    def offer(q, g):
        value = jnp.dot(selection, half_ref[q, g], preferred_element_type=F32).astype(BF16)
        for entry in range(KILLED):
            rows = slice(MIX * entry, MIX * entry + MIX)
            hand_ref[q, g, 0, entry] = value[rows, 0 : WIDE // 2]
            hand_ref[q, g, 1, entry] = value[rows, WIDE // 2 : WIDE]
        across(q, g).start()

    def combine(q, g):
        across(q, g).wait_recv()
        total = hand_ref[q, g, core].astype(F32) + core_ref[q, g].astype(F32)
        pair_ref[q, g] = total.astype(BF16)
        other_chips(lambda peer: scatter(q, g, peer, chip).start())

    def settle(q, g):
        other_chips(lambda peer: scatter(q, g, peer, peer).wait_recv())
        total = pair_ref[q, g, chip].astype(F32)
        for d in range(1, CHIPS):
            total = total + landed_ref[q, g, (chip + d) & (CHIPS - 1)].astype(F32)
        shared_ref[q, g, core, chip] = total.astype(BF16)
        other_chips(lambda peer: gather(q, g, peer, chip).start())

    def forward(q, g):
        other_chips(lambda peer: gather(q, g, peer, peer).wait_recv())
        hand_over(q, g, core).start()

    def arrived(q, g):
        hand_over(q, g, 1 - core).wait_recv()

    def received(q, g):
        return jnp.concatenate(
            [
                jnp.concatenate([shared_ref[q, g, 0, e], shared_ref[q, g, 1, e]], axis=1)
                for e in range(KILLED)
            ],
            axis=0,
        )

    def outward(part, g, peer, source):
        start, stop = PART[part]
        lanes = pl.ds(start, stop - start)
        return pltpu.make_async_remote_copy(
            src_ref=send_ref.at[g, peer, :, lanes],
            dst_ref=fourier_ref.at[pl.ds(g * TILE + source * 16, 16), lanes],
            send_sem=out_send.at[part % BOTH, g, peer],
            recv_sem=out_recv.at[part % BOTH, g, source],
            device_id={"space": peer},
            device_id_type=MESH,
        )

    def homeward(part, g, peer, source):
        start, stop = PART[part]
        lanes = pl.ds(start, stop - start)
        return pltpu.make_async_remote_copy(
            src_ref=give_ref.at[pl.ds(g * TILE + peer * 16, 16), lanes],
            dst_ref=back_ref.at[g, source, :, lanes],
            send_sem=back_send.at[part, g, peer],
            recv_sem=back_recv.at[part, g, source],
            device_id={"space": peer},
            device_id_type=MESH,
        )

    def own_out(g):
        rows = pl.ds(g * TILE + place * 16, 16)
        return pltpu.make_async_copy(send_ref.at[g, place], fourier_ref.at[rows], own_sem.at[0, g])

    def own_back(g):
        rows = pl.ds(g * TILE + place * 16, 16)
        return pltpu.make_async_copy(give_ref.at[rows], back_ref.at[g, place], own_sem.at[1, g])

    def each_group(body, first=0, last=GROUPS):
        def one(g, _):
            body(g)
            return 0

        lax.fori_loop(first, last, one, 0)

    def each_message(part, body):
        if part == 0:
            each_group(lambda g: body(BOTH, g), 0, EARLY)
        each_group(lambda g: body(part, g), EARLY, GROUPS)

    def send_out(part, g):
        spread("space", SPACE, lambda peer: outward(part, g, peer, place).start())

    x_copy(0).wait()
    regroup(0)
    pl.semaphore_wait(barrier, SPACE + MEMBERS - 2)
    offer(0, 0)

    x_copy(1).wait()
    regroup(1)
    offer(0, 1)
    combine(0, 0)
    keep, put_rows = keep_and_put(clones_ref, member)
    combine(0, 1)
    settle(0, 0)
    x_copy(2).wait()
    regroup(2)
    offer(0, 2)
    settle(0, 1)
    forward(0, 0)
    x_copy(3).wait()
    regroup(3)
    offer(0, 3)
    combine(0, 2)

    def legendre_step(g, _):
        arrived(0, g)
        now = jnp.dot(keep, half_ref[0, g], preferred_element_type=F32)
        now_ref[...] = now + jnp.dot(put_rows, received(0, g), preferred_element_type=F32)
        leg_copy(g).wait()

        def put(block, lane, value):
            send_ref[g, block, :, lane : lane + 128] = value

        legendre_group(
            place * LOCAL + g * GROUP, now_ref, leg_ref.at[pl.ds(g * GROUP, GROUP)], put
        )
        @pl.when(g < EARLY)
        def _():
            send_out(BOTH, g)

        @pl.when(g >= EARLY)
        def _():
            send_out(0, g)

        own_out(g).start()

        @pl.when(g + 2 < GROUPS)
        def _():
            settle(0, g + 2)

        @pl.when(g + 3 < GROUPS)
        def _():
            combine(0, g + 3)

        @pl.when(g + 1 < GROUPS)
        def _():
            forward(0, g + 1)

        @pl.when(g + 4 < GROUPS)
        def _():
            x_copy(g + 4).wait()
            regroup(g + 4)
            offer(0, g + 4)

        return 0

    lax.fori_loop(0, GROUPS, legendre_step, 0)

    def send_late(g, _):
        send_out(1, g)
        return 0

    lax.fori_loop(EARLY, GROUPS, send_late, 0)
    each_group(lambda g: offer(1, g))
    each_group(lambda g: combine(1, g))
    wide_copy.wait()
    tall_copy.wait()
    each_group(lambda g: own_out(g).wait())

    for part in range(2):
        each_message(
            part,
            lambda kind, g: spread(
                "space", SPACE, lambda peer: outward(kind, g, peer, peer).wait_recv()
            ),
        )
        grid_forward(part, sines[part], fourier_ref, wide_ref, forcing_ref)

        def backward(g):
            rows = pl.ds(pl.multiple_of(g * TILE, TILE), TILE)
            grid_backward(part, sines[part], rows, forcing_ref, tall_ref, give_ref)
            spread("space", SPACE, lambda peer: homeward(part, g, peer, place).start())

        each_group(backward)
        if part == 0:
            each_group(lambda g: settle(1, g))
        else:
            each_group(lambda g: forward(1, g))
    each_group(lambda g: own_back(g).start())

    placing = place_rows(clones_ref, member)
    row, _ = row_col(TRAJ, WIDTH)
    killed = by_trajectory(
        [entry_of(clones_ref, member * TRAJ + t) for t in range(TRAJ)], row
    )

    def complete(g):
        arrived(1, g)
        value = sum(
            jnp.dot(placing, received(q, g), preferred_element_type=F32) for q in range(2)
        )
        for c in range(2 * FIELDS):
            for p in range(GROUP):
                first = (c * GROUP + p) * TRAJ
                new = value[first : first + TRAJ, 0:WIDTH]
                xg_ref[g, c, p] = jnp.where(killed < KILLED, new, xg_ref[g, c, p])

    def new_copy(g):
        some = pl.ds(g * GROUP, GROUP)
        return pltpu.make_async_copy(xg_ref.at[g], new_any.at[:, some], state_sem.at[g])

    def project(g):
        own_back(g).wait()
        for part in range(2):
            spread(
                "space", SPACE, lambda peer: homeward(part, g, peer, peer).wait_recv()
            )
        project_group(
            place * LOCAL + g * GROUP,
            back_ref.at[g],
            leg_ref.at[pl.ds(g * GROUP, GROUP)],
            xg_ref.at[g],
            grav_ref,
            stab_ref,
        )
        new_copy(g).start()

    each_group(complete)
    each_group(project)
    for q in range(2):
        each_group(lambda g: across(q, g).wait_send())
        each_group(lambda g: other_chips(lambda peer: scatter(q, g, peer, chip).wait_send()))
        each_group(lambda g: other_chips(lambda peer: gather(q, g, peer, chip).wait_send()))
        each_group(lambda g: hand_over(q, g, core).wait_send())
    for part in range(2):
        each_message(
            part,
            lambda kind, g: spread(
                "space", SPACE, lambda peer: outward(kind, g, peer, place).wait_send()
            ),
        )
        each_group(
            lambda g: spread(
                "space", SPACE, lambda peer: homeward(part, g, peer, place).wait_send()
            )
        )
    each_group(lambda g: new_copy(g).wait())


STATE = (2 * FIELDS, LOCAL, TRAJ, WIDTH)


def step(state, legendre, sin_lat, gravity, stability, clones):
    tall, wide = zonal_tables()
    anywhere = pl.BlockSpec(memory_space=pl.ANY)
    vmem = pl.BlockSpec(memory_space=pltpu.VMEM)
    smem = pl.BlockSpec(memory_space=pltpu.SMEM)
    dma = pltpu.SemaphoreType.DMA
    pieces = (KILLED, MIX, WIDE // 2)
    band = (4 * PAIRS, LANES)
    return pl.pallas_call(
        main_kernel,
        in_specs=[smem, anywhere, anywhere, anywhere, anywhere, vmem, smem, smem],
        out_specs=anywhere,
        out_shape=jax.ShapeDtypeStruct(STATE, F32),
        scratch_shapes=[
            pltpu.VMEM((LOCAL, WIDTH, NHALF), BF16),
            pltpu.VMEM((4 * PAIRS, NLON), BF16),
            pltpu.VMEM((NLON, 4 * PAIRS), BF16),
            pltpu.VMEM(GROUPED, F32),
            pltpu.VMEM((2, GROUPS, TRAJ * MIX, WIDE), BF16),
            pltpu.VMEM((TRAJ * MIX, WIDE), F32),
            pltpu.VMEM((2, GROUPS, 2) + pieces, BF16),
            pltpu.VMEM((2, GROUPS) + pieces, BF16),
            pltpu.VMEM((2, GROUPS) + pieces, BF16),
            pltpu.VMEM((2, GROUPS) + pieces, BF16),
            pltpu.VMEM((2, GROUPS, 2) + pieces, BF16),
            pltpu.VMEM((GROUPS, SPACE, 16, LANES), BF16),
            pltpu.VMEM(band, BF16),
            pltpu.VMEM(band, BF16),
            pltpu.VMEM(band, BF16),
            pltpu.VMEM((GROUPS, SPACE, 16, LANES), BF16),
            dma((GROUPS,)),
            dma((GROUPS,)),
            dma((2,)),
            dma((GROUPS,)),
            dma((2, GROUPS)),
            dma((2, GROUPS)),
            dma((2, GROUPS)),
            dma((2, GROUPS, CHIPS)),
            dma((2, GROUPS, CHIPS)),
            dma((2, GROUPS, CHIPS)),
            dma((2, GROUPS, CHIPS)),
            dma((2, GROUPS)),
            dma((2, GROUPS)),
            dma((2, GROUPS, SPACE)),
            dma((2, GROUPS, SPACE)),
            dma((2, GROUPS, SPACE)),
            dma((2, GROUPS, SPACE)),
        ],
        compiler_params=pltpu.CompilerParams(
            vmem_limit_bytes=60 * 1024 * 1024, collective_id=0, has_side_effects=True
        ),
        name="step",
    )(
        clones.T,
        state,
        legendre,
        jnp.asarray(tall),
        jnp.asarray(wide),
        sin_lat,
        gravity,
        stability,
    )


def shards(spectra, legendre, sin_lat, gravity, stability, clones):
    state = spectra.transpose(1, 2, 0, 3)
    return step(state, legendre, sin_lat, gravity, stability, clones).transpose(2, 0, 1, 3)


def solution(mesh):
    placed = (P("member", None, "space", None), P("space", None, None), P(), P(), P(), P())
    return jax.shard_map(
        shards,
        mesh=mesh,
        in_specs=placed,
        out_specs=P("member", None, "space", None),
        check_vma=False,
    )
```

```python
import functools
import math

import jax
import jax.numpy as jnp
import numpy as np
from jax import lax
from jax.experimental import pallas as pl
from jax.experimental.pallas import tpu as pltpu
from jax.sharding import PartitionSpec as P

NW = 640
WIDTH = NW + 1
NLON = 1280
NLAT = 768
NHALF = 384
PAIRS = 320
TRAJ = 4
FIELDS = 6
LOCAL = 20
SPACE = 16
GROUP = 4
GROUPS = LOCAL // GROUP
FULL = 128 * FIELDS
LANES = FULL + 64 * FIELDS
PART = ((0, FULL), (FULL, LANES), (0, LANES))
BOTH = 2
MEMBERS = 8
CHIPS = 4
KILLED = 4
WIDE = 768
GROUPED = (GROUPS, 2 * FIELDS, GROUP, TRAJ, WIDTH)
MIX = 2 * FIELDS * GROUP
TILE = 16 * SPACE
EARLY = 2
MESH = pl.DeviceIdType.MESH
DT = 0.25
WAVE_SCALE = 16.0
DIFFUSION = 0.02
F32 = jnp.float32
BF16 = jnp.bfloat16


@functools.cache
def zonal_tables():
    pair = np.arange(PAIRS).reshape(SPACE, GROUPS, GROUP).transpose(1, 0, 2).reshape(-1)
    order = np.stack([pair, NW - 1 - pair], axis=1)
    phase = (order[:, :, None] * np.arange(NLON)) % NLON
    angle = phase * (2.0 * math.pi / NLON)
    table = np.stack([np.cos(angle), -np.sin(angle)], axis=2).reshape(4 * PAIRS, NLON)
    table = table.astype(jnp.bfloat16)
    return table, np.ascontiguousarray(table.T)


def row_col(rows, width):
    return (
        lax.broadcasted_iota(jnp.int32, (rows, width), 0),
        lax.broadcasted_iota(jnp.int32, (rows, width), 1),
    )


def sign_mask(pair):
    row, col = row_col(8, WIDTH)
    leading = (col < NW - pair).astype(jnp.int32)
    offset = jnp.where(leading == 1, col, col - (NW - pair))
    parity = (1 - 2 * (offset & 1)).astype(F32)
    sign = jnp.where(row >= 4, parity, 1.0)
    return jnp.where(((row >> 1) & 1) + leading == 1, sign, 0.0)


def swap4(value):
    return pltpu.roll(value, 4, 1)


def legendre_group(pair, now_ref, leg_ref, put):
    row8, _ = row_col(8, WIDTH)
    odd = (row8 & 1) == 1
    results = []
    for k in range(GROUP):
        mask = sign_mask(pair + k)
        pieces = []
        for t in range(TRAJ):
            for f in range(FIELDS):
                first = MIX * t + 2 * GROUP * f + k
                real, imag = (now_ref[row : row + 1, 0:WIDTH] for row in (first, first + GROUP))
                pieces.append(jnp.where(odd, imag, real) * mask)
        lhs = jnp.concatenate(pieces, axis=0).astype(BF16)
        dots = jnp.dot(lhs, leg_ref[k], preferred_element_type=F32)
        results.append(dots.reshape(TRAJ * FIELDS, 8, NHALF))
    upper = lax.broadcasted_iota(jnp.int32, (TRAJ * FIELDS, 8, NHALF), 1) < 4
    hemispheres = ([], [])
    for k in range(0, GROUP, 2):
        first, second = results[k], results[k + 1]
        hemispheres[0].append(jnp.where(upper, first, swap4(second)))
        hemispheres[1].append(jnp.where(upper, swap4(first), second))
    low = lax.broadcasted_iota(jnp.int32, (16, 128), 1) < 64
    for side in range(2):
        one, two = hemispheres[side]
        for t in range(TRAJ):
            for level in range(FIELDS // 2):
                tiles = []
                for f in (2 * level, 2 * level + 1):
                    tile = jnp.concatenate([one[t * FIELDS + f], two[t * FIELDS + f]], axis=0)
                    put(4 * t + 2 * side, 128 * f, tile[:, 0:128].astype(BF16))
                    put(4 * t + 2 * side + 1, 128 * f, tile[:, 128:256].astype(BF16))
                    tiles.append(tile[:, 256:384])
                a, b = tiles
                lane = FULL + 128 * level
                put(4 * t + 2 * side, lane, jnp.where(low, a, pltpu.roll(b, 64, 1)).astype(BF16))
                put(
                    4 * t + 2 * side + 1, lane, jnp.where(low, pltpu.roll(a, 64, 1), b).astype(BF16)
                )


def latitude_rows(sin_ref, place):
    low = lax.broadcasted_iota(jnp.int32, (1, 128), 1) < 64
    zero, one, two = (sin_ref[128 * i : 128 * i + 128].reshape(1, 128) for i in range(3))
    swapped = pltpu.roll(two, 64, 1)
    second = (place & 1) == 1
    sign = jnp.where((place & 3) >= 2, -1.0, 1.0).astype(F32)
    full = jnp.where(second, one, zero) * sign
    half = jnp.where(second, jnp.where(low, swapped, two), jnp.where(low, two, swapped)) * sign
    return full, half


def forcing_of(spin, spread, heat, heat_swapped, coriolis):
    spun = spin + coriolis
    return (
        -spun * spread,
        spun * spin - 0.5 * spread * spread,
        -(heat + 0.5 * (heat + heat_swapped)) * spread,
    )


def grid_forward(part, sines, f_ref, wide_ref, forcing_ref):
    start, stop = PART[part]
    tile = TILE

    def step(i, _):
        rows = pl.ds(pl.multiple_of(i * tile, tile), tile)
        sums = jnp.dot(wide_ref[rows, :], f_ref[:, start:stop], preferred_element_type=F32)
        sums = sums * (1.0 / NW)
        field = [sums[:, lane : lane + 128] for lane in range(0, stop - start, 128)]
        if part == 0:
            sets = [(field[a], field[2 + a], field[4 + a], field[5 - a]) for a in range(2)]
        else:
            sets = [(*field, pltpu.roll(field[2], 64, 1))]
        for a, fields in enumerate(sets):
            for g, made in enumerate(forcing_of(*fields, 2.0 * sines)):
                lane = start + 128 * (len(sets) * g + a)
                forcing_ref[rows, lane : lane + 128] = made.astype(BF16)
        return 0

    lax.fori_loop(0, NLON // tile, step, 0)


def grid_backward(part, sines, rows, forcing_ref, tall_ref, out_ref):
    start, stop = PART[part]
    weights = math.pi * jnp.sqrt(1.0 - sines * sines) / NLAT
    weights = jnp.concatenate([weights] * ((stop - start) // 128), axis=1)
    sums = jnp.dot(tall_ref[rows, :], forcing_ref[:, start:stop], preferred_element_type=F32)
    out_ref[rows, start:stop] = (sums * weights).astype(BF16)


def one_hot(condition):
    return jnp.where(condition, 1.0, 0.0).astype(BF16)


def square(rows):
    return row_col(rows, TRAJ * MIX)


def select_rows(clones_ref, member):
    row, col = square(MIX)
    parts = []
    for entry in range(KILLED):
        source = clones_ref[1, entry]
        wanted = jnp.where((source >> 2) == member, source & (TRAJ - 1), TRAJ)
        parts.append(one_hot((row == (col >> 2)) & ((col & 3) == wanted)))
    return jnp.concatenate(parts, axis=0)


def entry_of(clones_ref, number):
    found = KILLED
    for entry in range(KILLED):
        found = jnp.where(clones_ref[0, entry] == number, entry, found)
    return found


def entry_columns(col):
    return sum((col >= MIX * i).astype(jnp.int32) for i in range(1, KILLED))


def keep_and_put(clones_ref, member):
    row, col = square(MIX)
    entry = entry_columns(col)
    keep, put = [], []
    for t in range(TRAJ):
        found = entry_of(clones_ref, member * TRAJ + t)
        own = jnp.where(found == KILLED, t, TRAJ)
        keep.append(one_hot((row == (col >> 2)) & ((col & 3) == own)))
        put.append(one_hot((row == col - MIX * entry) & (entry == found)))
    return jnp.concatenate(keep, axis=0), jnp.concatenate(put, axis=0)


def by_trajectory(values, row):
    mixed = values[0]
    for t in range(1, TRAJ):
        mixed = jnp.where(row == t, values[t], mixed)
    return mixed


def place_rows(clones_ref, member):
    row, col = square(TRAJ * MIX)
    entry = entry_columns(col)
    found = [entry_of(clones_ref, member * TRAJ + t) for t in range(TRAJ)]
    return one_hot((entry == by_trajectory(found, row & 3)) & ((row >> 2) == col - MIX * entry))


def unmix():
    row, col = row_col(128, 128)
    t, half, side, part, pair = row & 3, (row >> 2) & 1, (row >> 3) & 1, (row >> 4) & 1, row >> 5
    return one_hot(col == 32 * t + 16 * side + 4 * pair + 2 * half + part)


def project_rows(back_ref):
    low = lax.broadcasted_iota(jnp.int32, (128, 128), 1) < 64
    order = unmix()

    def column(odd, lane):
        return jnp.concatenate(
            [
                back_ref[4 * t + 2 * side + odd, :, lane : lane + 128]
                for t in range(TRAJ)
                for side in range(2)
            ],
            axis=0,
        )

    fields = []
    for level in range(FIELDS // 2):
        lanes = [256 * level, 256 * level + 128, FULL + 128 * level]
        mixed = jnp.concatenate([column(odd, lane) for lane in lanes for odd in range(2)], axis=1)
        rows = jnp.dot(order, mixed, preferred_element_type=F32)
        a, b = rows[:, 512:640], rows[:, 640:768]
        last = (
            jnp.where(low, a, pltpu.roll(b, 64, 1)),
            jnp.where(low, pltpu.roll(a, 64, 1), b),
        )
        for h in range(2):
            fields.append(
                jnp.concatenate([rows[:, 256 * h : 256 * h + 256], last[h]], axis=1).astype(BF16)
            )
    return fields


def project_group(first_pair, back_ref, leg_ref, state_ref, grav_ref, stab_ref):
    g = [[grav_ref[a, b] for b in range(2)] for a in range(2)]
    s = [[stab_ref[a, b] for b in range(2)] for a in range(2)]
    gs = [[g[a][0] * s[0][b] + g[a][1] * s[1][b] for b in range(2)] for a in range(2)]
    fields = project_rows(back_ref)
    row8, _ = row_col(8, WIDTH)
    upper = row8 < 4
    _, col = row_col(1, WIDTH)
    for k in range(GROUP):
        pair = first_pair + k
        lhs = jnp.concatenate([rows[32 * k : 32 * k + 32] for rows in fields], axis=0)
        sums = lax.dot_general(
            lhs, leg_ref[k], (((1,), (1,)), ((), ())), preferred_element_type=F32
        )
        leading = col < NW - pair
        offset = jnp.where(leading, col, col - (NW - pair))
        parity = (1 - 2 * (offset & 1)).astype(F32)
        degree = jnp.where(leading, pair, NW - 1 - pair) + offset
        lam = WAVE_SCALE * (degree * (degree + 1)).astype(F32) / float(NW * NW)
        damp = 1.0 / (1.0 + DIFFUSION * lam * lam)
        coupling = DT * DT * lam
        diag = [1.0 + coupling * gs[a][a] for a in range(2)]
        cross = [coupling * gs[0][1], coupling * gs[1][0]]
        inverse = 1.0 / (diag[0] * diag[1] - cross[0] * cross[1])
        weight = [[DT * lam * g[a][b] for b in range(2)] for a in range(2)]
        left = jnp.broadcast_to(leading, (8, WIDTH))

        def moved(f):
            part = []
            for r in range(2):
                first = 32 * f + 16 * r
                part.append(sums[first : first + 8] + parity * sums[first + 8 : first + 16])
            near = jnp.where(upper, part[0], pltpu.roll(part[1], 4, 0))
            far = jnp.where(upper, pltpu.roll(part[0], 4, 0), part[1])
            old = jnp.concatenate([state_ref[2 * f, k], state_ref[2 * f + 1, k]], axis=0)
            return old + DT * jnp.where(left, near, far)

        def store(f, value):
            state_ref[2 * f, k] = value[0:4]
            state_ref[2 * f + 1, k] = value[4:8]

        for a in range(2):
            store(a, damp * moved(a))
        heat = [moved(4), moved(5)]
        right = [moved(2 + a) + (weight[a][0] * heat[0] + weight[a][1] * heat[1]) for a in range(2)]
        new = [
            (diag[1] * right[0] - cross[0] * right[1]) * inverse,
            (diag[0] * right[1] - cross[1] * right[0]) * inverse,
        ]
        for a in range(2):
            store(2 + a, damp * new[a])
            store(4 + a, damp * (heat[a] - DT * (s[a][0] * new[0] + s[a][1] * new[1])))


def spread(axis, count, body):
    me = lax.axis_index(axis)

    for d in range(1, count):
        body((me + d) & (count - 1))


def main_kernel(
    clones_ref,
    x_any,
    leg_any,
    tall_any,
    wide_any,
    sin_ref,
    grav_ref,
    stab_ref,
    new_any,
    leg_ref,
    tall_ref,
    wide_ref,
    xg_ref,
    half_ref,
    now_ref,
    hand_ref,
    core_ref,
    pair_ref,
    landed_ref,
    shared_ref,
    send_ref,
    fourier_ref,
    forcing_ref,
    give_ref,
    back_ref,
    x_sem,
    leg_sem,
    table_sem,
    state_sem,
    own_sem,
    core_send,
    core_recv,
    rs_send,
    rs_recv,
    ag_send,
    ag_recv,
    over_send,
    over_recv,
    out_send,
    out_recv,
    back_send,
    back_recv,
):
    member = lax.axis_index("member")
    place = lax.axis_index("space")
    core = member & 1
    chip = member >> 1
    partner = member + 1 - 2 * core
    sines = latitude_rows(sin_ref, place)

    def x_copy(g):
        some = pl.ds(g * GROUP, GROUP)
        return pltpu.make_async_copy(x_any.at[:, some], xg_ref.at[g], x_sem.at[g])

    def leg_copy(g):
        some = pl.ds(g * GROUP, GROUP)
        return pltpu.make_async_copy(leg_any.at[some], leg_ref.at[some], leg_sem.at[g])

    for copy in (x_copy, leg_copy):
        for g in range(GROUPS):
            copy(g).start()
    wide_copy = pltpu.make_async_copy(wide_any, wide_ref, table_sem.at[0])
    tall_copy = pltpu.make_async_copy(tall_any, tall_ref, table_sem.at[1])
    wide_copy.start()
    tall_copy.start()

    barrier = pltpu.get_barrier_semaphore()
    spread(
        "space",
        SPACE,
        lambda peer: pl.semaphore_signal(
            barrier, inc=1, device_id={"space": peer}, device_id_type=MESH
        ),
    )
    spread(
        "member",
        MEMBERS,
        lambda peer: pl.semaphore_signal(
            barrier, inc=1, device_id={"member": peer}, device_id_type=MESH
        ),
    )

    def across(q, g):
        return pltpu.make_async_remote_copy(
            src_ref=hand_ref.at[q, g, 1 - core],
            dst_ref=core_ref.at[q, g],
            send_sem=core_send.at[q, g],
            recv_sem=core_recv.at[q, g],
            device_id={"member": partner},
            device_id_type=MESH,
        )

    def scatter(q, g, peer, source):
        return pltpu.make_async_remote_copy(
            src_ref=pair_ref.at[q, g, peer],
            dst_ref=landed_ref.at[q, g, source],
            send_sem=rs_send.at[q, g, peer],
            recv_sem=rs_recv.at[q, g, source],
            device_id={"member": 2 * peer + core},
            device_id_type=MESH,
        )

    def gather(q, g, peer, source):
        return pltpu.make_async_remote_copy(
            src_ref=shared_ref.at[q, g, core, source],
            dst_ref=shared_ref.at[q, g, core, source],
            send_sem=ag_send.at[q, g, peer],
            recv_sem=ag_recv.at[q, g, source],
            device_id={"member": 2 * peer + core},
            device_id_type=MESH,
        )

    def hand_over(q, g, half):
        return pltpu.make_async_remote_copy(
            src_ref=shared_ref.at[q, g, half],
            dst_ref=shared_ref.at[q, g, half],
            send_sem=over_send.at[q, g],
            recv_sem=over_recv.at[q, g],
            device_id={"member": partner},
            device_id_type=MESH,
        )

    def other_chips(body):
        for d in range(1, CHIPS):
            body((chip + d) & (CHIPS - 1))

    def regroup(g):
        rows = jnp.concatenate(
            [xg_ref[g, c, p] for c in range(2 * FIELDS) for p in range(GROUP)], axis=0
        )
        _, lane = row_col(TRAJ * MIX, 128)
        value = jnp.concatenate(
            [rows[:, 0:NW], jnp.where(lane < 1, rows[:, NW:WIDTH], 0.0)], axis=1
        )
        high = value.astype(BF16)
        half_ref[0, g] = high
        half_ref[1, g] = (value - high.astype(F32)).astype(BF16)

    selection = select_rows(clones_ref, member)

    def offer(q, g):
        value = jnp.dot(selection, half_ref[q, g], preferred_element_type=F32).astype(BF16)
        for entry in range(KILLED):
            rows = slice(MIX * entry, MIX * entry + MIX)
            hand_ref[q, g, 0, entry] = value[rows, 0 : WIDE // 2]
            hand_ref[q, g, 1, entry] = value[rows, WIDE // 2 : WIDE]
        across(q, g).start()

    def combine(q, g):
        across(q, g).wait_recv()
        total = hand_ref[q, g, core].astype(F32) + core_ref[q, g].astype(F32)
        pair_ref[q, g] = total.astype(BF16)
        other_chips(lambda peer: scatter(q, g, peer, chip).start())

    def settle(q, g):
        other_chips(lambda peer: scatter(q, g, peer, peer).wait_recv())
        total = pair_ref[q, g, chip].astype(F32)
        for d in range(1, CHIPS):
            total = total + landed_ref[q, g, (chip + d) & (CHIPS - 1)].astype(F32)
        shared_ref[q, g, core, chip] = total.astype(BF16)
        other_chips(lambda peer: gather(q, g, peer, chip).start())

    def forward(q, g):
        other_chips(lambda peer: gather(q, g, peer, peer).wait_recv())
        hand_over(q, g, core).start()

    def arrived(q, g):
        hand_over(q, g, 1 - core).wait_recv()

    def received(q, g):
        return jnp.concatenate(
            [
                jnp.concatenate([shared_ref[q, g, 0, e], shared_ref[q, g, 1, e]], axis=1)
                for e in range(KILLED)
            ],
            axis=0,
        )

    def outward(part, g, peer, source):
        start, stop = PART[part]
        lanes = pl.ds(start, stop - start)
        return pltpu.make_async_remote_copy(
            src_ref=send_ref.at[g, peer, :, lanes],
            dst_ref=fourier_ref.at[pl.ds(g * TILE + source * 16, 16), lanes],
            send_sem=out_send.at[part % BOTH, g, peer],
            recv_sem=out_recv.at[part % BOTH, g, source],
            device_id={"space": peer},
            device_id_type=MESH,
        )

    def homeward(part, g, peer, source):
        start, stop = PART[part]
        lanes = pl.ds(start, stop - start)
        return pltpu.make_async_remote_copy(
            src_ref=give_ref.at[pl.ds(g * TILE + peer * 16, 16), lanes],
            dst_ref=back_ref.at[g, source, :, lanes],
            send_sem=back_send.at[part, g, peer],
            recv_sem=back_recv.at[part, g, source],
            device_id={"space": peer},
            device_id_type=MESH,
        )

    def own_out(g):
        rows = pl.ds(g * TILE + place * 16, 16)
        return pltpu.make_async_copy(send_ref.at[g, place], fourier_ref.at[rows], own_sem.at[0, g])

    def own_back(g):
        rows = pl.ds(g * TILE + place * 16, 16)
        return pltpu.make_async_copy(give_ref.at[rows], back_ref.at[g, place], own_sem.at[1, g])

    def each_group(body, first=0, last=GROUPS):
        def one(g, _):
            body(g)
            return 0

        lax.fori_loop(first, last, one, 0)

    def each_message(part, body):
        if part == 0:
            each_group(lambda g: body(BOTH, g), 0, EARLY)
        each_group(lambda g: body(part, g), EARLY, GROUPS)

    def send_out(part, g):
        spread("space", SPACE, lambda peer: outward(part, g, peer, place).start())

    keep, put_rows = keep_and_put(clones_ref, member)
    for g in range(2):
        x_copy(g).wait()
        regroup(g)
    pl.semaphore_wait(barrier, SPACE + MEMBERS - 2)
    offer(0, 0)
    offer(0, 1)
    combine(0, 0)
    combine(0, 1)
    settle(0, 0)
    x_copy(2).wait()
    regroup(2)
    offer(0, 2)
    settle(0, 1)
    combine(0, 2)
    forward(0, 0)

    def legendre_step(g, _):
        arrived(0, g)
        now = jnp.dot(keep, half_ref[0, g], preferred_element_type=F32)
        now_ref[...] = now + jnp.dot(put_rows, received(0, g), preferred_element_type=F32)
        leg_copy(g).wait()

        def put(block, lane, value):
            send_ref[g, block, :, lane : lane + 128] = value

        legendre_group(
            place * LOCAL + g * GROUP, now_ref, leg_ref.at[pl.ds(g * GROUP, GROUP)], put
        )
        @pl.when(g < EARLY)
        def _():
            send_out(BOTH, g)

        @pl.when(g >= EARLY)
        def _():
            send_out(0, g)

        own_out(g).start()

        @pl.when(g + 2 < GROUPS)
        def _():
            settle(0, g + 2)

        @pl.when(g + 1 < GROUPS)
        def _():
            forward(0, g + 1)

        @pl.when(g + 3 < GROUPS)
        def _():
            x_copy(g + 3).wait()
            regroup(g + 3)
            offer(0, g + 3)
            combine(0, g + 3)

        return 0

    lax.fori_loop(0, GROUPS, legendre_step, 0)

    def send_late(g, _):
        send_out(1, g)
        return 0

    lax.fori_loop(EARLY, GROUPS, send_late, 0)
    each_group(lambda g: offer(1, g))
    each_group(lambda g: combine(1, g))
    wide_copy.wait()
    tall_copy.wait()
    each_group(lambda g: own_out(g).wait())

    for part in range(2):
        each_message(
            part,
            lambda kind, g: spread(
                "space", SPACE, lambda peer: outward(kind, g, peer, peer).wait_recv()
            ),
        )
        grid_forward(part, sines[part], fourier_ref, wide_ref, forcing_ref)

        def backward(g):
            rows = pl.ds(pl.multiple_of(g * TILE, TILE), TILE)
            grid_backward(part, sines[part], rows, forcing_ref, tall_ref, give_ref)
            spread("space", SPACE, lambda peer: homeward(part, g, peer, place).start())

        each_group(backward)
        if part == 0:
            each_group(lambda g: settle(1, g))
        else:
            each_group(lambda g: forward(1, g))
    each_group(lambda g: own_back(g).start())

    placing = place_rows(clones_ref, member)
    row, _ = row_col(TRAJ, WIDTH)
    killed = by_trajectory(
        [entry_of(clones_ref, member * TRAJ + t) for t in range(TRAJ)], row
    )

    def complete(g):
        arrived(1, g)
        value = sum(
            jnp.dot(placing, received(q, g), preferred_element_type=F32) for q in range(2)
        )
        for c in range(2 * FIELDS):
            for p in range(GROUP):
                first = (c * GROUP + p) * TRAJ
                new = value[first : first + TRAJ, 0:WIDTH]
                xg_ref[g, c, p] = jnp.where(killed < KILLED, new, xg_ref[g, c, p])

    def new_copy(g):
        some = pl.ds(g * GROUP, GROUP)
        return pltpu.make_async_copy(xg_ref.at[g], new_any.at[:, some], state_sem.at[g])

    def project(g):
        own_back(g).wait()
        for part in range(2):
            spread(
                "space", SPACE, lambda peer: homeward(part, g, peer, peer).wait_recv()
            )
        project_group(
            place * LOCAL + g * GROUP,
            back_ref.at[g],
            leg_ref.at[pl.ds(g * GROUP, GROUP)],
            xg_ref.at[g],
            grav_ref,
            stab_ref,
        )
        new_copy(g).start()

    each_group(complete)
    each_group(project)
    for q in range(2):
        each_group(lambda g: across(q, g).wait_send())
        each_group(lambda g: other_chips(lambda peer: scatter(q, g, peer, chip).wait_send()))
        each_group(lambda g: other_chips(lambda peer: gather(q, g, peer, chip).wait_send()))
        each_group(lambda g: hand_over(q, g, core).wait_send())
    for part in range(2):
        each_message(
            part,
            lambda kind, g: spread(
                "space", SPACE, lambda peer: outward(kind, g, peer, place).wait_send()
            ),
        )
        each_group(
            lambda g: spread(
                "space", SPACE, lambda peer: homeward(part, g, peer, place).wait_send()
            )
        )
    each_group(lambda g: new_copy(g).wait())


STATE = (2 * FIELDS, LOCAL, TRAJ, WIDTH)


def step(state, legendre, sin_lat, gravity, stability, clones):
    tall, wide = zonal_tables()
    anywhere = pl.BlockSpec(memory_space=pl.ANY)
    vmem = pl.BlockSpec(memory_space=pltpu.VMEM)
    smem = pl.BlockSpec(memory_space=pltpu.SMEM)
    dma = pltpu.SemaphoreType.DMA
    pieces = (KILLED, MIX, WIDE // 2)
    band = (4 * PAIRS, LANES)
    return pl.pallas_call(
        main_kernel,
        in_specs=[smem, anywhere, anywhere, anywhere, anywhere, vmem, smem, smem],
        out_specs=anywhere,
        out_shape=jax.ShapeDtypeStruct(STATE, F32),
        scratch_shapes=[
            pltpu.VMEM((LOCAL, WIDTH, NHALF), BF16),
            pltpu.VMEM((4 * PAIRS, NLON), BF16),
            pltpu.VMEM((NLON, 4 * PAIRS), BF16),
            pltpu.VMEM(GROUPED, F32),
            pltpu.VMEM((2, GROUPS, TRAJ * MIX, WIDE), BF16),
            pltpu.VMEM((TRAJ * MIX, WIDE), F32),
            pltpu.VMEM((2, GROUPS, 2) + pieces, BF16),
            pltpu.VMEM((2, GROUPS) + pieces, BF16),
            pltpu.VMEM((2, GROUPS) + pieces, BF16),
            pltpu.VMEM((2, GROUPS) + pieces, BF16),
            pltpu.VMEM((2, GROUPS, 2) + pieces, BF16),
            pltpu.VMEM((GROUPS, SPACE, 16, LANES), BF16),
            pltpu.VMEM(band, BF16),
            pltpu.VMEM(band, BF16),
            pltpu.VMEM(band, BF16),
            pltpu.VMEM((GROUPS, SPACE, 16, LANES), BF16),
            dma((GROUPS,)),
            dma((GROUPS,)),
            dma((2,)),
            dma((GROUPS,)),
            dma((2, GROUPS)),
            dma((2, GROUPS)),
            dma((2, GROUPS)),
            dma((2, GROUPS, CHIPS)),
            dma((2, GROUPS, CHIPS)),
            dma((2, GROUPS, CHIPS)),
            dma((2, GROUPS, CHIPS)),
            dma((2, GROUPS)),
            dma((2, GROUPS)),
            dma((2, GROUPS, SPACE)),
            dma((2, GROUPS, SPACE)),
            dma((2, GROUPS, SPACE)),
            dma((2, GROUPS, SPACE)),
        ],
        compiler_params=pltpu.CompilerParams(
            vmem_limit_bytes=60 * 1024 * 1024, collective_id=0, has_side_effects=True
        ),
        name="step",
    )(
        clones.T,
        state,
        legendre,
        jnp.asarray(tall),
        jnp.asarray(wide),
        sin_lat,
        gravity,
        stability,
    )


def shards(spectra, legendre, sin_lat, gravity, stability, clones):
    state = spectra.transpose(1, 2, 0, 3)
    return step(state, legendre, sin_lat, gravity, stability, clones).transpose(2, 0, 1, 3)


def solution(mesh):
    placed = (P("member", None, "space", None), P("space", None, None), P(), P(), P(), P())
    return jax.shard_map(
        shards,
        mesh=mesh,
        in_specs=placed,
        out_specs=P("member", None, "space", None),
        check_vma=False,
    )
```

```python
import functools
import math

import jax
import jax.numpy as jnp
import numpy as np
from jax import lax
from jax.experimental import pallas as pl
from jax.experimental.pallas import tpu as pltpu
from jax.sharding import PartitionSpec as P

NW = 640
WIDTH = NW + 1
NLON = 1280
NLAT = 768
NHALF = 384
PAIRS = 320
TRAJ = 4
FIELDS = 6
LOCAL = 20
SPACE = 16
GROUP = 4
GROUPS = LOCAL // GROUP
FULL = 128 * FIELDS
LANES = FULL + 64 * FIELDS
PART = ((0, FULL), (FULL, LANES), (0, LANES))
BOTH = 2
MEMBERS = 8
CHIPS = 4
KILLED = 4
WIDE = 768
GROUPED = (GROUPS, 2 * FIELDS, GROUP, TRAJ, WIDTH)
MIX = 2 * FIELDS * GROUP
TILE = 16 * SPACE
EARLY = 1
MESH = pl.DeviceIdType.MESH
DT = 0.25
WAVE_SCALE = 16.0
DIFFUSION = 0.02
F32 = jnp.float32
BF16 = jnp.bfloat16


@functools.cache
def zonal_tables():
    pair = np.arange(PAIRS).reshape(SPACE, GROUPS, GROUP).transpose(1, 0, 2).reshape(-1)
    order = np.stack([pair, NW - 1 - pair], axis=1)
    phase = (order[:, :, None] * np.arange(NLON)) % NLON
    angle = phase * (2.0 * math.pi / NLON)
    table = np.stack([np.cos(angle), -np.sin(angle)], axis=2).reshape(4 * PAIRS, NLON)
    table = table.astype(jnp.bfloat16)
    return table, np.ascontiguousarray(table.T)


def row_col(rows, width):
    return (
        lax.broadcasted_iota(jnp.int32, (rows, width), 0),
        lax.broadcasted_iota(jnp.int32, (rows, width), 1),
    )


def sign_mask(pair):
    row, col = row_col(8, WIDTH)
    leading = (col < NW - pair).astype(jnp.int32)
    offset = jnp.where(leading == 1, col, col - (NW - pair))
    parity = (1 - 2 * (offset & 1)).astype(F32)
    sign = jnp.where(row >= 4, parity, 1.0)
    return jnp.where(((row >> 1) & 1) + leading == 1, sign, 0.0)


def swap4(value):
    return pltpu.roll(value, 4, 1)


def legendre_group(pair, now_ref, leg_ref, put):
    row8, _ = row_col(8, WIDTH)
    odd = (row8 & 1) == 1
    results = []
    for k in range(GROUP):
        mask = sign_mask(pair + k)
        pieces = []
        for t in range(TRAJ):
            for f in range(FIELDS):
                first = MIX * t + 2 * GROUP * f + k
                real, imag = (now_ref[row : row + 1, 0:WIDTH] for row in (first, first + GROUP))
                pieces.append(jnp.where(odd, imag, real) * mask)
        lhs = jnp.concatenate(pieces, axis=0).astype(BF16)
        dots = jnp.dot(lhs, leg_ref[k], preferred_element_type=F32)
        results.append(dots.reshape(TRAJ * FIELDS, 8, NHALF))
    upper = lax.broadcasted_iota(jnp.int32, (TRAJ * FIELDS, 8, NHALF), 1) < 4
    hemispheres = ([], [])
    for k in range(0, GROUP, 2):
        first, second = results[k], results[k + 1]
        hemispheres[0].append(jnp.where(upper, first, swap4(second)))
        hemispheres[1].append(jnp.where(upper, swap4(first), second))
    low = lax.broadcasted_iota(jnp.int32, (16, 128), 1) < 64
    for side in range(2):
        one, two = hemispheres[side]
        for t in range(TRAJ):
            for level in range(FIELDS // 2):
                tiles = []
                for f in (2 * level, 2 * level + 1):
                    tile = jnp.concatenate([one[t * FIELDS + f], two[t * FIELDS + f]], axis=0)
                    put(4 * t + 2 * side, 128 * f, tile[:, 0:128].astype(BF16))
                    put(4 * t + 2 * side + 1, 128 * f, tile[:, 128:256].astype(BF16))
                    tiles.append(tile[:, 256:384])
                a, b = tiles
                lane = FULL + 128 * level
                put(4 * t + 2 * side, lane, jnp.where(low, a, pltpu.roll(b, 64, 1)).astype(BF16))
                put(
                    4 * t + 2 * side + 1, lane, jnp.where(low, pltpu.roll(a, 64, 1), b).astype(BF16)
                )


def latitude_rows(sin_ref, place):
    low = lax.broadcasted_iota(jnp.int32, (1, 128), 1) < 64
    zero, one, two = (sin_ref[128 * i : 128 * i + 128].reshape(1, 128) for i in range(3))
    swapped = pltpu.roll(two, 64, 1)
    second = (place & 1) == 1
    sign = jnp.where((place & 3) >= 2, -1.0, 1.0).astype(F32)
    full = jnp.where(second, one, zero) * sign
    half = jnp.where(second, jnp.where(low, swapped, two), jnp.where(low, two, swapped)) * sign
    return full, half


def forcing_of(spin, spread, heat, heat_swapped, coriolis):
    spun = spin + coriolis
    return (
        -spun * spread,
        spun * spin - 0.5 * spread * spread,
        -(heat + 0.5 * (heat + heat_swapped)) * spread,
    )


def grid_forward(part, sines, f_ref, wide_ref, forcing_ref):
    start, stop = PART[part]
    tile = TILE

    def step(i, _):
        rows = pl.ds(pl.multiple_of(i * tile, tile), tile)
        sums = jnp.dot(wide_ref[rows, :], f_ref[:, start:stop], preferred_element_type=F32)
        sums = sums * (1.0 / NW)
        field = [sums[:, lane : lane + 128] for lane in range(0, stop - start, 128)]
        if part == 0:
            sets = [(field[a], field[2 + a], field[4 + a], field[5 - a]) for a in range(2)]
        else:
            sets = [(*field, pltpu.roll(field[2], 64, 1))]
        for a, fields in enumerate(sets):
            for g, made in enumerate(forcing_of(*fields, 2.0 * sines)):
                lane = start + 128 * (len(sets) * g + a)
                forcing_ref[rows, lane : lane + 128] = made.astype(BF16)
        return 0

    lax.fori_loop(0, NLON // tile, step, 0)


def grid_backward(part, sines, rows, forcing_ref, tall_ref, out_ref):
    start, stop = PART[part]
    weights = math.pi * jnp.sqrt(1.0 - sines * sines) / NLAT
    weights = jnp.concatenate([weights] * ((stop - start) // 128), axis=1)
    sums = jnp.dot(tall_ref[rows, :], forcing_ref[:, start:stop], preferred_element_type=F32)
    out_ref[rows, start:stop] = (sums * weights).astype(BF16)


def one_hot(condition):
    return jnp.where(condition, 1.0, 0.0).astype(BF16)


def square(rows):
    return row_col(rows, TRAJ * MIX)


def select_rows(clones_ref, member):
    row, col = square(MIX)
    parts = []
    for entry in range(KILLED):
        source = clones_ref[1, entry]
        wanted = jnp.where((source >> 2) == member, source & (TRAJ - 1), TRAJ)
        parts.append(one_hot((row == (col >> 2)) & ((col & 3) == wanted)))
    return jnp.concatenate(parts, axis=0)


def entry_of(clones_ref, number):
    found = KILLED
    for entry in range(KILLED):
        found = jnp.where(clones_ref[0, entry] == number, entry, found)
    return found


def entry_columns(col):
    return sum((col >= MIX * i).astype(jnp.int32) for i in range(1, KILLED))


def keep_and_put(clones_ref, member):
    row, col = square(MIX)
    entry = entry_columns(col)
    keep, put = [], []
    for t in range(TRAJ):
        found = entry_of(clones_ref, member * TRAJ + t)
        own = jnp.where(found == KILLED, t, TRAJ)
        keep.append(one_hot((row == (col >> 2)) & ((col & 3) == own)))
        put.append(one_hot((row == col - MIX * entry) & (entry == found)))
    return jnp.concatenate(keep, axis=0), jnp.concatenate(put, axis=0)


def by_trajectory(values, row):
    mixed = values[0]
    for t in range(1, TRAJ):
        mixed = jnp.where(row == t, values[t], mixed)
    return mixed


def place_rows(clones_ref, member):
    row, col = square(TRAJ * MIX)
    entry = entry_columns(col)
    found = [entry_of(clones_ref, member * TRAJ + t) for t in range(TRAJ)]
    return one_hot((entry == by_trajectory(found, row & 3)) & ((row >> 2) == col - MIX * entry))


def unmix():
    row, col = row_col(128, 128)
    t, half, side, part, pair = row & 3, (row >> 2) & 1, (row >> 3) & 1, (row >> 4) & 1, row >> 5
    return one_hot(col == 32 * t + 16 * side + 4 * pair + 2 * half + part)


def project_rows(back_ref):
    low = lax.broadcasted_iota(jnp.int32, (128, 128), 1) < 64
    order = unmix()

    def column(odd, lane):
        return jnp.concatenate(
            [
                back_ref[4 * t + 2 * side + odd, :, lane : lane + 128]
                for t in range(TRAJ)
                for side in range(2)
            ],
            axis=0,
        )

    fields = []
    for level in range(FIELDS // 2):
        lanes = [256 * level, 256 * level + 128, FULL + 128 * level]
        mixed = jnp.concatenate([column(odd, lane) for lane in lanes for odd in range(2)], axis=1)
        rows = jnp.dot(order, mixed, preferred_element_type=F32)
        a, b = rows[:, 512:640], rows[:, 640:768]
        last = (
            jnp.where(low, a, pltpu.roll(b, 64, 1)),
            jnp.where(low, pltpu.roll(a, 64, 1), b),
        )
        for h in range(2):
            fields.append(
                jnp.concatenate([rows[:, 256 * h : 256 * h + 256], last[h]], axis=1).astype(BF16)
            )
    return fields


def project_group(first_pair, back_ref, leg_ref, state_ref, grav_ref, stab_ref):
    g = [[grav_ref[a, b] for b in range(2)] for a in range(2)]
    s = [[stab_ref[a, b] for b in range(2)] for a in range(2)]
    gs = [[g[a][0] * s[0][b] + g[a][1] * s[1][b] for b in range(2)] for a in range(2)]
    fields = project_rows(back_ref)
    row8, _ = row_col(8, WIDTH)
    upper = row8 < 4
    _, col = row_col(1, WIDTH)
    for k in range(GROUP):
        pair = first_pair + k
        lhs = jnp.concatenate([rows[32 * k : 32 * k + 32] for rows in fields], axis=0)
        sums = lax.dot_general(
            lhs, leg_ref[k], (((1,), (1,)), ((), ())), preferred_element_type=F32
        )
        leading = col < NW - pair
        offset = jnp.where(leading, col, col - (NW - pair))
        parity = (1 - 2 * (offset & 1)).astype(F32)
        degree = jnp.where(leading, pair, NW - 1 - pair) + offset
        lam = WAVE_SCALE * (degree * (degree + 1)).astype(F32) / float(NW * NW)
        damp = 1.0 / (1.0 + DIFFUSION * lam * lam)
        coupling = DT * DT * lam
        diag = [1.0 + coupling * gs[a][a] for a in range(2)]
        cross = [coupling * gs[0][1], coupling * gs[1][0]]
        inverse = 1.0 / (diag[0] * diag[1] - cross[0] * cross[1])
        weight = [[DT * lam * g[a][b] for b in range(2)] for a in range(2)]
        left = jnp.broadcast_to(leading, (8, WIDTH))

        def moved(f):
            part = []
            for r in range(2):
                first = 32 * f + 16 * r
                part.append(sums[first : first + 8] + parity * sums[first + 8 : first + 16])
            near = jnp.where(upper, part[0], pltpu.roll(part[1], 4, 0))
            far = jnp.where(upper, pltpu.roll(part[0], 4, 0), part[1])
            old = jnp.concatenate([state_ref[2 * f, k], state_ref[2 * f + 1, k]], axis=0)
            return old + DT * jnp.where(left, near, far)

        def store(f, value):
            state_ref[2 * f, k] = value[0:4]
            state_ref[2 * f + 1, k] = value[4:8]

        for a in range(2):
            store(a, damp * moved(a))
        heat = [moved(4), moved(5)]
        right = [moved(2 + a) + (weight[a][0] * heat[0] + weight[a][1] * heat[1]) for a in range(2)]
        new = [
            (diag[1] * right[0] - cross[0] * right[1]) * inverse,
            (diag[0] * right[1] - cross[1] * right[0]) * inverse,
        ]
        for a in range(2):
            store(2 + a, damp * new[a])
            store(4 + a, damp * (heat[a] - DT * (s[a][0] * new[0] + s[a][1] * new[1])))


def spread(axis, count, body):
    me = lax.axis_index(axis)

    for d in range(1, count):
        body((me + d) & (count - 1))


def main_kernel(
    clones_ref,
    x_any,
    leg_any,
    tall_any,
    wide_any,
    sin_ref,
    grav_ref,
    stab_ref,
    new_any,
    leg_ref,
    tall_ref,
    wide_ref,
    xg_ref,
    half_ref,
    now_ref,
    hand_ref,
    core_ref,
    pair_ref,
    landed_ref,
    shared_ref,
    send_ref,
    fourier_ref,
    forcing_ref,
    give_ref,
    back_ref,
    x_sem,
    leg_sem,
    table_sem,
    state_sem,
    own_sem,
    core_send,
    core_recv,
    rs_send,
    rs_recv,
    ag_send,
    ag_recv,
    over_send,
    over_recv,
    out_send,
    out_recv,
    back_send,
    back_recv,
):
    member = lax.axis_index("member")
    place = lax.axis_index("space")
    core = member & 1
    chip = member >> 1
    partner = member + 1 - 2 * core
    sines = latitude_rows(sin_ref, place)

    def x_copy(g):
        some = pl.ds(g * GROUP, GROUP)
        return pltpu.make_async_copy(x_any.at[:, some], xg_ref.at[g], x_sem.at[g])

    def leg_copy(g):
        some = pl.ds(g * GROUP, GROUP)
        return pltpu.make_async_copy(leg_any.at[some], leg_ref.at[some], leg_sem.at[g])

    for copy in (x_copy, leg_copy):
        for g in range(GROUPS):
            copy(g).start()
    wide_copy = pltpu.make_async_copy(wide_any, wide_ref, table_sem.at[0])
    tall_copy = pltpu.make_async_copy(tall_any, tall_ref, table_sem.at[1])
    wide_copy.start()
    tall_copy.start()

    barrier = pltpu.get_barrier_semaphore()
    spread(
        "space",
        SPACE,
        lambda peer: pl.semaphore_signal(
            barrier, inc=1, device_id={"space": peer}, device_id_type=MESH
        ),
    )
    spread(
        "member",
        MEMBERS,
        lambda peer: pl.semaphore_signal(
            barrier, inc=1, device_id={"member": peer}, device_id_type=MESH
        ),
    )

    def across(q, g):
        return pltpu.make_async_remote_copy(
            src_ref=hand_ref.at[q, g, 1 - core],
            dst_ref=core_ref.at[q, g],
            send_sem=core_send.at[q, g],
            recv_sem=core_recv.at[q, g],
            device_id={"member": partner},
            device_id_type=MESH,
        )

    def scatter(q, g, peer, source):
        return pltpu.make_async_remote_copy(
            src_ref=pair_ref.at[q, g, peer],
            dst_ref=landed_ref.at[q, g, source],
            send_sem=rs_send.at[q, g, peer],
            recv_sem=rs_recv.at[q, g, source],
            device_id={"member": 2 * peer + core},
            device_id_type=MESH,
        )

    def gather(q, g, peer, source):
        return pltpu.make_async_remote_copy(
            src_ref=shared_ref.at[q, g, core, source],
            dst_ref=shared_ref.at[q, g, core, source],
            send_sem=ag_send.at[q, g, peer],
            recv_sem=ag_recv.at[q, g, source],
            device_id={"member": 2 * peer + core},
            device_id_type=MESH,
        )

    def hand_over(q, g, half):
        return pltpu.make_async_remote_copy(
            src_ref=shared_ref.at[q, g, half],
            dst_ref=shared_ref.at[q, g, half],
            send_sem=over_send.at[q, g],
            recv_sem=over_recv.at[q, g],
            device_id={"member": partner},
            device_id_type=MESH,
        )

    def other_chips(body):
        for d in range(1, CHIPS):
            body((chip + d) & (CHIPS - 1))

    def regroup(g):
        rows = jnp.concatenate(
            [xg_ref[g, c, p] for c in range(2 * FIELDS) for p in range(GROUP)], axis=0
        )
        _, lane = row_col(TRAJ * MIX, 128)
        value = jnp.concatenate(
            [rows[:, 0:NW], jnp.where(lane < 1, rows[:, NW:WIDTH], 0.0)], axis=1
        )
        high = value.astype(BF16)
        half_ref[0, g] = high
        half_ref[1, g] = (value - high.astype(F32)).astype(BF16)

    selection = select_rows(clones_ref, member)

    def offer(q, g):
        value = jnp.dot(selection, half_ref[q, g], preferred_element_type=F32).astype(BF16)
        for entry in range(KILLED):
            rows = slice(MIX * entry, MIX * entry + MIX)
            hand_ref[q, g, 0, entry] = value[rows, 0 : WIDE // 2]
            hand_ref[q, g, 1, entry] = value[rows, WIDE // 2 : WIDE]
        across(q, g).start()

    def combine(q, g):
        across(q, g).wait_recv()
        total = hand_ref[q, g, core].astype(F32) + core_ref[q, g].astype(F32)
        pair_ref[q, g] = total.astype(BF16)
        other_chips(lambda peer: scatter(q, g, peer, chip).start())

    def settle(q, g):
        other_chips(lambda peer: scatter(q, g, peer, peer).wait_recv())
        total = pair_ref[q, g, chip].astype(F32)
        for d in range(1, CHIPS):
            total = total + landed_ref[q, g, (chip + d) & (CHIPS - 1)].astype(F32)
        shared_ref[q, g, core, chip] = total.astype(BF16)
        other_chips(lambda peer: gather(q, g, peer, chip).start())

    def forward(q, g):
        other_chips(lambda peer: gather(q, g, peer, peer).wait_recv())
        hand_over(q, g, core).start()

    def arrived(q, g):
        hand_over(q, g, 1 - core).wait_recv()

    def received(q, g):
        return jnp.concatenate(
            [
                jnp.concatenate([shared_ref[q, g, 0, e], shared_ref[q, g, 1, e]], axis=1)
                for e in range(KILLED)
            ],
            axis=0,
        )

    def outward(part, g, peer, source):
        start, stop = PART[part]
        lanes = pl.ds(start, stop - start)
        return pltpu.make_async_remote_copy(
            src_ref=send_ref.at[g, peer, :, lanes],
            dst_ref=fourier_ref.at[pl.ds(g * TILE + source * 16, 16), lanes],
            send_sem=out_send.at[part % BOTH, g, peer],
            recv_sem=out_recv.at[part % BOTH, g, source],
            device_id={"space": peer},
            device_id_type=MESH,
        )

    def homeward(part, g, peer, source):
        start, stop = PART[part]
        lanes = pl.ds(start, stop - start)
        return pltpu.make_async_remote_copy(
            src_ref=give_ref.at[pl.ds(g * TILE + peer * 16, 16), lanes],
            dst_ref=back_ref.at[g, source, :, lanes],
            send_sem=back_send.at[part, g, peer],
            recv_sem=back_recv.at[part, g, source],
            device_id={"space": peer},
            device_id_type=MESH,
        )

    def own_out(g):
        rows = pl.ds(g * TILE + place * 16, 16)
        return pltpu.make_async_copy(send_ref.at[g, place], fourier_ref.at[rows], own_sem.at[0, g])

    def own_back(g):
        rows = pl.ds(g * TILE + place * 16, 16)
        return pltpu.make_async_copy(give_ref.at[rows], back_ref.at[g, place], own_sem.at[1, g])

    def each_group(body, first=0, last=GROUPS):
        def one(g, _):
            body(g)
            return 0

        lax.fori_loop(first, last, one, 0)

    def each_message(part, body):
        if part == 0:
            each_group(lambda g: body(BOTH, g), 0, EARLY)
        each_group(lambda g: body(part, g), EARLY, GROUPS)

    def send_out(part, g):
        spread("space", SPACE, lambda peer: outward(part, g, peer, place).start())

    keep, put_rows = keep_and_put(clones_ref, member)
    for g in range(2):
        x_copy(g).wait()
        regroup(g)
    pl.semaphore_wait(barrier, SPACE + MEMBERS - 2)
    offer(0, 0)
    offer(0, 1)
    combine(0, 0)
    combine(0, 1)
    settle(0, 0)
    x_copy(2).wait()
    regroup(2)
    offer(0, 2)
    settle(0, 1)
    combine(0, 2)
    forward(0, 0)

    def legendre_step(g, _):
        arrived(0, g)
        now = jnp.dot(keep, half_ref[0, g], preferred_element_type=F32)
        now_ref[...] = now + jnp.dot(put_rows, received(0, g), preferred_element_type=F32)
        leg_copy(g).wait()

        def put(block, lane, value):
            send_ref[g, block, :, lane : lane + 128] = value

        legendre_group(
            place * LOCAL + g * GROUP, now_ref, leg_ref.at[pl.ds(g * GROUP, GROUP)], put
        )
        @pl.when(g < EARLY)
        def _():
            send_out(BOTH, g)

        @pl.when(g >= EARLY)
        def _():
            send_out(0, g)

        own_out(g).start()

        @pl.when(g + 2 < GROUPS)
        def _():
            settle(0, g + 2)

        @pl.when(g + 1 < GROUPS)
        def _():
            forward(0, g + 1)

        @pl.when(g + 3 < GROUPS)
        def _():
            x_copy(g + 3).wait()
            regroup(g + 3)
            offer(0, g + 3)
            combine(0, g + 3)

        return 0

    lax.fori_loop(0, GROUPS, legendre_step, 0)

    def send_late(g, _):
        send_out(1, g)
        return 0

    lax.fori_loop(EARLY, GROUPS, send_late, 0)
    each_group(lambda g: offer(1, g))
    each_group(lambda g: combine(1, g))
    wide_copy.wait()
    tall_copy.wait()
    each_group(lambda g: own_out(g).wait())

    for part in range(2):
        each_message(
            part,
            lambda kind, g: spread(
                "space", SPACE, lambda peer: outward(kind, g, peer, peer).wait_recv()
            ),
        )
        grid_forward(part, sines[part], fourier_ref, wide_ref, forcing_ref)

        def backward(g):
            rows = pl.ds(pl.multiple_of(g * TILE, TILE), TILE)
            grid_backward(part, sines[part], rows, forcing_ref, tall_ref, give_ref)
            spread("space", SPACE, lambda peer: homeward(part, g, peer, place).start())

        each_group(backward)
        if part == 0:
            each_group(lambda g: settle(1, g))
        else:
            each_group(lambda g: forward(1, g))
    each_group(lambda g: own_back(g).start())

    placing = place_rows(clones_ref, member)
    row, _ = row_col(TRAJ, WIDTH)
    killed = by_trajectory(
        [entry_of(clones_ref, member * TRAJ + t) for t in range(TRAJ)], row
    )

    def complete(g):
        arrived(1, g)
        value = sum(
            jnp.dot(placing, received(q, g), preferred_element_type=F32) for q in range(2)
        )
        for c in range(2 * FIELDS):
            for p in range(GROUP):
                first = (c * GROUP + p) * TRAJ
                new = value[first : first + TRAJ, 0:WIDTH]
                xg_ref[g, c, p] = jnp.where(killed < KILLED, new, xg_ref[g, c, p])

    def new_copy(g):
        some = pl.ds(g * GROUP, GROUP)
        return pltpu.make_async_copy(xg_ref.at[g], new_any.at[:, some], state_sem.at[g])

    def project(g):
        own_back(g).wait()
        for part in range(2):
            spread(
                "space", SPACE, lambda peer: homeward(part, g, peer, peer).wait_recv()
            )
        project_group(
            place * LOCAL + g * GROUP,
            back_ref.at[g],
            leg_ref.at[pl.ds(g * GROUP, GROUP)],
            xg_ref.at[g],
            grav_ref,
            stab_ref,
        )
        new_copy(g).start()

    each_group(complete)
    each_group(project)
    for q in range(2):
        each_group(lambda g: across(q, g).wait_send())
        each_group(lambda g: other_chips(lambda peer: scatter(q, g, peer, chip).wait_send()))
        each_group(lambda g: other_chips(lambda peer: gather(q, g, peer, chip).wait_send()))
        each_group(lambda g: hand_over(q, g, core).wait_send())
    for part in range(2):
        each_message(
            part,
            lambda kind, g: spread(
                "space", SPACE, lambda peer: outward(kind, g, peer, place).wait_send()
            ),
        )
        each_group(
            lambda g: spread(
                "space", SPACE, lambda peer: homeward(part, g, peer, place).wait_send()
            )
        )
    each_group(lambda g: new_copy(g).wait())


STATE = (2 * FIELDS, LOCAL, TRAJ, WIDTH)


def step(state, legendre, sin_lat, gravity, stability, clones):
    tall, wide = zonal_tables()
    anywhere = pl.BlockSpec(memory_space=pl.ANY)
    vmem = pl.BlockSpec(memory_space=pltpu.VMEM)
    smem = pl.BlockSpec(memory_space=pltpu.SMEM)
    dma = pltpu.SemaphoreType.DMA
    pieces = (KILLED, MIX, WIDE // 2)
    band = (4 * PAIRS, LANES)
    return pl.pallas_call(
        main_kernel,
        in_specs=[smem, anywhere, anywhere, anywhere, anywhere, vmem, smem, smem],
        out_specs=anywhere,
        out_shape=jax.ShapeDtypeStruct(STATE, F32),
        scratch_shapes=[
            pltpu.VMEM((LOCAL, WIDTH, NHALF), BF16),
            pltpu.VMEM((4 * PAIRS, NLON), BF16),
            pltpu.VMEM((NLON, 4 * PAIRS), BF16),
            pltpu.VMEM(GROUPED, F32),
            pltpu.VMEM((2, GROUPS, TRAJ * MIX, WIDE), BF16),
            pltpu.VMEM((TRAJ * MIX, WIDE), F32),
            pltpu.VMEM((2, GROUPS, 2) + pieces, BF16),
            pltpu.VMEM((2, GROUPS) + pieces, BF16),
            pltpu.VMEM((2, GROUPS) + pieces, BF16),
            pltpu.VMEM((2, GROUPS) + pieces, BF16),
            pltpu.VMEM((2, GROUPS, 2) + pieces, BF16),
            pltpu.VMEM((GROUPS, SPACE, 16, LANES), BF16),
            pltpu.VMEM(band, BF16),
            pltpu.VMEM(band, BF16),
            pltpu.VMEM(band, BF16),
            pltpu.VMEM((GROUPS, SPACE, 16, LANES), BF16),
            dma((GROUPS,)),
            dma((GROUPS,)),
            dma((2,)),
            dma((GROUPS,)),
            dma((2, GROUPS)),
            dma((2, GROUPS)),
            dma((2, GROUPS)),
            dma((2, GROUPS, CHIPS)),
            dma((2, GROUPS, CHIPS)),
            dma((2, GROUPS, CHIPS)),
            dma((2, GROUPS, CHIPS)),
            dma((2, GROUPS)),
            dma((2, GROUPS)),
            dma((2, GROUPS, SPACE)),
            dma((2, GROUPS, SPACE)),
            dma((2, GROUPS, SPACE)),
            dma((2, GROUPS, SPACE)),
        ],
        compiler_params=pltpu.CompilerParams(
            vmem_limit_bytes=60 * 1024 * 1024, collective_id=0, has_side_effects=True
        ),
        name="step",
    )(
        clones.T,
        state,
        legendre,
        jnp.asarray(tall),
        jnp.asarray(wide),
        sin_lat,
        gravity,
        stability,
    )


def shards(spectra, legendre, sin_lat, gravity, stability, clones):
    state = spectra.transpose(1, 2, 0, 3)
    return step(state, legendre, sin_lat, gravity, stability, clones).transpose(2, 0, 1, 3)


def solution(mesh):
    placed = (P("member", None, "space", None), P("space", None, None), P(), P(), P(), P())
    return jax.shard_map(
        shards,
        mesh=mesh,
        in_specs=placed,
        out_specs=P("member", None, "space", None),
        check_vma=False,
    )
```

```python
import functools
import math

import jax
import jax.numpy as jnp
import numpy as np
from jax import lax
from jax.experimental import pallas as pl
from jax.experimental.pallas import tpu as pltpu
from jax.sharding import PartitionSpec as P

NW = 640
WIDTH = NW + 1
NLON = 1280
NLAT = 768
NHALF = 384
PAIRS = 320
TRAJ = 4
FIELDS = 6
LOCAL = 20
SPACE = 16
GROUP = 4
GROUPS = LOCAL // GROUP
FULL = 128 * FIELDS
LANES = FULL + 64 * FIELDS
PART = ((0, FULL), (FULL, LANES), (0, LANES))
BOTH = 2
MEMBERS = 8
CHIPS = 4
KILLED = 4
WIDE = 768
GROUPED = (GROUPS, 2 * FIELDS, GROUP, TRAJ, WIDTH)
MIX = 2 * FIELDS * GROUP
TILE = 16 * SPACE
EARLY = 0
MESH = pl.DeviceIdType.MESH
DT = 0.25
WAVE_SCALE = 16.0
DIFFUSION = 0.02
F32 = jnp.float32
BF16 = jnp.bfloat16


@functools.cache
def zonal_tables():
    pair = np.arange(PAIRS).reshape(SPACE, GROUPS, GROUP).transpose(1, 0, 2).reshape(-1)
    order = np.stack([pair, NW - 1 - pair], axis=1)
    phase = (order[:, :, None] * np.arange(NLON)) % NLON
    angle = phase * (2.0 * math.pi / NLON)
    table = np.stack([np.cos(angle), -np.sin(angle)], axis=2).reshape(4 * PAIRS, NLON)
    table = table.astype(jnp.bfloat16)
    return table, np.ascontiguousarray(table.T)


def row_col(rows, width):
    return (
        lax.broadcasted_iota(jnp.int32, (rows, width), 0),
        lax.broadcasted_iota(jnp.int32, (rows, width), 1),
    )


def sign_mask(pair):
    row, col = row_col(8, WIDTH)
    leading = (col < NW - pair).astype(jnp.int32)
    offset = jnp.where(leading == 1, col, col - (NW - pair))
    parity = (1 - 2 * (offset & 1)).astype(F32)
    sign = jnp.where(row >= 4, parity, 1.0)
    return jnp.where(((row >> 1) & 1) + leading == 1, sign, 0.0)


def swap4(value):
    return pltpu.roll(value, 4, 1)


def legendre_group(pair, now_ref, leg_ref, put):
    row8, _ = row_col(8, WIDTH)
    odd = (row8 & 1) == 1
    results = []
    for k in range(GROUP):
        mask = sign_mask(pair + k)
        pieces = []
        for t in range(TRAJ):
            for f in range(FIELDS):
                first = MIX * t + 2 * GROUP * f + k
                real, imag = (now_ref[row : row + 1, 0:WIDTH] for row in (first, first + GROUP))
                pieces.append(jnp.where(odd, imag, real) * mask)
        lhs = jnp.concatenate(pieces, axis=0).astype(BF16)
        dots = jnp.dot(lhs, leg_ref[k], preferred_element_type=F32)
        results.append(dots.reshape(TRAJ * FIELDS, 8, NHALF))
    upper = lax.broadcasted_iota(jnp.int32, (TRAJ * FIELDS, 8, NHALF), 1) < 4
    hemispheres = ([], [])
    for k in range(0, GROUP, 2):
        first, second = results[k], results[k + 1]
        hemispheres[0].append(jnp.where(upper, first, swap4(second)))
        hemispheres[1].append(jnp.where(upper, swap4(first), second))
    low = lax.broadcasted_iota(jnp.int32, (16, 128), 1) < 64
    for side in range(2):
        one, two = hemispheres[side]
        for t in range(TRAJ):
            for level in range(FIELDS // 2):
                tiles = []
                for f in (2 * level, 2 * level + 1):
                    tile = jnp.concatenate([one[t * FIELDS + f], two[t * FIELDS + f]], axis=0)
                    put(4 * t + 2 * side, 128 * f, tile[:, 0:128].astype(BF16))
                    put(4 * t + 2 * side + 1, 128 * f, tile[:, 128:256].astype(BF16))
                    tiles.append(tile[:, 256:384])
                a, b = tiles
                lane = FULL + 128 * level
                put(4 * t + 2 * side, lane, jnp.where(low, a, pltpu.roll(b, 64, 1)).astype(BF16))
                put(
                    4 * t + 2 * side + 1, lane, jnp.where(low, pltpu.roll(a, 64, 1), b).astype(BF16)
                )


def latitude_rows(sin_ref, place):
    low = lax.broadcasted_iota(jnp.int32, (1, 128), 1) < 64
    zero, one, two = (sin_ref[128 * i : 128 * i + 128].reshape(1, 128) for i in range(3))
    swapped = pltpu.roll(two, 64, 1)
    second = (place & 1) == 1
    sign = jnp.where((place & 3) >= 2, -1.0, 1.0).astype(F32)
    full = jnp.where(second, one, zero) * sign
    half = jnp.where(second, jnp.where(low, swapped, two), jnp.where(low, two, swapped)) * sign
    return full, half


def forcing_of(spin, spread, heat, heat_swapped, coriolis):
    spun = spin + coriolis
    return (
        -spun * spread,
        spun * spin - 0.5 * spread * spread,
        -(heat + 0.5 * (heat + heat_swapped)) * spread,
    )


def grid_forward(part, sines, f_ref, wide_ref, forcing_ref):
    start, stop = PART[part]
    tile = TILE

    def step(i, _):
        rows = pl.ds(pl.multiple_of(i * tile, tile), tile)
        sums = jnp.dot(wide_ref[rows, :], f_ref[:, start:stop], preferred_element_type=F32)
        sums = sums * (1.0 / NW)
        field = [sums[:, lane : lane + 128] for lane in range(0, stop - start, 128)]
        if part == 0:
            sets = [(field[a], field[2 + a], field[4 + a], field[5 - a]) for a in range(2)]
        else:
            sets = [(*field, pltpu.roll(field[2], 64, 1))]
        for a, fields in enumerate(sets):
            for g, made in enumerate(forcing_of(*fields, 2.0 * sines)):
                lane = start + 128 * (len(sets) * g + a)
                forcing_ref[rows, lane : lane + 128] = made.astype(BF16)
        return 0

    lax.fori_loop(0, NLON // tile, step, 0)


def grid_backward(part, sines, rows, forcing_ref, tall_ref, out_ref):
    start, stop = PART[part]
    weights = math.pi * jnp.sqrt(1.0 - sines * sines) / NLAT
    weights = jnp.concatenate([weights] * ((stop - start) // 128), axis=1)
    sums = jnp.dot(tall_ref[rows, :], forcing_ref[:, start:stop], preferred_element_type=F32)
    out_ref[rows, start:stop] = (sums * weights).astype(BF16)


def one_hot(condition):
    return jnp.where(condition, 1.0, 0.0).astype(BF16)


def square(rows):
    return row_col(rows, TRAJ * MIX)


def select_rows(clones_ref, member):
    row, col = square(MIX)
    parts = []
    for entry in range(KILLED):
        source = clones_ref[1, entry]
        wanted = jnp.where((source >> 2) == member, source & (TRAJ - 1), TRAJ)
        parts.append(one_hot((row == (col >> 2)) & ((col & 3) == wanted)))
    return jnp.concatenate(parts, axis=0)


def entry_of(clones_ref, number):
    found = KILLED
    for entry in range(KILLED):
        found = jnp.where(clones_ref[0, entry] == number, entry, found)
    return found


def entry_columns(col):
    return sum((col >= MIX * i).astype(jnp.int32) for i in range(1, KILLED))


def keep_and_put(clones_ref, member):
    row, col = square(MIX)
    entry = entry_columns(col)
    keep, put = [], []
    for t in range(TRAJ):
        found = entry_of(clones_ref, member * TRAJ + t)
        own = jnp.where(found == KILLED, t, TRAJ)
        keep.append(one_hot((row == (col >> 2)) & ((col & 3) == own)))
        put.append(one_hot((row == col - MIX * entry) & (entry == found)))
    return jnp.concatenate(keep, axis=0), jnp.concatenate(put, axis=0)


def by_trajectory(values, row):
    mixed = values[0]
    for t in range(1, TRAJ):
        mixed = jnp.where(row == t, values[t], mixed)
    return mixed


def place_rows(clones_ref, member):
    row, col = square(TRAJ * MIX)
    entry = entry_columns(col)
    found = [entry_of(clones_ref, member * TRAJ + t) for t in range(TRAJ)]
    return one_hot((entry == by_trajectory(found, row & 3)) & ((row >> 2) == col - MIX * entry))


def unmix():
    row, col = row_col(128, 128)
    t, half, side, part, pair = row & 3, (row >> 2) & 1, (row >> 3) & 1, (row >> 4) & 1, row >> 5
    return one_hot(col == 32 * t + 16 * side + 4 * pair + 2 * half + part)


def project_rows(back_ref):
    low = lax.broadcasted_iota(jnp.int32, (128, 128), 1) < 64
    order = unmix()

    def column(odd, lane):
        return jnp.concatenate(
            [
                back_ref[4 * t + 2 * side + odd, :, lane : lane + 128]
                for t in range(TRAJ)
                for side in range(2)
            ],
            axis=0,
        )

    fields = []
    for level in range(FIELDS // 2):
        lanes = [256 * level, 256 * level + 128, FULL + 128 * level]
        mixed = jnp.concatenate([column(odd, lane) for lane in lanes for odd in range(2)], axis=1)
        rows = jnp.dot(order, mixed, preferred_element_type=F32)
        a, b = rows[:, 512:640], rows[:, 640:768]
        last = (
            jnp.where(low, a, pltpu.roll(b, 64, 1)),
            jnp.where(low, pltpu.roll(a, 64, 1), b),
        )
        for h in range(2):
            fields.append(
                jnp.concatenate([rows[:, 256 * h : 256 * h + 256], last[h]], axis=1).astype(BF16)
            )
    return fields


def project_group(first_pair, back_ref, leg_ref, state_ref, grav_ref, stab_ref):
    g = [[grav_ref[a, b] for b in range(2)] for a in range(2)]
    s = [[stab_ref[a, b] for b in range(2)] for a in range(2)]
    gs = [[g[a][0] * s[0][b] + g[a][1] * s[1][b] for b in range(2)] for a in range(2)]
    fields = project_rows(back_ref)
    row8, _ = row_col(8, WIDTH)
    upper = row8 < 4
    _, col = row_col(1, WIDTH)
    for k in range(GROUP):
        pair = first_pair + k
        lhs = jnp.concatenate([rows[32 * k : 32 * k + 32] for rows in fields], axis=0)
        sums = lax.dot_general(
            lhs, leg_ref[k], (((1,), (1,)), ((), ())), preferred_element_type=F32
        )
        leading = col < NW - pair
        offset = jnp.where(leading, col, col - (NW - pair))
        parity = (1 - 2 * (offset & 1)).astype(F32)
        degree = jnp.where(leading, pair, NW - 1 - pair) + offset
        lam = WAVE_SCALE * (degree * (degree + 1)).astype(F32) / float(NW * NW)
        damp = 1.0 / (1.0 + DIFFUSION * lam * lam)
        coupling = DT * DT * lam
        diag = [1.0 + coupling * gs[a][a] for a in range(2)]
        cross = [coupling * gs[0][1], coupling * gs[1][0]]
        inverse = 1.0 / (diag[0] * diag[1] - cross[0] * cross[1])
        weight = [[DT * lam * g[a][b] for b in range(2)] for a in range(2)]
        left = jnp.broadcast_to(leading, (8, WIDTH))

        def moved(f):
            part = []
            for r in range(2):
                first = 32 * f + 16 * r
                part.append(sums[first : first + 8] + parity * sums[first + 8 : first + 16])
            near = jnp.where(upper, part[0], pltpu.roll(part[1], 4, 0))
            far = jnp.where(upper, pltpu.roll(part[0], 4, 0), part[1])
            old = jnp.concatenate([state_ref[2 * f, k], state_ref[2 * f + 1, k]], axis=0)
            return old + DT * jnp.where(left, near, far)

        def store(f, value):
            state_ref[2 * f, k] = value[0:4]
            state_ref[2 * f + 1, k] = value[4:8]

        for a in range(2):
            store(a, damp * moved(a))
        heat = [moved(4), moved(5)]
        right = [moved(2 + a) + (weight[a][0] * heat[0] + weight[a][1] * heat[1]) for a in range(2)]
        new = [
            (diag[1] * right[0] - cross[0] * right[1]) * inverse,
            (diag[0] * right[1] - cross[1] * right[0]) * inverse,
        ]
        for a in range(2):
            store(2 + a, damp * new[a])
            store(4 + a, damp * (heat[a] - DT * (s[a][0] * new[0] + s[a][1] * new[1])))


def spread(axis, count, body):
    me = lax.axis_index(axis)

    for d in range(1, count):
        body((me + d) & (count - 1))


def main_kernel(
    clones_ref,
    x_any,
    leg_any,
    tall_any,
    wide_any,
    sin_ref,
    grav_ref,
    stab_ref,
    new_any,
    leg_ref,
    tall_ref,
    wide_ref,
    xg_ref,
    half_ref,
    now_ref,
    hand_ref,
    core_ref,
    pair_ref,
    landed_ref,
    shared_ref,
    send_ref,
    fourier_ref,
    forcing_ref,
    give_ref,
    back_ref,
    x_sem,
    leg_sem,
    table_sem,
    state_sem,
    own_sem,
    core_send,
    core_recv,
    rs_send,
    rs_recv,
    ag_send,
    ag_recv,
    over_send,
    over_recv,
    out_send,
    out_recv,
    back_send,
    back_recv,
):
    member = lax.axis_index("member")
    place = lax.axis_index("space")
    core = member & 1
    chip = member >> 1
    partner = member + 1 - 2 * core
    sines = latitude_rows(sin_ref, place)

    def x_copy(g):
        some = pl.ds(g * GROUP, GROUP)
        return pltpu.make_async_copy(x_any.at[:, some], xg_ref.at[g], x_sem.at[g])

    def leg_copy(g):
        some = pl.ds(g * GROUP, GROUP)
        return pltpu.make_async_copy(leg_any.at[some], leg_ref.at[some], leg_sem.at[g])

    for copy in (x_copy, leg_copy):
        for g in range(GROUPS):
            copy(g).start()
    wide_copy = pltpu.make_async_copy(wide_any, wide_ref, table_sem.at[0])
    tall_copy = pltpu.make_async_copy(tall_any, tall_ref, table_sem.at[1])
    wide_copy.start()
    tall_copy.start()

    barrier = pltpu.get_barrier_semaphore()
    spread(
        "space",
        SPACE,
        lambda peer: pl.semaphore_signal(
            barrier, inc=1, device_id={"space": peer}, device_id_type=MESH
        ),
    )
    spread(
        "member",
        MEMBERS,
        lambda peer: pl.semaphore_signal(
            barrier, inc=1, device_id={"member": peer}, device_id_type=MESH
        ),
    )

    def across(q, g):
        return pltpu.make_async_remote_copy(
            src_ref=hand_ref.at[q, g, 1 - core],
            dst_ref=core_ref.at[q, g],
            send_sem=core_send.at[q, g],
            recv_sem=core_recv.at[q, g],
            device_id={"member": partner},
            device_id_type=MESH,
        )

    def scatter(q, g, peer, source):
        return pltpu.make_async_remote_copy(
            src_ref=pair_ref.at[q, g, peer],
            dst_ref=landed_ref.at[q, g, source],
            send_sem=rs_send.at[q, g, peer],
            recv_sem=rs_recv.at[q, g, source],
            device_id={"member": 2 * peer + core},
            device_id_type=MESH,
        )

    def gather(q, g, peer, source):
        return pltpu.make_async_remote_copy(
            src_ref=shared_ref.at[q, g, core, source],
            dst_ref=shared_ref.at[q, g, core, source],
            send_sem=ag_send.at[q, g, peer],
            recv_sem=ag_recv.at[q, g, source],
            device_id={"member": 2 * peer + core},
            device_id_type=MESH,
        )

    def hand_over(q, g, half):
        return pltpu.make_async_remote_copy(
            src_ref=shared_ref.at[q, g, half],
            dst_ref=shared_ref.at[q, g, half],
            send_sem=over_send.at[q, g],
            recv_sem=over_recv.at[q, g],
            device_id={"member": partner},
            device_id_type=MESH,
        )

    def other_chips(body):
        for d in range(1, CHIPS):
            body((chip + d) & (CHIPS - 1))

    def regroup(g):
        rows = jnp.concatenate(
            [xg_ref[g, c, p] for c in range(2 * FIELDS) for p in range(GROUP)], axis=0
        )
        _, lane = row_col(TRAJ * MIX, 128)
        value = jnp.concatenate(
            [rows[:, 0:NW], jnp.where(lane < 1, rows[:, NW:WIDTH], 0.0)], axis=1
        )
        high = value.astype(BF16)
        half_ref[0, g] = high
        half_ref[1, g] = (value - high.astype(F32)).astype(BF16)

    selection = select_rows(clones_ref, member)

    def offer(q, g):
        value = jnp.dot(selection, half_ref[q, g], preferred_element_type=F32).astype(BF16)
        for entry in range(KILLED):
            rows = slice(MIX * entry, MIX * entry + MIX)
            hand_ref[q, g, 0, entry] = value[rows, 0 : WIDE // 2]
            hand_ref[q, g, 1, entry] = value[rows, WIDE // 2 : WIDE]
        across(q, g).start()

    def combine(q, g):
        across(q, g).wait_recv()
        total = hand_ref[q, g, core].astype(F32) + core_ref[q, g].astype(F32)
        pair_ref[q, g] = total.astype(BF16)
        other_chips(lambda peer: scatter(q, g, peer, chip).start())

    def settle(q, g):
        other_chips(lambda peer: scatter(q, g, peer, peer).wait_recv())
        total = pair_ref[q, g, chip].astype(F32)
        for d in range(1, CHIPS):
            total = total + landed_ref[q, g, (chip + d) & (CHIPS - 1)].astype(F32)
        shared_ref[q, g, core, chip] = total.astype(BF16)
        other_chips(lambda peer: gather(q, g, peer, chip).start())

    def forward(q, g):
        other_chips(lambda peer: gather(q, g, peer, peer).wait_recv())
        hand_over(q, g, core).start()

    def arrived(q, g):
        hand_over(q, g, 1 - core).wait_recv()

    def received(q, g):
        return jnp.concatenate(
            [
                jnp.concatenate([shared_ref[q, g, 0, e], shared_ref[q, g, 1, e]], axis=1)
                for e in range(KILLED)
            ],
            axis=0,
        )

    def outward(part, g, peer, source):
        start, stop = PART[part]
        lanes = pl.ds(start, stop - start)
        return pltpu.make_async_remote_copy(
            src_ref=send_ref.at[g, peer, :, lanes],
            dst_ref=fourier_ref.at[pl.ds(g * TILE + source * 16, 16), lanes],
            send_sem=out_send.at[part % BOTH, g, peer],
            recv_sem=out_recv.at[part % BOTH, g, source],
            device_id={"space": peer},
            device_id_type=MESH,
        )

    def homeward(part, g, peer, source):
        start, stop = PART[part]
        lanes = pl.ds(start, stop - start)
        return pltpu.make_async_remote_copy(
            src_ref=give_ref.at[pl.ds(g * TILE + peer * 16, 16), lanes],
            dst_ref=back_ref.at[g, source, :, lanes],
            send_sem=back_send.at[part, g, peer],
            recv_sem=back_recv.at[part, g, source],
            device_id={"space": peer},
            device_id_type=MESH,
        )

    def own_out(g):
        rows = pl.ds(g * TILE + place * 16, 16)
        return pltpu.make_async_copy(send_ref.at[g, place], fourier_ref.at[rows], own_sem.at[0, g])

    def own_back(g):
        rows = pl.ds(g * TILE + place * 16, 16)
        return pltpu.make_async_copy(give_ref.at[rows], back_ref.at[g, place], own_sem.at[1, g])

    def each_group(body, first=0, last=GROUPS):
        def one(g, _):
            body(g)
            return 0

        lax.fori_loop(first, last, one, 0)

    def each_message(part, body):
        if part == 0:
            each_group(lambda g: body(BOTH, g), 0, EARLY)
        each_group(lambda g: body(part, g), EARLY, GROUPS)

    def send_out(part, g):
        spread("space", SPACE, lambda peer: outward(part, g, peer, place).start())

    keep, put_rows = keep_and_put(clones_ref, member)
    for g in range(2):
        x_copy(g).wait()
        regroup(g)
    pl.semaphore_wait(barrier, SPACE + MEMBERS - 2)
    offer(0, 0)
    offer(0, 1)
    combine(0, 0)
    combine(0, 1)
    settle(0, 0)
    x_copy(2).wait()
    regroup(2)
    offer(0, 2)
    settle(0, 1)
    combine(0, 2)
    forward(0, 0)

    def legendre_step(g, _):
        arrived(0, g)
        now = jnp.dot(keep, half_ref[0, g], preferred_element_type=F32)
        now_ref[...] = now + jnp.dot(put_rows, received(0, g), preferred_element_type=F32)
        leg_copy(g).wait()

        def put(block, lane, value):
            send_ref[g, block, :, lane : lane + 128] = value

        legendre_group(
            place * LOCAL + g * GROUP, now_ref, leg_ref.at[pl.ds(g * GROUP, GROUP)], put
        )
        @pl.when(g < EARLY)
        def _():
            send_out(BOTH, g)

        @pl.when(g >= EARLY)
        def _():
            send_out(0, g)

        own_out(g).start()

        @pl.when(g + 2 < GROUPS)
        def _():
            settle(0, g + 2)

        @pl.when(g + 1 < GROUPS)
        def _():
            forward(0, g + 1)

        @pl.when(g + 3 < GROUPS)
        def _():
            x_copy(g + 3).wait()
            regroup(g + 3)
            offer(0, g + 3)
            combine(0, g + 3)

        return 0

    lax.fori_loop(0, GROUPS, legendre_step, 0)

    def send_late(g, _):
        send_out(1, g)
        return 0

    lax.fori_loop(EARLY, GROUPS, send_late, 0)
    each_group(lambda g: offer(1, g))
    each_group(lambda g: combine(1, g))
    wide_copy.wait()
    tall_copy.wait()
    each_group(lambda g: own_out(g).wait())

    for part in range(2):
        each_message(
            part,
            lambda kind, g: spread(
                "space", SPACE, lambda peer: outward(kind, g, peer, peer).wait_recv()
            ),
        )
        grid_forward(part, sines[part], fourier_ref, wide_ref, forcing_ref)

        def backward(g):
            rows = pl.ds(pl.multiple_of(g * TILE, TILE), TILE)
            grid_backward(part, sines[part], rows, forcing_ref, tall_ref, give_ref)
            spread("space", SPACE, lambda peer: homeward(part, g, peer, place).start())

        each_group(backward)
        if part == 0:
            each_group(lambda g: settle(1, g))
        else:
            each_group(lambda g: forward(1, g))
    each_group(lambda g: own_back(g).start())

    placing = place_rows(clones_ref, member)
    row, _ = row_col(TRAJ, WIDTH)
    killed = by_trajectory(
        [entry_of(clones_ref, member * TRAJ + t) for t in range(TRAJ)], row
    )

    def complete(g):
        arrived(1, g)
        value = sum(
            jnp.dot(placing, received(q, g), preferred_element_type=F32) for q in range(2)
        )
        for c in range(2 * FIELDS):
            for p in range(GROUP):
                first = (c * GROUP + p) * TRAJ
                new = value[first : first + TRAJ, 0:WIDTH]
                xg_ref[g, c, p] = jnp.where(killed < KILLED, new, xg_ref[g, c, p])

    def new_copy(g):
        some = pl.ds(g * GROUP, GROUP)
        return pltpu.make_async_copy(xg_ref.at[g], new_any.at[:, some], state_sem.at[g])

    def project(g):
        own_back(g).wait()
        for part in range(2):
            spread(
                "space", SPACE, lambda peer: homeward(part, g, peer, peer).wait_recv()
            )
        project_group(
            place * LOCAL + g * GROUP,
            back_ref.at[g],
            leg_ref.at[pl.ds(g * GROUP, GROUP)],
            xg_ref.at[g],
            grav_ref,
            stab_ref,
        )
        new_copy(g).start()

    each_group(complete)
    each_group(project)
    for q in range(2):
        each_group(lambda g: across(q, g).wait_send())
        each_group(lambda g: other_chips(lambda peer: scatter(q, g, peer, chip).wait_send()))
        each_group(lambda g: other_chips(lambda peer: gather(q, g, peer, chip).wait_send()))
        each_group(lambda g: hand_over(q, g, core).wait_send())
    for part in range(2):
        each_message(
            part,
            lambda kind, g: spread(
                "space", SPACE, lambda peer: outward(kind, g, peer, place).wait_send()
            ),
        )
        each_group(
            lambda g: spread(
                "space", SPACE, lambda peer: homeward(part, g, peer, place).wait_send()
            )
        )
    each_group(lambda g: new_copy(g).wait())


STATE = (2 * FIELDS, LOCAL, TRAJ, WIDTH)


def step(state, legendre, sin_lat, gravity, stability, clones):
    tall, wide = zonal_tables()
    anywhere = pl.BlockSpec(memory_space=pl.ANY)
    vmem = pl.BlockSpec(memory_space=pltpu.VMEM)
    smem = pl.BlockSpec(memory_space=pltpu.SMEM)
    dma = pltpu.SemaphoreType.DMA
    pieces = (KILLED, MIX, WIDE // 2)
    band = (4 * PAIRS, LANES)
    return pl.pallas_call(
        main_kernel,
        in_specs=[smem, anywhere, anywhere, anywhere, anywhere, vmem, smem, smem],
        out_specs=anywhere,
        out_shape=jax.ShapeDtypeStruct(STATE, F32),
        scratch_shapes=[
            pltpu.VMEM((LOCAL, WIDTH, NHALF), BF16),
            pltpu.VMEM((4 * PAIRS, NLON), BF16),
            pltpu.VMEM((NLON, 4 * PAIRS), BF16),
            pltpu.VMEM(GROUPED, F32),
            pltpu.VMEM((2, GROUPS, TRAJ * MIX, WIDE), BF16),
            pltpu.VMEM((TRAJ * MIX, WIDE), F32),
            pltpu.VMEM((2, GROUPS, 2) + pieces, BF16),
            pltpu.VMEM((2, GROUPS) + pieces, BF16),
            pltpu.VMEM((2, GROUPS) + pieces, BF16),
            pltpu.VMEM((2, GROUPS) + pieces, BF16),
            pltpu.VMEM((2, GROUPS, 2) + pieces, BF16),
            pltpu.VMEM((GROUPS, SPACE, 16, LANES), BF16),
            pltpu.VMEM(band, BF16),
            pltpu.VMEM(band, BF16),
            pltpu.VMEM(band, BF16),
            pltpu.VMEM((GROUPS, SPACE, 16, LANES), BF16),
            dma((GROUPS,)),
            dma((GROUPS,)),
            dma((2,)),
            dma((GROUPS,)),
            dma((2, GROUPS)),
            dma((2, GROUPS)),
            dma((2, GROUPS)),
            dma((2, GROUPS, CHIPS)),
            dma((2, GROUPS, CHIPS)),
            dma((2, GROUPS, CHIPS)),
            dma((2, GROUPS, CHIPS)),
            dma((2, GROUPS)),
            dma((2, GROUPS)),
            dma((2, GROUPS, SPACE)),
            dma((2, GROUPS, SPACE)),
            dma((2, GROUPS, SPACE)),
            dma((2, GROUPS, SPACE)),
        ],
        compiler_params=pltpu.CompilerParams(
            vmem_limit_bytes=60 * 1024 * 1024, collective_id=0, has_side_effects=True
        ),
        name="step",
    )(
        clones.T,
        state,
        legendre,
        jnp.asarray(tall),
        jnp.asarray(wide),
        sin_lat,
        gravity,
        stability,
    )


def shards(spectra, legendre, sin_lat, gravity, stability, clones):
    state = spectra.transpose(1, 2, 0, 3)
    return step(state, legendre, sin_lat, gravity, stability, clones).transpose(2, 0, 1, 3)


def solution(mesh):
    placed = (P("member", None, "space", None), P("space", None, None), P(), P(), P(), P())
    return jax.shard_map(
        shards,
        mesh=mesh,
        in_specs=placed,
        out_specs=P("member", None, "space", None),
        check_vma=False,
    )
```
